256 devices in a mesh: dp: 8 (over x, core), proto: 32 (over y, z).
Axes of the slice: x: 4, y: 4, z: 8, core: 2. Of those that a mesh axis runs over, the one named last changes fastest.
Arguments:
- first_view_embed: bfloat16 [8192, 512], P(('dp', 'proto')), may hold values from -40 to 40
- second_view_embed: bfloat16 [8192, 512], P(('dp', 'proto')), may hold values from -40 to 40
- prototypes: float32 [65536, 512], P(('dp', 'proto')), may hold values from -12 to 12
- pairing: int32 [8192], P('dp'), may hold values from 0 to 1023, as said below
Outputs:
- proto_grad: float32 [65536, 512], P(('dp', 'proto'))
- mean_loss: float32 [], replicated
The draws below stay inside these ranges and needn't reach their ends.
Inputs may be any that keep to these rules, and one draw needn't show every extreme that they name: `pairing`: within each aligned block of 1024 frames the entries are a permutation of 0 to 1023.
All inputs are finite; a program needn't handle non-finite values.
Results may differ from the reference program's by a relative error of at most 0.015.
Values may be sent and summed in bfloat16 or wider, within the bound.
A program may use at most 128 MiB of HBM per device.

```python
import math
import jax
import jax.numpy as jnp
from jax import lax

D = 512
PROTO_DEV = 2048
FRAMES_DEV = 1024
ITERS = 3
FRAMES = 8192
PROTOS = 65536


def center_table(key):
    table_key = jax.random.fold_in(key, 101)
    return jax.random.truncated_normal(table_key, -4.0, 4.0, (FRAMES // 8, D), jnp.float32)


def center_labels(key):
    label_key = jax.random.fold_in(key, 102)
    return jax.random.randint(label_key, (FRAMES,), 0, FRAMES // 8).astype(jnp.int32)


def permute_block(block_key):
    return jax.random.permutation(block_key, FRAMES_DEV)


def shared_pairing(key):
    pair_key = jax.random.fold_in(key, 31)
    block_keys = jax.random.split(pair_key, FRAMES // FRAMES_DEV)
    return jax.vmap(permute_block)(block_keys).astype(jnp.int32)


def block_strength():
    blocks = FRAMES // FRAMES_DEV
    rising = 1.0 + 3.0 * jnp.arange(blocks, dtype=jnp.float32) / max(blocks - 1, 1)
    return jnp.repeat(rising, FRAMES_DEV)[:, None]


def view_rows(centers, key):
    jitter_key, scale_key = jax.random.split(key, 2)
    jitter = jax.random.truncated_normal(jitter_key, -4.0, 4.0, (FRAMES, D), jnp.float32)
    scales = jnp.exp(jax.random.uniform(scale_key, (FRAMES, 1), jnp.float32, -0.7, 1.6))
    return (centers + jitter * scales).astype(jnp.bfloat16)


def draw_first_view_embed(key, part):
    table = center_table(key)
    labels = center_labels(key)
    centers = jnp.take(table, labels, axis=0) * block_strength()
    key = jax.random.fold_in(key, 11)
    return view_rows(centers, key)


def draw_second_view_embed(key, part):
    table = center_table(key)
    labels = center_labels(key)
    pairs = shared_pairing(key)
    inverse = jnp.argsort(pairs, axis=1).astype(jnp.int32)
    block_first = (jnp.arange(FRAMES // FRAMES_DEV, dtype=jnp.int32) * FRAMES_DEV)[:, None]
    source = (block_first + inverse).reshape(FRAMES).astype(jnp.int32)
    second_labels = jnp.take(labels, source, axis=0)
    centers = jnp.take(table, second_labels, axis=0) * block_strength()
    key = jax.random.fold_in(key, 12)
    return view_rows(centers, key)


def draw_prototypes(key, part):
    count = FRAMES // 8
    table = center_table(key)
    key = jax.random.fold_in(key, 21)
    jitter_key, scale_key, pick_key, spread_key = jax.random.split(key, 4)
    pick = jax.random.randint(pick_key, (PROTOS,), 0, count).astype(jnp.int32)
    base = jnp.take(table, pick, axis=0)
    rows_per = PROTO_DEV // (FRAMES // FRAMES_DEV)
    owners = PROTOS // PROTO_DEV
    owner = jnp.arange(PROTOS, dtype=jnp.int32) // rows_per % owners
    place = owner.astype(jnp.float32) / max(owners - 1, 1)
    noise = jax.random.uniform(spread_key, (PROTOS,), jnp.float32, 0.0, 1.0)
    spread_amount = jnp.exp(-1.204 + 1.92 * place + 0.2 * noise)[:, None]
    jitter = jax.random.truncated_normal(jitter_key, -3.0, 3.0, (PROTOS, D), jnp.float32)
    scales = jnp.exp(jax.random.uniform(scale_key, (PROTOS, 1), jnp.float32, -1.2, 0.0))
    return (base + jitter * spread_amount) * scales


def draw_pairing(key, part):
    return shared_pairing(key).reshape(FRAMES).astype(jnp.int32)


def setup_inputs(seed: int = 0) -> dict:
    arg_keys = jax.random.split(jax.random.key(seed), 5)
    return {
        "first_view_embed": draw_first_view_embed(jax.random.fold_in(arg_keys[4], 71), 0),
        "second_view_embed": draw_second_view_embed(jax.random.fold_in(arg_keys[4], 71), 0),
        "prototypes": draw_prototypes(jax.random.fold_in(arg_keys[4], 71), 0),
        "pairing": draw_pairing(jax.random.fold_in(arg_keys[4], 71), 0),
    }


MIN_MASS_BOUND = 0.05
SOFT_TEMP = 0.1
NORM_EPS = 1e-06

def unit_rows(matrix):
    widened = matrix.astype(jnp.float32)
    return (widened * lax.rsqrt(lax.optimization_barrier(jnp.sum(widened * widened, axis=-1, keepdims=True)) + NORM_EPS)).astype(jnp.bfloat16)

def reference(first_view_embed, second_view_embed, prototypes, pairing):
    unit_first = unit_rows(first_view_embed)
    unit_second = unit_rows(second_view_embed)
    block_starts = jnp.arange(FRAMES, dtype=jnp.int32) // FRAMES_DEV * FRAMES_DEV
    partner = jnp.take(unit_second, (block_starts + pairing).astype(jnp.int32), axis=0)
    both_views = jnp.stack([unit_first, partner])
    unit_protos = unit_rows(prototypes)
    block_count = PROTOS // PROTO_DEV
    block_ids = jnp.arange(block_count, dtype=jnp.int32)

    def scores_of(block_index):
        shard_rows = lax.dynamic_slice_in_dim(unit_protos, (block_index * PROTO_DEV).astype(jnp.int32), PROTO_DEV, 0)
        return jnp.stack([jnp.dot(both_views[0], shard_rows.T, preferred_element_type=jnp.float32), jnp.dot(both_views[1], shard_rows.T, preferred_element_type=jnp.float32)])

    def balance_pass(running, block_index):
        sample_factor, sample_marginal, soft_sum = running
        centroid_similarity = scores_of(block_index)
        optimal_transport_solver = jnp.exp(centroid_similarity / MIN_MASS_BOUND)
        cluster_factor = 1.0 / lax.optimization_barrier(jnp.sum(sample_factor[:, :, None] * optimal_transport_solver, axis=1))
        sample_marginal = sample_marginal + lax.optimization_barrier(jnp.sum(optimal_transport_solver * cluster_factor[:, None, :], axis=2))
        soft_sum = soft_sum + lax.optimization_barrier(jnp.sum(jnp.exp(centroid_similarity / SOFT_TEMP), axis=2))
        return ((sample_factor, sample_marginal, soft_sum), cluster_factor)
    sample_factor = jnp.ones((2, FRAMES), jnp.float32)
    soft_total = jnp.zeros((2, FRAMES), jnp.float32)
    column_blocks = jnp.zeros((block_count, 2, PROTO_DEV), jnp.float32)
    for sweep_index in range(ITERS):
        zeros = jnp.zeros((2, FRAMES), jnp.float32)
        (unused, sample_marginal, soft_total), column_blocks = lax.scan(balance_pass, (sample_factor, zeros, zeros), block_ids)
        sample_factor = 1.0 / sample_marginal
    log_total = jnp.log(soft_total)
    grad_scale = PROTOS / (SOFT_TEMP * math.sqrt(2.0 * FRAMES))

    def closing_pass(loss_sum, inputs):
        block_index, cluster_factor = inputs
        centroid_similarity = scores_of(block_index)
        optimal_transport_solver = jnp.exp(centroid_similarity / MIN_MASS_BOUND)
        code_targets = sample_factor[:, :, None] * optimal_transport_solver * cluster_factor[:, None, :]
        swapped = code_targets[::-1]
        predicted = jnp.exp(centroid_similarity / SOFT_TEMP) / soft_total[:, :, None]
        loss_sum = loss_sum + jnp.sum(swapped * (log_total[:, :, None] - centroid_similarity / SOFT_TEMP))
        weights = ((predicted - swapped) * grad_scale).astype(jnp.bfloat16)
        grad_block = jnp.dot(weights[0].T, both_views[0], preferred_element_type=jnp.float32)
        grad_block = grad_block + jnp.dot(weights[1].T, both_views[1], preferred_element_type=jnp.float32)
        return (loss_sum, grad_block)
    loss_sum, grad_blocks = lax.scan(closing_pass, jnp.zeros((), jnp.float32), (block_ids, column_blocks))
    return (grad_blocks.reshape(PROTOS, D), loss_sum / (2.0 * FRAMES))
```

```python
import functools
import math

import jax
import jax.numpy as jnp
from jax import lax
from jax.experimental import pallas as pl
from jax.experimental.pallas import tpu as pltpu
from jax.sharding import PartitionSpec as P

ITERS = 3
SOFT_TEMP = 0.1
NORM_EPS = 1e-06
CORES = 2
DEPTH = 8

F32 = jnp.float32
BF16 = jnp.bfloat16
NT = (((1,), (1,)), ((), ()))
NN = (((1,), (0,)), ((), ()))


def unit_rows(matrix):
    widened = matrix.astype(F32)
    return (
        widened * lax.rsqrt(jnp.sum(widened * widened, axis=-1, keepdims=True) + NORM_EPS)
    ).astype(BF16)


def drain(ref, sem):
    pltpu.make_async_copy(ref, ref, sem).wait()


def rows_to_lanes(acc_ref, view, out_ref, rows):
    for b in range(rows // 128):
        block = acc_ref[view, b * 128 : (b + 1) * 128, :]
        out_ref[b : b + 1, :] = jnp.sum(block.T, axis=0, keepdims=True)


def lanes_to_rows(dense, out_ref, view, rows):
    for b in range(rows // 128):
        block = jnp.broadcast_to(dense[b : b + 1, :], (128, 128))
        out_ref[view, b * 128 : (b + 1) * 128, :] = block.T


def kernel(
    sizes,
    first_ref,
    second_ref,
    protos_ref,
    pair_ref,
    grad_ref,
    loss_ref,
    v_ref,
    partner_ref,
    p_ref,
    onehot_ref,
    ut_ref,
    e_ref,
    acc_ref,
    soft_acc_ref,
    rb_ref,
    sb_ref,
    cs_ref,
    c_ref,
    r_ref,
    row_ref,
    t_ref,
    w_ref,
    g_ref,
    dp_src,
    dp_buf,
    y_src,
    y_buf,
    z_src,
    z_buf,
    soft_src,
    soft_ybuf,
    soft_mid,
    soft_zbuf,
    loss_src,
    loss_ybuf,
    loss_zbuf,
    loss_xbuf,
    ss_ref,
    sr_ref,
    xs_ref,
    xr_ref,
    ay_s,
    ay_r,
    az_s,
    az_r,
    bz_s,
    bz_r,
    by_s,
    by_r,
    px_s,
    px_r,
    ps_s,
    ps_r,
    dp_s,
    dp_r,
    y_s,
    y_r,
    z_s,
    z_r,
    soft_s,
    soft_r,
    loss_s,
    loss_r,
    ss_s,
    ss_r,
    xs_s,
    xs_r,
):
    nx, ny, nz, fr, width, pr = sizes
    frames = fr * ny * nz
    group = fr * ny
    protos = pr * nx * CORES
    ptiles = protos // 128
    tiles_pr = pr // 128
    fdense = frames // 128
    grad_scale = protos * ny * nz / (SOFT_TEMP * math.sqrt(2.0 * frames * nx * CORES))

    dp, pi = lax.axis_index("dp"), lax.axis_index("proto")
    x, core = dp // CORES, dp % CORES
    y, z = pi // nz, pi % nz

    def at(dx=0, dc=0, dy=0, dz=0):
        return {
            "dp": lax.rem(x + dx, nx) * CORES + lax.rem(core + dc, CORES),
            "proto": lax.rem(y + dy, ny) * nz + lax.rem(z + dz, nz),
        }

    def send(src, dst, ssem, rsem, device):
        pltpu.make_async_remote_copy(
            src_ref=src,
            dst_ref=dst,
            send_sem=ssem,
            recv_sem=rsem,
            device_id=device,
            device_id_type=pl.DeviceIdType.MESH,
        ).start()

    sib = at(dc=1)
    xs = [at(dx=d) for d in range(1, nx)]
    ys = [at(dy=d) for d in range(1, ny)]
    zs = [at(dz=d) for d in range(1, nz)]
    dps = [at(dx=d, dc=e) for d in range(nx) for e in range(CORES) if d or e]

    barrier = pltpu.get_barrier_semaphore()
    for device in dps + ys + zs:
        pl.semaphore_signal(
            barrier, inc=1, device_id=device, device_id_type=pl.DeviceIdType.MESH
        )
    v_ref[0, z, y] = unit_rows(first_ref[...])
    v_ref[1, z, y] = unit_rows(second_ref[...])
    p_ref[dp] = unit_rows(protos_ref[...])
    pl.semaphore_wait(barrier, len(dps) + len(ys) + len(zs))

    for device in ys:
        send(v_ref.at[0, z, y], v_ref.at[0, z, y], ay_s, ay_r, device)
    for j, device in enumerate(xs):
        send(p_ref.at[dp], p_ref.at[dp], px_s, px_r.at[j], device)
    z_order = []
    for d in range(1, nz // 2 + 1):
        z_order.append(d)
        if nz - d != d:
            z_order.append(nz - d)
    for d in z_order:
        send(v_ref.at[1, z, y], v_ref.at[1, z, y], bz_s, bz_r.at[d - 1], zs[d - 1])
    send(p_ref.at[dp], p_ref.at[dp], ps_s, ps_r, sib)
    for device in ys:
        send(v_ref.at[1, z, y], v_ref.at[1, z, y], by_s, by_r, device)

    pair = pair_ref[...]
    where = (pair % (nz * fr) // fr) * group + (pair // (nz * fr)) * fr + pair % fr
    where = where.astype(F32)
    for b in range(fdense):
        column = jnp.broadcast_to(where[b : b + 1, :], (128, 128)).T
        for t in range(fdense):
            lane = (lax.broadcasted_iota(jnp.int32, (128, 128), 1) + t * 128).astype(F32)
            block = jnp.where(column == lane, 1.0, 0.0).astype(BF16)
            for q in range(128 // fr):
                natural = b * 128 + q * fr
                row = (natural % (nz * fr) // fr) * group + natural // (nz * fr) * fr
                onehot_ref[row : row + fr, t * 128 : (t + 1) * 128] = block[
                    q * fr : (q + 1) * fr, :
                ]
    cs_ref[...] = jnp.zeros_like(cs_ref)
    soft_acc_ref[...] = jnp.zeros_like(soft_acc_ref)

    def wait_frames_z(d):
        zb = lax.rem(z + nz - d, nz)
        drain(v_ref.at[1, zb, y], bz_r.at[d - 1])
        for device in ys:
            send(v_ref.at[1, zb, y], v_ref.at[1, zb, y], by_s, by_r, device)

    half = ny // 2

    def ring_blocks(step):
        up = lax.rem(z + nz - (step - 1), nz)
        down = lax.rem(z + step - 1, nz)
        if step < nz // 2:
            return v_ref.at[0, up], v_ref.at[0, down]
        return v_ref.at[0, up, pl.ds(0, half)], v_ref.at[0, down, pl.ds(half, half)]

    def ring_send(step):
        up, down = ring_blocks(step)
        send(up, up, az_s.at[0, step - 1], az_r.at[0, step - 1], zs[0])
        send(down, down, az_s.at[1, step - 1], az_r.at[1, step - 1], zs[nz - 2])

    def ring_wait(step):
        up, down = ring_blocks(step)
        drain(up, az_r.at[0, step - 1])
        drain(down, az_r.at[1, step - 1])

    def wait_protos_x(j):
        owner = lax.rem(x + nx - (j + 1), nx) * CORES + core
        drain(p_ref.at[owner], px_r.at[j])
        send(p_ref.at[owner], p_ref.at[owner], ps_s, ps_r, sib)

    def first_pass(view, rows, row, block):
        count = block.shape[0]

        def step(j, carry):
            cols = pl.ds(pl.multiple_of(j * pr, pr), pr)
            scores = lax.dot_general(block, p_ref[j], NT, preferred_element_type=F32)
            e = jnp.exp(scores / SOFT_TEMP)
            e_ref[view, rows, cols] = e
            total = e[:, 0:128]
            for t in range(1, tiles_pr):
                total = total + e[:, t * 128 : (t + 1) * 128]
            soft_acc_ref[view, rows, :] += total
            cs_ref[view, :, cols] += jnp.sum((e * e).reshape(count // 8, 8, pr), axis=0)
            return carry

        lax.fori_loop(0, nx * CORES, step, 0)

    def zero_block(zb):
        rows = pl.ds(pl.multiple_of(zb * group, group), group)
        first_pass(0, rows, zb, v_ref[0, zb].reshape(group, width))

    drain(v_ref.at[0, 0, pl.ds(0, ny - 1)], ay_r)
    ring_send(1)
    near = z_order[: (nz - 1) // 2]
    far = z_order[(nz - 1) // 2 :]
    for d in near:
        wait_frames_z(d)
    if nz // 2 > 1:
        ring_wait(1)
        ring_send(2)
    for d in far:
        wait_frames_z(d)
    x_order = sorted(range(nx - 1), key=lambda j: min(j + 1, nx - j - 1))
    for j in x_order[:-1]:
        wait_protos_x(j)
    for step in range(3, nz // 2):
        ring_wait(step - 1)
        ring_send(step)
    wait_protos_x(x_order[-1])
    drain(p_ref.at[pl.ds(0, nx)], ps_r)
    if nz // 2 > 2:
        ring_wait(nz // 2 - 1)
        ring_send(nz // 2)
    drain(v_ref.at[1, :, pl.ds(0, ny - 1)], by_r)

    chunk = min(256, frames)

    def permute(i, carry):
        rows = pl.ds(pl.multiple_of(i * chunk, chunk), chunk)
        partner_ref[rows, :] = lax.dot_general(
            onehot_ref[rows, :],
            v_ref[1].reshape(frames, width),
            NN,
            preferred_element_type=F32,
        ).astype(BF16)
        first_pass(1, rows, i, partner_ref[rows, :])
        return carry

    lax.fori_loop(0, frames // chunk, permute, 0)

    def dp_start(view, it, source):
        slot = it % 2
        if it >= 2:
            drain(dp_buf.at[view, slot], dp_s.at[view, slot])
        dp_src[view, slot] = source
        for j, device in enumerate(dps):
            send(
                dp_src.at[view, slot],
                dp_buf.at[view, slot, j],
                dp_s.at[view, slot],
                dp_r.at[view, slot],
                device,
            )

    def dp_wait(view, it):
        slot = it % 2
        drain(dp_buf.at[view, slot], dp_r.at[view, slot])
        total = dp_src[view, slot]
        for j in range(len(dps)):
            total = total + dp_buf[view, slot, j]
        return total

    def y_start(view, it):
        slot = it % 2
        if it >= 2:
            drain(y_buf.at[view, slot], y_s.at[view, slot])
        y_src[view, slot] = row_ref[view]
        for j, device in enumerate(ys):
            send(
                y_src.at[view, slot],
                y_buf.at[view, slot, j],
                y_s.at[view, slot],
                y_r.at[view, slot],
                device,
            )

    def y_wait(view, it):
        slot = it % 2
        drain(y_buf.at[view, slot], y_r.at[view, slot])
        total = y_src[view, slot]
        for j in range(len(ys)):
            total = total + y_buf[view, slot, j]
        if it >= 2:
            drain(z_buf.at[view, slot], z_s.at[view, slot])
        z_src[view, slot] = total
        for j, device in enumerate(zs):
            send(
                z_src.at[view, slot],
                z_buf.at[view, slot, j],
                z_s.at[view, slot],
                z_r.at[view, slot],
                device,
            )

    def z_wait(view, it):
        slot = it % 2
        drain(z_buf.at[view, slot], z_r.at[view, slot])
        total = z_src[view, slot]
        for j in range(len(zs)):
            total = total + z_buf[view, slot, j]
        return total

    def column_totals(view):
        parts = [
            jnp.sum(cs_ref[view, :, t * 128 : (t + 1) * 128], axis=0, keepdims=True)
            for t in range(ptiles)
        ]
        return jnp.concatenate(parts, axis=0)

    def frame_sums(view):
        def step(i, carry):
            rows = pl.ds(pl.multiple_of(i * 64, 64), 64)
            total = jnp.zeros((64, 128), F32)
            for t in range(ptiles):
                e = e_ref[view, rows, t * 128 : (t + 1) * 128]
                total = total + (e * e) * c_ref[view, t : t + 1, :]
            acc_ref[view, rows, :] = total
            return carry

        lax.fori_loop(0, frames // 64, step, 0)
        rows_to_lanes(acc_ref, view, row_ref.at[view], frames)

    def proto_sums(view):
        def step(i, totals):
            rows = pl.ds(pl.multiple_of(i * 32, 32), 32)
            scale = rb_ref[view, rows, :]
            out = []
            for t in range(ptiles):
                e = e_ref[view, rows, t * 128 : (t + 1) * 128]
                out.append(
                    totals[t] + jnp.sum(((e * e) * scale).reshape(4, 8, 128), axis=0)
                )
            return tuple(out)

        totals = lax.fori_loop(
            0, frames // 32, step, tuple(jnp.zeros((8, 128), F32) for _ in range(ptiles))
        )
        for t in range(ptiles):
            cs_ref[view, :, t * 128 : (t + 1) * 128] = totals[t]

    dp_start(1, 0, column_totals(1))
    for d in range(nz // 2):
        zero_block(lax.rem(z + d, nz))
        if d:
            zero_block(lax.rem(z + nz - d, nz))
    ring_wait(nz // 2)
    zero_block(lax.rem(z + nz // 2, nz))
    dp_start(0, 0, column_totals(0))

    for view in range(2):
        rows_to_lanes(soft_acc_ref, view, soft_src.at[pl.ds(view * fdense, fdense)], frames)
    for j, device in enumerate(ys):
        send(soft_src, soft_ybuf.at[j], soft_s.at[0], soft_r.at[0], device)

    eye = jnp.where(
        lax.broadcasted_iota(jnp.int32, (width, width), 0)
        == lax.broadcasted_iota(jnp.int32, (width, width), 1),
        1.0,
        0.0,
    ).astype(BF16)

    def transpose_view(view):
        for i in range(frames // chunk):
            if view:
                block = partner_ref[i * chunk : (i + 1) * chunk, :]
            else:
                count = chunk // group
                block = v_ref[0, i * count : (i + 1) * count].reshape(chunk, width)
            ut_ref[view, :, i * chunk : (i + 1) * chunk] = lax.dot_general(
                eye, block, NT, preferred_element_type=F32
            ).astype(BF16)

    transpose_view(1)

    for it in range(ITERS):
        for view in (1, 0):
            c_ref[view] = 1.0 / dp_wait(view, it)
            frame_sums(view)
            y_start(view, it)
        if it == 0:
            transpose_view(0)
            drain(soft_ybuf, soft_r.at[0])
            total = soft_src[...]
            for j in range(len(ys)):
                total = total + soft_ybuf[j]
            soft_mid[...] = total
        for view in (1, 0):
            y_wait(view, it)
        if it == 0:
            for j, device in enumerate(zs):
                send(soft_mid, soft_zbuf.at[j], soft_s.at[1], soft_r.at[1], device)
        if it == 1:
            drain(soft_zbuf, soft_r.at[1])
            total = soft_mid[...]
            for j in range(len(zs)):
                total = total + soft_zbuf[j]
            soft_mid_total = total
            for view in range(2):
                dense = soft_mid_total[view * fdense : (view + 1) * fdense]
                lanes_to_rows(grad_scale / dense, sb_ref, view, frames)
                r_ref[2 + view] = jnp.log(dense)
        if it == ITERS - 1:
            def step(i, carry):
                rows = pl.ds(pl.multiple_of(i * 32, 32), 32)
                sums = [jnp.zeros((32, 128), F32), jnp.zeros((32, 128), F32)]
                for t in range(ptiles):
                    e = [e_ref[v, rows, t * 128 : (t + 1) * 128] for v in range(2)]
                    for v in range(2):
                        term = (e[v] * e[v]) * c_ref[v, t : t + 1, :]
                        sums[v] = sums[v] + term * jnp.log(e[1 - v])
                for v in range(2):
                    acc_ref[v, rows, :] = sums[v]
                return carry

            lax.fori_loop(0, frames // 32, step, 0)
            for v in range(2):
                rows_to_lanes(acc_ref, v, t_ref.at[v], frames)
        for view in (1, 0):
            r = 1.0 / z_wait(view, it)
            r_ref[view] = r
            if it < ITERS - 1:
                lanes_to_rows(r, rb_ref, view, frames)
                proto_sums(view)
                dp_start(view, it + 1, column_totals(view))
            else:
                lanes_to_rows(r * grad_scale, rb_ref, view, frames)

    loss = jnp.zeros((fdense, 128), F32)
    for v in range(2):
        loss = loss + r_ref[v] * (r_ref[3 - v] * row_ref[v] - t_ref[v])
    loss_src[0] = loss
    for j, device in enumerate(ys):
        send(loss_src.at[0], loss_ybuf.at[j], loss_s.at[0], loss_r.at[0], device)

    def loss_step(stage, buf, nextbuf, partners):
        drain(buf, loss_r.at[stage])
        total = loss_src[stage]
        for j in range(buf.shape[0]):
            total = total + buf[j]
        if nextbuf is None:
            return total
        loss_src[stage + 1] = total
        for j, device in enumerate(partners):
            send(
                loss_src.at[stage + 1],
                nextbuf.at[j],
                loss_s.at[stage + 1],
                loss_r.at[stage + 1],
                device,
            )
        return total

    def block_grad(owner, out):
        def weigh(i, carry):
            rows = pl.ds(pl.multiple_of(i * 64, 64), 64)
            for t in range(tiles_pr):
                tile = owner * tiles_pr + t
                cols = pl.ds(pl.multiple_of(tile * 128, 128), 128)
                e = [e_ref[v, rows, cols] for v in range(2)]
                assigned = [
                    (e[v] * e[v]) * (rb_ref[v, rows, :] * c_ref[v, pl.ds(tile, 1), :])
                    for v in range(2)
                ]
                for v in range(2):
                    w_ref[v, rows, t * 128 : (t + 1) * 128] = (
                        e[v] * sb_ref[v, rows, :] - assigned[1 - v]
                    ).astype(BF16)
            return carry

        lax.fori_loop(0, frames // 64, weigh, 0)
        mrows = min(256, width)
        for m in range(width // mrows):
            rows = slice(m * mrows, (m + 1) * mrows)
            total = lax.dot_general(
                ut_ref[0, rows, :], w_ref[0], NN, preferred_element_type=F32
            ) + lax.dot_general(
                ut_ref[1, rows, :], w_ref[1], NN, preferred_element_type=F32
            )
            out[rows, :] = total.astype(out.dtype)

    order = sorted(range(nx), key=lambda d: -min(d, nx - d))
    for k, d in enumerate(order):
        xt = lax.rem(x + d, nx)
        block_grad(xt * CORES + (1 - core), ss_ref.at[k])
        send(ss_ref.at[k], sr_ref.at[k], ss_s, ss_r.at[k], sib)
        block_grad(xt * CORES + core, g_ref)
        drain(sr_ref.at[k], ss_r.at[k])
        if d:
            xs_ref[d - 1] = (g_ref[...] + sr_ref[k].astype(F32)).astype(BF16)
            send(xs_ref.at[d - 1], xr_ref.at[d - 1], xs_s, xs_r, xs[d - 1])
        else:
            g_ref[...] = g_ref[...] + sr_ref[k].astype(F32)
        if k == 1:
            loss_step(0, loss_ybuf, loss_zbuf, zs)
    loss_step(1, loss_zbuf, loss_xbuf, dps)
    drain(xr_ref, xs_r)
    for i in range(width // 128):
        for t in range(tiles_pr):
            rows, cols = slice(i * 128, (i + 1) * 128), slice(t * 128, (t + 1) * 128)
            total = g_ref[rows, cols]
            for j in range(nx - 1):
                total = total + xr_ref[j, rows, cols].astype(F32)
            grad_ref[cols, rows] = total.T
    total = loss_step(2, loss_xbuf, None, None)
    loss_ref[0, 0] = jnp.sum(total) / (2.0 * frames * nx * CORES)

    drain(v_ref.at[0, 0, pl.ds(0, ny - 1)], ay_s)
    for step in range(1, nz // 2 + 1):
        up, down = ring_blocks(step)
        drain(up, az_s.at[0, step - 1])
        drain(down, az_s.at[1, step - 1])
    drain(v_ref.at[1, pl.ds(0, nz - 1), 0], bz_s)
    drain(v_ref.at[1, :, pl.ds(0, ny - 1)], by_s)
    drain(p_ref.at[pl.ds(0, nx - 1)], px_s)
    drain(p_ref.at[pl.ds(0, nx)], ps_s)
    for view in range(2):
        for slot in range(min(2, ITERS)):
            drain(dp_buf.at[view, slot], dp_s.at[view, slot])
            drain(y_buf.at[view, slot], y_s.at[view, slot])
            drain(z_buf.at[view, slot], z_s.at[view, slot])
    drain(soft_ybuf, soft_s.at[0])
    drain(soft_zbuf, soft_s.at[1])
    drain(loss_ybuf, loss_s.at[0])
    drain(loss_zbuf, loss_s.at[1])
    drain(loss_xbuf, loss_s.at[2])
    drain(sr_ref, ss_s)
    drain(xr_ref, xs_s)


def solution(mesh):
    ndp, nproto = mesh.shape["dp"], mesh.shape["proto"]
    nx, nz = ndp // CORES, DEPTH
    ny = nproto // nz

    def local(first, second, protos, pairing):
        fr, width = first.shape
        pr = protos.shape[0]
        frames = fr * nproto
        cols = pr * ndp
        fd = frames // 128
        ct = cols // 128
        sem = pltpu.SemaphoreType.DMA
        sizes = (nx, ny, nz, fr, width, pr)
        vmem = pltpu.VMEM
        grad, loss = pl.pallas_call(
            functools.partial(kernel, sizes),
            out_shape=(
                jax.ShapeDtypeStruct((pr, width), F32),
                jax.ShapeDtypeStruct((1, 1), F32),
            ),
            in_specs=[pl.BlockSpec(memory_space=pltpu.VMEM)] * 4,
            out_specs=(
                pl.BlockSpec(memory_space=pltpu.VMEM),
                pl.BlockSpec(memory_space=pltpu.SMEM),
            ),
            scratch_shapes=[
                vmem((2, nz, ny, fr, width), BF16),
                vmem((frames, width), BF16),
                vmem((ndp, pr, width), BF16),
                vmem((frames, frames), BF16),
                vmem((2, width, frames), BF16),
                vmem((2, frames, cols), F32),
                vmem((2, frames, 128), F32),
                vmem((2, frames, 128), F32),
                vmem((2, frames, 128), F32),
                vmem((2, frames, 128), F32),
                vmem((2, 8, cols), F32),
                vmem((2, ct, 128), F32),
                vmem((4, fd, 128), F32),
                vmem((2, fd, 128), F32),
                vmem((2, fd, 128), F32),
                vmem((2, frames, pr), BF16),
                vmem((width, pr), F32),
                vmem((2, 2, ct, 128), F32),
                vmem((2, 2, ndp - 1, ct, 128), F32),
                vmem((2, 2, fd, 128), F32),
                vmem((2, 2, ny - 1, fd, 128), F32),
                vmem((2, 2, fd, 128), F32),
                vmem((2, 2, nz - 1, fd, 128), F32),
                vmem((2 * fd, 128), F32),
                vmem((ny - 1, 2 * fd, 128), F32),
                vmem((2 * fd, 128), F32),
                vmem((nz - 1, 2 * fd, 128), F32),
                vmem((3, fd, 128), F32),
                vmem((ny - 1, fd, 128), F32),
                vmem((nz - 1, fd, 128), F32),
                vmem((ndp - 1, fd, 128), F32),
                vmem((nx, width, pr), BF16),
                vmem((nx, width, pr), BF16),
                vmem((nx - 1, width, pr), BF16),
                vmem((nx - 1, width, pr), BF16),
                sem, sem,
                sem((2, nz // 2)), sem((2, nz // 2)),
                sem, sem((nz - 1,)),
                sem, sem,
                sem, sem((nx - 1,)),
                sem, sem,
                sem((2, 2)), sem((2, 2)),
                sem((2, 2)), sem((2, 2)),
                sem((2, 2)), sem((2, 2)),
                sem((2,)), sem((2,)),
                sem((3,)), sem((3,)),
                sem, sem((nx,)),
                sem, sem,
            ],
            compiler_params=pltpu.CompilerParams(
                collective_id=0, has_side_effects=True, vmem_limit_bytes=56 * 2**20
            ),
        )(first, second, protos, pairing.reshape(fd, 128))
        return grad, loss[0, 0]

    return jax.shard_map(
        local,
        mesh=mesh,
        in_specs=(
            P(("dp", "proto"), None),
            P(("dp", "proto"), None),
            P(("dp", "proto"), None),
            P("dp"),
        ),
        out_specs=(P(("dp", "proto"), None), P()),
        check_vma=False,
    )
```

```python
import functools
import math

import jax
import jax.numpy as jnp
from jax import lax
from jax.experimental import pallas as pl
from jax.experimental.pallas import tpu as pltpu
from jax.sharding import PartitionSpec as P

ITERS = 3
SOFT_TEMP = 0.1
LOG2_E = math.log2(math.e)
NORM_EPS = 1e-06
CORES = 2
DEPTH = 8

F32 = jnp.float32
BF16 = jnp.bfloat16
NT = (((1,), (1,)), ((), ()))
NN = (((1,), (0,)), ((), ()))


def unit_rows(matrix):
    widened = matrix.astype(F32)
    return (
        widened * lax.rsqrt(jnp.sum(widened * widened, axis=-1, keepdims=True) + NORM_EPS)
    ).astype(BF16)


def drain(ref, sem):
    pltpu.make_async_copy(ref, ref, sem).wait()


def rows_to_lanes(acc_ref, view, out_ref, rows):
    for b in range(rows // 128):
        block = acc_ref[view, b * 128 : (b + 1) * 128, :]
        out_ref[b : b + 1, :] = jnp.sum(block.T, axis=0, keepdims=True)


def lanes_to_rows(dense, out_ref, view, rows):
    for b in range(rows // 128):
        block = jnp.broadcast_to(dense[b : b + 1, :], (128, 128))
        out_ref[view, b * 128 : (b + 1) * 128, :] = block.T


def kernel(
    sizes,
    first_ref,
    second_ref,
    protos_ref,
    pair_ref,
    grad_ref,
    loss_ref,
    v_ref,
    partner_ref,
    p_ref,
    onehot_ref,
    ut_ref,
    k_ref,
    acc_ref,
    soft_acc_ref,
    rb_ref,
    sb_ref,
    cs_ref,
    c_ref,
    r_ref,
    row_ref,
    t_ref,
    w_ref,
    g_ref,
    dp_src,
    dp_buf,
    y_src,
    y_buf,
    z_src,
    z_buf,
    soft_src,
    soft_ybuf,
    soft_mid,
    soft_zbuf,
    loss_src,
    loss_ybuf,
    loss_zbuf,
    loss_xbuf,
    ss_ref,
    sr_ref,
    xs_ref,
    xr_ref,
    ay_s,
    ay_r,
    az_s,
    az_r,
    bz_s,
    bz_r,
    by_s,
    by_r,
    px_s,
    px_r,
    ps_s,
    ps_r,
    dp_s,
    dp_r,
    y_s,
    y_r,
    z_s,
    z_r,
    soft_s,
    soft_r,
    loss_s,
    loss_r,
    ss_s,
    ss_r,
    xs_s,
    xs_r,
):
    nx, ny, nz, fr, width, pr = sizes
    frames = fr * ny * nz
    group = fr * ny
    protos = pr * nx * CORES
    ptiles = protos // 128
    tiles_pr = pr // 128
    fdense = frames // 128
    grad_scale = protos * ny * nz / (SOFT_TEMP * math.sqrt(2.0 * frames * nx * CORES))

    dp, pi = lax.axis_index("dp"), lax.axis_index("proto")
    x, core = dp // CORES, dp % CORES
    y, z = pi // nz, pi % nz

    def at(dx=0, dc=0, dy=0, dz=0):
        return {
            "dp": lax.rem(x + dx, nx) * CORES + lax.rem(core + dc, CORES),
            "proto": lax.rem(y + dy, ny) * nz + lax.rem(z + dz, nz),
        }

    def send(src, dst, ssem, rsem, device):
        pltpu.make_async_remote_copy(
            src_ref=src,
            dst_ref=dst,
            send_sem=ssem,
            recv_sem=rsem,
            device_id=device,
            device_id_type=pl.DeviceIdType.MESH,
        ).start()

    sib = at(dc=1)
    xs = [at(dx=d) for d in range(1, nx)]
    ys = [at(dy=d) for d in range(1, ny)]
    zs = [at(dz=d) for d in range(1, nz)]
    dps = [at(dx=d, dc=e) for d in range(nx) for e in range(CORES) if d or e]

    half = ny // 2
    last = nz // 2

    def ring_ways(step, q):
        return [way for way in range(2) if step < last or (q < half) == (way == 0)]

    def ring_chunk(step, q, way):
        far = nz - step if way == 0 else step
        return v_ref.at[0, lax.rem(z + far, nz), lax.rem(y + ny - q, ny)]

    def ring_send(step, q):
        for way in ring_ways(step, q):
            chunk = ring_chunk(step - 1, q, way)
            to = zs[0] if way == 0 else zs[nz - 2]
            send(chunk, chunk, az_s, az_r.at[way, step - 1, q], to)

    def ring_wait(step, q):
        for way in ring_ways(step, q):
            drain(ring_chunk(step, q, way), az_r.at[way, step - 1, q])

    barrier = pltpu.get_barrier_semaphore()
    for device in dps + ys + zs:
        pl.semaphore_signal(
            barrier, inc=1, device_id=device, device_id_type=pl.DeviceIdType.MESH
        )
    v_ref[0, z, y] = unit_rows(first_ref[...])
    v_ref[1, z, y] = unit_rows(second_ref[...])
    p_ref[dp] = unit_rows(protos_ref[...])
    pl.semaphore_wait(barrier, len(dps) + len(ys) + len(zs))

    for j, device in enumerate(ys):
        send(v_ref.at[0, z, y], v_ref.at[0, z, y], ay_s, ay_r.at[j], device)
    ring_send(1, 0)
    for j, device in enumerate(xs):
        send(p_ref.at[dp], p_ref.at[dp], px_s, px_r.at[j], device)
    for d in sorted(range(1, nz), key=lambda d: min(d, nz - d)):
        send(v_ref.at[1, z, y], v_ref.at[1, z, y], bz_s, bz_r.at[d - 1], zs[d - 1])
    for device in ys:
        send(v_ref.at[1, z, y], v_ref.at[1, z, y], by_s, by_r, device)
    send(p_ref.at[dp], p_ref.at[dp], ps_s, ps_r, sib)

    pair = pair_ref[...]
    where = (pair % (nz * fr) // fr) * group + (pair // (nz * fr)) * fr + pair % fr
    where = where.astype(F32)
    for b in range(fdense):
        column = jnp.broadcast_to(where[b : b + 1, :], (128, 128)).T
        for t in range(fdense):
            lane = (lax.broadcasted_iota(jnp.int32, (128, 128), 1) + t * 128).astype(F32)
            block = jnp.where(column == lane, 1.0, 0.0).astype(BF16)
            for q in range(128 // fr):
                natural = b * 128 + q * fr
                row = (natural % (nz * fr) // fr) * group + natural // (nz * fr) * fr
                onehot_ref[row : row + fr, t * 128 : (t + 1) * 128] = block[
                    q * fr : (q + 1) * fr, :
                ]
    cs_ref[...] = jnp.zeros_like(cs_ref)
    soft_acc_ref[...] = jnp.zeros_like(soft_acc_ref)

    def wait_frames_z(d):
        zb = lax.rem(z + nz - d, nz)
        drain(v_ref.at[1, zb, y], bz_r.at[d - 1])
        for device in ys:
            send(v_ref.at[1, zb, y], v_ref.at[1, zb, y], by_s, by_r, device)

    def wait_protos_x(j):
        owner = lax.rem(x + nx - (j + 1), nx) * CORES + core
        drain(p_ref.at[owner], px_r.at[j])
        send(p_ref.at[owner], p_ref.at[owner], ps_s, ps_r, sib)

    def first_pass(view, starts, block):
        count = block.shape[0]
        each = count // len(starts)
        soft = jnp.zeros((count, 128), F32)
        for j in range(nx * CORES):
            scores = lax.dot_general(block, p_ref[j], NT, preferred_element_type=F32)
            e = jnp.exp2(scores * (LOG2_E / SOFT_TEMP))
            k = e * e
            for i, start in enumerate(starts):
                rows = pl.ds(pl.multiple_of(start, each), each)
                k_ref[view, rows, j * pr : (j + 1) * pr] = k[i * each : (i + 1) * each]
            for t in range(tiles_pr):
                soft = soft + e[:, t * 128 : (t + 1) * 128]
            cs_ref[view, :, j * pr : (j + 1) * pr] += jnp.sum(
                k.reshape(count // 8, 8, pr), axis=0
            )
        for i, start in enumerate(starts):
            rows = pl.ds(pl.multiple_of(start, each), each)
            soft_acc_ref[view, rows, :] = soft[i * each : (i + 1) * each]

    def zero_pair(one, two):
        block = jnp.concatenate(
            [v_ref[0, one].reshape(group, width), v_ref[0, two].reshape(group, width)], axis=0
        )
        first_pass(0, [one * group, two * group], block)

    def frames_y(j):
        drain(v_ref.at[0, z, lax.rem(y + ny - (j + 1), ny)], ay_r.at[j])
        ring_send(1, j + 1)

    def ring_next(step, q):
        ring_wait(step, q)
        ring_send(step + 1, q)

    events = []
    for j in range(ny - 1):
        events.append((3.6 + 0.3 * j, functools.partial(frames_y, j)))
    for step in range(1, last):
        for q in range(ny):
            when = (4.5 if q else 0.0) + 3.3 * step + 0.65 * q
            events.append((when, functools.partial(ring_next, step, q)))
    for d in range(1, nz):
        when = 3.0 + 1.7 * min(d, nz - d) + 0.01 * d
        events.append((when, functools.partial(wait_frames_z, d)))
    for j in range(nx - 1):
        when = 6.0 + 3.5 * min(j + 1, nx - j - 1) + 0.01 * j
        events.append((when, functools.partial(wait_protos_x, j)))
    for when, event in sorted(events, key=lambda pair: pair[0]):
        event()
    drain(p_ref.at[pl.ds(0, nx)], ps_r)
    drain(v_ref.at[1, :, pl.ds(0, ny - 1)], by_r)

    chunk = min(256, frames)

    def permute(i, carry):
        rows = pl.ds(pl.multiple_of(i * chunk, chunk), chunk)
        partner_ref[rows, :] = lax.dot_general(
            onehot_ref[rows, :],
            v_ref[1].reshape(frames, width),
            NN,
            preferred_element_type=F32,
        ).astype(BF16)
        first_pass(1, [i * chunk], partner_ref[rows, :])
        return carry

    lax.fori_loop(0, frames // chunk, permute, 0)

    def dp_start(view, it, source):
        slot = it % 2
        if it >= 2:
            drain(dp_buf.at[view, slot], dp_s.at[view, slot])
        dp_src[view, slot] = source
        for j, device in enumerate(dps):
            send(
                dp_src.at[view, slot],
                dp_buf.at[view, slot, j],
                dp_s.at[view, slot],
                dp_r.at[view, slot],
                device,
            )

    def dp_wait(view, it):
        slot = it % 2
        drain(dp_buf.at[view, slot], dp_r.at[view, slot])
        total = dp_src[view, slot]
        for j in range(len(dps)):
            total = total + dp_buf[view, slot, j]
        return total

    def y_start(view, it):
        slot = it % 2
        if it >= 2:
            drain(y_buf.at[view, slot], y_s.at[view, slot])
        y_src[view, slot] = row_ref[view]
        for j, device in enumerate(ys):
            send(
                y_src.at[view, slot],
                y_buf.at[view, slot, j],
                y_s.at[view, slot],
                y_r.at[view, slot],
                device,
            )

    def y_wait(view, it):
        slot = it % 2
        drain(y_buf.at[view, slot], y_r.at[view, slot])
        total = y_src[view, slot]
        for j in range(len(ys)):
            total = total + y_buf[view, slot, j]
        if it >= 2:
            drain(z_buf.at[view, slot], z_s.at[view, slot])
        z_src[view, slot] = total
        for j, device in enumerate(zs):
            send(
                z_src.at[view, slot],
                z_buf.at[view, slot, j],
                z_s.at[view, slot],
                z_r.at[view, slot],
                device,
            )

    def z_wait(view, it):
        slot = it % 2
        drain(z_buf.at[view, slot], z_r.at[view, slot])
        total = z_src[view, slot]
        for j in range(len(zs)):
            total = total + z_buf[view, slot, j]
        return total

    def column_totals(view):
        parts = [
            jnp.sum(cs_ref[view, :, t * 128 : (t + 1) * 128], axis=0, keepdims=True)
            for t in range(ptiles)
        ]
        return jnp.concatenate(parts, axis=0)

    def frame_sums(view):
        def step(i, carry):
            rows = pl.ds(pl.multiple_of(i * 64, 64), 64)
            total = jnp.zeros((64, 128), F32)
            for t in range(ptiles):
                k = k_ref[view, rows, t * 128 : (t + 1) * 128]
                total = total + k * c_ref[view, t : t + 1, :]
            acc_ref[view, rows, :] = total
            return carry

        lax.fori_loop(0, frames // 64, step, 0)
        rows_to_lanes(acc_ref, view, row_ref.at[view], frames)

    def proto_sums(view):
        def step(i, totals):
            rows = pl.ds(pl.multiple_of(i * 32, 32), 32)
            scale = rb_ref[view, rows, :]
            out = []
            for t in range(ptiles):
                k = k_ref[view, rows, t * 128 : (t + 1) * 128]
                out.append(totals[t] + jnp.sum((k * scale).reshape(4, 8, 128), axis=0))
            return tuple(out)

        totals = lax.fori_loop(
            0, frames // 32, step, tuple(jnp.zeros((8, 128), F32) for _ in range(ptiles))
        )
        for t in range(ptiles):
            cs_ref[view, :, t * 128 : (t + 1) * 128] = totals[t]

    dp_start(1, 0, column_totals(1))

    def pairs(i, carry):
        zero_pair(lax.rem(z + i, nz), lax.rem(z + nz - i, nz))
        return carry

    lax.fori_loop(1, last, pairs, 0)
    for q in range(ny):
        ring_wait(last, q)
    zero_pair(z, lax.rem(z + last, nz))
    dp_start(0, 0, column_totals(0))

    for view in range(2):
        rows_to_lanes(soft_acc_ref, view, soft_src.at[pl.ds(view * fdense, fdense)], frames)
    for j, device in enumerate(ys):
        send(soft_src, soft_ybuf.at[j], soft_s.at[0], soft_r.at[0], device)

    eye = jnp.where(
        lax.broadcasted_iota(jnp.int32, (width, width), 0)
        == lax.broadcasted_iota(jnp.int32, (width, width), 1),
        1.0,
        0.0,
    ).astype(BF16)

    def transpose_view(view):
        for i in range(frames // chunk):
            if view:
                block = partner_ref[i * chunk : (i + 1) * chunk, :]
            else:
                count = chunk // group
                block = v_ref[0, i * count : (i + 1) * count].reshape(chunk, width)
            ut_ref[view, :, i * chunk : (i + 1) * chunk] = lax.dot_general(
                eye, block, NT, preferred_element_type=F32
            ).astype(BF16)

    transpose_view(1)

    for it in range(ITERS):
        for view in (1, 0):
            c_ref[view] = 1.0 / dp_wait(view, it)
            frame_sums(view)
            y_start(view, it)
        if it == 0:
            transpose_view(0)
            drain(soft_ybuf, soft_r.at[0])
            total = soft_src[...]
            for j in range(len(ys)):
                total = total + soft_ybuf[j]
            soft_mid[...] = total
        for view in (1, 0):
            y_wait(view, it)
        if it == 0:
            for j, device in enumerate(zs):
                send(soft_mid, soft_zbuf.at[j], soft_s.at[1], soft_r.at[1], device)
        if it == 1:
            drain(soft_zbuf, soft_r.at[1])
            total = soft_mid[...]
            for j in range(len(zs)):
                total = total + soft_zbuf[j]
            soft_mid_total = total
            for view in range(2):
                dense = soft_mid_total[view * fdense : (view + 1) * fdense]
                lanes_to_rows(grad_scale / dense, sb_ref, view, frames)
                r_ref[2 + view] = jnp.log(dense)
        if it == ITERS - 1:
            def step(i, carry):
                rows = pl.ds(pl.multiple_of(i * 32, 32), 32)
                sums = [jnp.zeros((32, 128), F32), jnp.zeros((32, 128), F32)]
                for t in range(ptiles):
                    k = [k_ref[v, rows, t * 128 : (t + 1) * 128] for v in range(2)]
                    for v in range(2):
                        term = k[v] * c_ref[v, t : t + 1, :]
                        sums[v] = sums[v] + term * jnp.log(k[1 - v])
                for v in range(2):
                    acc_ref[v, rows, :] = 0.5 * sums[v]
                return carry

            lax.fori_loop(0, frames // 32, step, 0)
            for v in range(2):
                rows_to_lanes(acc_ref, v, t_ref.at[v], frames)
        for view in (1, 0):
            r = 1.0 / z_wait(view, it)
            r_ref[view] = r
            if it < ITERS - 1:
                lanes_to_rows(r, rb_ref, view, frames)
                proto_sums(view)
                dp_start(view, it + 1, column_totals(view))
            else:
                lanes_to_rows(r * grad_scale, rb_ref, view, frames)

    loss = jnp.zeros((fdense, 128), F32)
    for v in range(2):
        loss = loss + r_ref[v] * (r_ref[3 - v] * row_ref[v] - t_ref[v])
    loss_src[0] = loss
    for j, device in enumerate(ys):
        send(loss_src.at[0], loss_ybuf.at[j], loss_s.at[0], loss_r.at[0], device)

    def loss_step(stage, buf, nextbuf, partners):
        drain(buf, loss_r.at[stage])
        total = loss_src[stage]
        for j in range(buf.shape[0]):
            total = total + buf[j]
        if nextbuf is None:
            return total
        loss_src[stage + 1] = total
        for j, device in enumerate(partners):
            send(
                loss_src.at[stage + 1],
                nextbuf.at[j],
                loss_s.at[stage + 1],
                loss_r.at[stage + 1],
                device,
            )
        return total

    def block_grad(owner, out):
        def weigh(i, carry):
            rows = pl.ds(pl.multiple_of(i * 64, 64), 64)
            for t in range(tiles_pr):
                tile = owner * tiles_pr + t
                cols = pl.ds(pl.multiple_of(tile * 128, 128), 128)
                k = [k_ref[v, rows, cols] for v in range(2)]
                assigned = [
                    k[v] * (rb_ref[v, rows, :] * c_ref[v, pl.ds(tile, 1), :])
                    for v in range(2)
                ]
                for v in range(2):
                    w_ref[v, rows, t * 128 : (t + 1) * 128] = (
                        (k[v] * lax.rsqrt(k[v])) * sb_ref[v, rows, :] - assigned[1 - v]
                    ).astype(BF16)
            return carry

        lax.fori_loop(0, frames // 64, weigh, 0)
        mrows = min(256, width)
        for m in range(width // mrows):
            rows = slice(m * mrows, (m + 1) * mrows)
            total = lax.dot_general(
                ut_ref[0, rows, :], w_ref[0], NN, preferred_element_type=F32
            ) + lax.dot_general(
                ut_ref[1, rows, :], w_ref[1], NN, preferred_element_type=F32
            )
            out[rows, :] = total.astype(out.dtype)

    order = sorted(range(nx), key=lambda d: -min(d, nx - d))
    for k, d in enumerate(order):
        xt = lax.rem(x + d, nx)
        block_grad(xt * CORES + (1 - core), ss_ref.at[k])
        send(ss_ref.at[k], sr_ref.at[k], ss_s, ss_r.at[k], sib)
        block_grad(xt * CORES + core, g_ref)
        drain(sr_ref.at[k], ss_r.at[k])
        if d:
            xs_ref[d - 1] = (g_ref[...] + sr_ref[k].astype(F32)).astype(BF16)
            send(xs_ref.at[d - 1], xr_ref.at[d - 1], xs_s, xs_r, xs[d - 1])
        else:
            g_ref[...] = g_ref[...] + sr_ref[k].astype(F32)
        if k == 1:
            loss_step(0, loss_ybuf, loss_zbuf, zs)
    loss_step(1, loss_zbuf, loss_xbuf, dps)
    drain(xr_ref, xs_r)
    for i in range(width // 128):
        for t in range(tiles_pr):
            rows, cols = slice(i * 128, (i + 1) * 128), slice(t * 128, (t + 1) * 128)
            total = g_ref[rows, cols]
            for j in range(nx - 1):
                total = total + xr_ref[j, rows, cols].astype(F32)
            grad_ref[cols, rows] = total.T
    total = loss_step(2, loss_xbuf, None, None)
    loss_ref[0, 0] = jnp.sum(total) / (2.0 * frames * nx * CORES)

    drain(v_ref.at[0, 0, pl.ds(0, ny - 1)], ay_s)
    drain(v_ref.at[0, pl.ds(0, nz - 1)], az_s)
    drain(v_ref.at[1, pl.ds(0, nz - 1), 0], bz_s)
    drain(v_ref.at[1, :, pl.ds(0, ny - 1)], by_s)
    drain(p_ref.at[pl.ds(0, nx - 1)], px_s)
    drain(p_ref.at[pl.ds(0, nx)], ps_s)
    for view in range(2):
        for slot in range(min(2, ITERS)):
            drain(dp_buf.at[view, slot], dp_s.at[view, slot])
            drain(y_buf.at[view, slot], y_s.at[view, slot])
            drain(z_buf.at[view, slot], z_s.at[view, slot])
    drain(soft_ybuf, soft_s.at[0])
    drain(soft_zbuf, soft_s.at[1])
    drain(loss_ybuf, loss_s.at[0])
    drain(loss_zbuf, loss_s.at[1])
    drain(loss_xbuf, loss_s.at[2])
    drain(sr_ref, ss_s)
    drain(xr_ref, xs_s)


def solution(mesh):
    ndp, nproto = mesh.shape["dp"], mesh.shape["proto"]
    nx, nz = ndp // CORES, DEPTH
    ny = nproto // nz

    def local(first, second, protos, pairing):
        fr, width = first.shape
        pr = protos.shape[0]
        frames = fr * nproto
        cols = pr * ndp
        fd = frames // 128
        ct = cols // 128
        sem = pltpu.SemaphoreType.DMA
        sizes = (nx, ny, nz, fr, width, pr)
        vmem = pltpu.VMEM
        grad, loss = pl.pallas_call(
            functools.partial(kernel, sizes),
            out_shape=(
                jax.ShapeDtypeStruct((pr, width), F32),
                jax.ShapeDtypeStruct((1, 1), F32),
            ),
            in_specs=[pl.BlockSpec(memory_space=pltpu.VMEM)] * 4,
            out_specs=(
                pl.BlockSpec(memory_space=pltpu.VMEM),
                pl.BlockSpec(memory_space=pltpu.SMEM),
            ),
            scratch_shapes=[
                vmem((2, nz, ny, fr, width), BF16),
                vmem((frames, width), BF16),
                vmem((ndp, pr, width), BF16),
                vmem((frames, frames), BF16),
                vmem((2, width, frames), BF16),
                vmem((2, frames, cols), F32),
                vmem((2, frames, 128), F32),
                vmem((2, frames, 128), F32),
                vmem((2, frames, 128), F32),
                vmem((2, frames, 128), F32),
                vmem((2, 8, cols), F32),
                vmem((2, ct, 128), F32),
                vmem((4, fd, 128), F32),
                vmem((2, fd, 128), F32),
                vmem((2, fd, 128), F32),
                vmem((2, frames, pr), BF16),
                vmem((width, pr), F32),
                vmem((2, 2, ct, 128), F32),
                vmem((2, 2, ndp - 1, ct, 128), F32),
                vmem((2, 2, fd, 128), F32),
                vmem((2, 2, ny - 1, fd, 128), F32),
                vmem((2, 2, fd, 128), F32),
                vmem((2, 2, nz - 1, fd, 128), F32),
                vmem((2 * fd, 128), F32),
                vmem((ny - 1, 2 * fd, 128), F32),
                vmem((2 * fd, 128), F32),
                vmem((nz - 1, 2 * fd, 128), F32),
                vmem((3, fd, 128), F32),
                vmem((ny - 1, fd, 128), F32),
                vmem((nz - 1, fd, 128), F32),
                vmem((ndp - 1, fd, 128), F32),
                vmem((nx, width, pr), BF16),
                vmem((nx, width, pr), BF16),
                vmem((nx - 1, width, pr), BF16),
                vmem((nx - 1, width, pr), BF16),
                sem, sem((ny - 1,)),
                sem, sem((2, nz // 2, ny)),
                sem, sem((nz - 1,)),
                sem, sem,
                sem, sem((nx - 1,)),
                sem, sem,
                sem((2, 2)), sem((2, 2)),
                sem((2, 2)), sem((2, 2)),
                sem((2, 2)), sem((2, 2)),
                sem((2,)), sem((2,)),
                sem((3,)), sem((3,)),
                sem, sem((nx,)),
                sem, sem,
            ],
            compiler_params=pltpu.CompilerParams(
                collective_id=0, has_side_effects=True, vmem_limit_bytes=56 * 2**20
            ),
        )(first, second, protos, pairing.reshape(fd, 128))
        return grad, loss[0, 0]

    return jax.shard_map(
        local,
        mesh=mesh,
        in_specs=(
            P(("dp", "proto"), None),
            P(("dp", "proto"), None),
            P(("dp", "proto"), None),
            P("dp"),
        ),
        out_specs=(P(("dp", "proto"), None), P()),
        check_vma=False,
    )
```

```python
import functools
import math

import jax
import jax.numpy as jnp
from jax import lax
from jax.experimental import pallas as pl
from jax.experimental.pallas import tpu as pltpu
from jax.sharding import PartitionSpec as P

ITERS = 3
SOFT_TEMP = 0.1
LOG2_E = math.log2(math.e)
NORM_EPS = 1e-06
CORES = 2
DEPTH = 8

F32 = jnp.float32
BF16 = jnp.bfloat16
NT = (((1,), (1,)), ((), ()))
NN = (((1,), (0,)), ((), ()))


def unit_rows(matrix):
    widened = matrix.astype(F32)
    return (
        widened * lax.rsqrt(jnp.sum(widened * widened, axis=-1, keepdims=True) + NORM_EPS)
    ).astype(BF16)


def drain(ref, sem):
    pltpu.make_async_copy(ref, ref, sem).wait()


def rows_to_lanes(acc_ref, view, out_ref, rows):
    for b in range(rows // 128):
        block = acc_ref[view, b * 128 : (b + 1) * 128, :]
        out_ref[b : b + 1, :] = jnp.sum(block.T, axis=0, keepdims=True)


def lanes_to_rows(dense, out_ref, view, rows):
    for b in range(rows // 128):
        block = jnp.broadcast_to(dense[b : b + 1, :], (128, 128))
        out_ref[view, b * 128 : (b + 1) * 128, :] = block.T


def kernel(
    sizes,
    first_ref,
    second_ref,
    protos_ref,
    pair_ref,
    grad_ref,
    loss_ref,
    v_ref,
    partner_ref,
    p_ref,
    onehot_ref,
    ut_ref,
    k_ref,
    ka_ref,
    acc_ref,
    soft_acc_ref,
    rb_ref,
    sb_ref,
    cs_ref,
    c_ref,
    r_ref,
    row_ref,
    t_ref,
    w_ref,
    g_ref,
    dp_src,
    dp_buf,
    y_src,
    y_buf,
    z_src,
    z_buf,
    soft_src,
    soft_ybuf,
    soft_mid,
    soft_zbuf,
    loss_src,
    loss_ybuf,
    loss_zbuf,
    loss_xbuf,
    ss_ref,
    sr_ref,
    xs_ref,
    xr_ref,
    xo_ref,
    ay_s,
    ay_r,
    zr_s,
    zr_r,
    zo_s,
    zo_r,
    fy_s,
    fy_r,
    px_s,
    px_r,
    po_r,
    ps_s,
    ps_r,
    dp_s,
    dp_r,
    y_s,
    y_r,
    z_s,
    z_r,
    soft_s,
    soft_r,
    loss_s,
    loss_r,
    ss_s,
    ss_r,
    xs_s,
    xs_r,
    xo_s,
    xo_r,
):
    nx, ny, nz, fr, width, pr = sizes
    frames = fr * ny * nz
    group = fr * ny
    protos = pr * nx * CORES
    ptiles = protos // 128
    tiles_pr = pr // 128
    fdense = frames // 128
    grad_scale = protos * ny * nz / (SOFT_TEMP * math.sqrt(2.0 * frames * nx * CORES))

    dp, pi = lax.axis_index("dp"), lax.axis_index("proto")
    x, core = dp // CORES, dp % CORES
    y, z = pi // nz, pi % nz

    def at(dx=0, dc=0, dy=0, dz=0):
        return {
            "dp": lax.rem(x + dx, nx) * CORES + lax.rem(core + dc, CORES),
            "proto": lax.rem(y + dy, ny) * nz + lax.rem(z + dz, nz),
        }

    def send(src, dst, ssem, rsem, device):
        pltpu.make_async_remote_copy(
            src_ref=src,
            dst_ref=dst,
            send_sem=ssem,
            recv_sem=rsem,
            device_id=device,
            device_id_type=pl.DeviceIdType.MESH,
        ).start()

    sib = at(dc=1)
    xs = [at(dx=d) for d in range(1, nx)]
    ys = [at(dy=d) for d in range(1, ny)]
    zs = [at(dz=d) for d in range(1, nz)]
    dps = [at(dx=d, dc=e) for d in range(nx) for e in range(CORES) if d or e]

    last = nz // 2
    near = max(1, last - 2)
    split = near > 1

    def chunk(dz, q=0):
        return v_ref.at[lax.rem(z + nz + dz, nz), lax.rem(y + ny - q, ny)]

    def ring_send(step, q):
        for way, sign in enumerate((-1, 1)):
            part = chunk(sign * (step - 1), q)
            if q and split and step == near:
                part = part.at[0]
            send(part, part, zr_s.at[min(q, 1)], zr_r.at[way, step - 1, q], zs[0 if way == 0 else nz - 2])

    def ring_skip():
        for way in range(2):
            to = zs[1 if way == 0 else nz - 3]
            send(chunk(0), chunk(0), zr_s.at[0], zr_r.at[way, 1, 0], to)

    def ring_wait(step, q):
        for way, sign in enumerate((-1, 1)):
            part = chunk(sign * step, q)
            drain(part.at[0] if q and split and step == near else part, zr_r.at[way, step - 1, q])

    def far_part(dz):
        return chunk(dz).at[1] if abs(dz) == near else chunk(dz)

    def far_send(dz, index):
        for device in ys:
            send(far_part(dz), far_part(dz), fy_s, fy_r.at[index], device)

    def far_wait(dz, index):
        block = v_ref.at[lax.rem(z + nz + dz, nz), pl.ds(0, ny - 1)]
        drain(block.at[:, 1] if abs(dz) == near else block, fy_r.at[index])

    def far_index(dz):
        if dz == last:
            return 0
        return 2 * (abs(dz) - near) + (1 if dz < 0 else 2)

    half = pr // 2

    def proto_half(dx, part):
        owner = lax.rem(x + nx + dx, nx) * CORES + core
        return p_ref.at[owner, pl.ds(part * half, half)]

    def proto_near(way, part):
        piece = proto_half(-1 if way == 0 else 1, part)
        drain(piece, px_r.at[way, part])
        if part == way:
            send(piece, piece, px_s, po_r.at[part], xs[0 if way == 0 else nx - 2])
        send(piece, piece, ps_s, ps_r, sib)

    def proto_far(part):
        piece = proto_half(2, part)
        drain(piece, po_r.at[part])
        send(piece, piece, ps_s, ps_r, sib)

    barrier = pltpu.get_barrier_semaphore()
    for device in dps + ys + zs:
        pl.semaphore_signal(
            barrier, inc=1, device_id=device, device_id_type=pl.DeviceIdType.MESH
        )
    v_ref[z, y, 0] = unit_rows(first_ref[...])
    v_ref[z, y, 1] = unit_rows(second_ref[...])
    p_ref[dp] = unit_rows(protos_ref[...])
    pl.semaphore_wait(barrier, len(dps) + len(ys) + len(zs))

    for j, device in enumerate(ys):
        send(chunk(0), chunk(0), ay_s, ay_r.at[j], device)
    if last > 2:
        ring_skip()
    send(chunk(0), chunk(0), zo_s, zo_r, zs[last - 1])
    ring_send(1, 0)
    for part in range(2):
        for way in range(2):
            piece = proto_half(0, part if way == 0 else 1 - part)
            where = px_r.at[way, part if way == 0 else 1 - part]
            send(piece, piece, px_s, where, xs[0 if way == 0 else nx - 2])
    send(p_ref.at[dp], p_ref.at[dp], ps_s, ps_r, sib)

    pair = pair_ref[...]
    where = (pair % (nz * fr) // fr) * group + (pair // (nz * fr)) * fr + pair % fr
    where = where.astype(F32)
    for b in range(fdense):
        column = jnp.broadcast_to(where[b : b + 1, :], (128, 128)).T
        for t in range(fdense):
            lane = (lax.broadcasted_iota(jnp.int32, (128, 128), 1) + t * 128).astype(F32)
            block = jnp.where(column == lane, 1.0, 0.0).astype(BF16)
            for q in range(128 // fr):
                natural = b * 128 + q * fr
                row = (natural % (nz * fr) // fr) * group + natural // (nz * fr) * fr
                onehot_ref[row : row + fr, t * 128 : (t + 1) * 128] = block[
                    q * fr : (q + 1) * fr, :
                ]
    cs_ref[...] = jnp.zeros_like(cs_ref)
    soft_acc_ref[...] = jnp.zeros_like(soft_acc_ref)

    def first_pass(view, starts, block):
        count = block.shape[0]
        each = count // len(starts)
        soft = jnp.zeros((count, 128), F32)
        for j in range(nx * CORES):
            scores = lax.dot_general(block, p_ref[j], NT, preferred_element_type=F32)
            e = jnp.exp2(scores * (LOG2_E / SOFT_TEMP))
            k = e * e
            for i, start in enumerate(starts):
                rows = pl.ds(pl.multiple_of(start, each), each)
                k_ref[view, rows, j * pr : (j + 1) * pr] = k[i * each : (i + 1) * each]
            for t in range(tiles_pr):
                soft = soft + e[:, t * 128 : (t + 1) * 128]
            cs_ref[view, :, j * pr : (j + 1) * pr] += jnp.sum(
                k.reshape(count // 8, 8, pr), axis=0
            )
        for i, start in enumerate(starts):
            rows = pl.ds(pl.multiple_of(start, each), each)
            soft_acc_ref[view, rows, :] = soft[i * each : (i + 1) * each]

    def frames_y(q):
        drain(chunk(0, q), ay_r.at[q - 1])
        ring_send(1, q)

    def ring_next(step, q):
        ring_wait(step, q)
        if (1 < step < last - 1) if q == 0 else step < near:
            ring_send(step + 1, q)
        if q == 0 and (step > near or (split and step == near)):
            far_send(-step, far_index(-step))
            far_send(step, far_index(step))

    def opposite():
        drain(chunk(last), zo_r)
        far_send(last, far_index(last))

    events = [(6.5, opposite)]
    for q in range(1, ny):
        events.append((4.0 + 0.5 * q, functools.partial(frames_y, q)))
    for step in range(1, last):
        when = 7.0 if step == 1 else 3.9 + 5.0 * (step - 2)
        events.append((when, functools.partial(ring_next, step, 0)))
    for q in range(1, ny):
        for step in range(1, near):
            when = 6.0 + 3.5 * step + 1.3 * q
            events.append((when, functools.partial(ring_next, step, q)))
    for way in range(2):
        events.append((6.0 + 0.1 * way, functools.partial(proto_near, way, way)))
        events.append((8.6 + 0.1 * way, functools.partial(proto_near, way, 1 - way)))
        events.append((12.0 + 0.1 * way, functools.partial(proto_far, way)))
    for when, event in sorted(events, key=lambda pair: pair[0]):
        event()
    drain(p_ref.at[pl.ds(0, nx)], ps_r)

    def pair_wait(p):
        if p == 0:
            if near == 1:
                for q in range(1, ny):
                    ring_wait(1, q)
        elif p == 1:
            far_wait(last, far_index(last))
        else:
            step = last + 1 - p
            if step <= near:
                for q in range(1, ny):
                    ring_wait(step, q)
            far_wait(-step, far_index(-step))
            far_wait(step, far_index(step))

    def pair_pass(n, carry):
        p, view = n // 2, n % 2
        for known in range(last):

            @pl.when(n == 2 * known)
            def _(known=known):
                pair_wait(known)

        step = lax.max(1, (last + 1 - p) * lax.min(p, 1))
        one = lax.rem(z + step, nz)
        two = lax.rem(z + nz - step * lax.min((p - 1) * (p - 1), 1), nz)
        block = jnp.concatenate(
            [v_ref[b, :, view].reshape(group, width) for b in (one, two)], axis=0
        )
        first_pass(view, [one * group, two * group], block)
        return carry

    lax.fori_loop(0, 2 * last, pair_pass, 0)

    def dp_start(view, it, source):
        slot = it % 2

        @pl.when(it >= 2)
        def _():
            drain(dp_buf.at[view, slot], dp_s.at[view, slot])

        dp_src[view, slot] = source
        for j, device in enumerate(dps):
            send(
                dp_src.at[view, slot],
                dp_buf.at[view, slot, j],
                dp_s.at[view, slot],
                dp_r.at[view, slot],
                device,
            )

    def dp_wait(view, it):
        slot = it % 2
        drain(dp_buf.at[view, slot], dp_r.at[view, slot])
        total = dp_src[view, slot]
        for j in range(len(dps)):
            total = total + dp_buf[view, slot, j]
        return total

    def y_start(view, it):
        slot = it % 2

        @pl.when(it >= 2)
        def _():
            drain(y_buf.at[view, slot], y_s.at[view, slot])

        y_src[view, slot] = row_ref[view]
        for j, device in enumerate(ys):
            send(
                y_src.at[view, slot],
                y_buf.at[view, slot, j],
                y_s.at[view, slot],
                y_r.at[view, slot],
                device,
            )

    def y_wait(view, it):
        slot = it % 2
        drain(y_buf.at[view, slot], y_r.at[view, slot])
        total = y_src[view, slot]
        for j in range(len(ys)):
            total = total + y_buf[view, slot, j]

        @pl.when(it >= 2)
        def _():
            drain(z_buf.at[view, slot], z_s.at[view, slot])

        z_src[view, slot] = total
        for j, device in enumerate(zs):
            send(
                z_src.at[view, slot],
                z_buf.at[view, slot, j],
                z_s.at[view, slot],
                z_r.at[view, slot],
                device,
            )

    def z_wait(view, it):
        slot = it % 2
        drain(z_buf.at[view, slot], z_r.at[view, slot])
        total = z_src[view, slot]
        for j in range(len(zs)):
            total = total + z_buf[view, slot, j]
        return total

    def column_totals(view):
        parts = [
            jnp.sum(cs_ref[view, :, t * 128 : (t + 1) * 128], axis=0, keepdims=True)
            for t in range(ptiles)
        ]
        return jnp.concatenate(parts, axis=0)

    def frame_sums(view):
        def step(b, carry):
            rows = pl.ds(pl.multiple_of(b * 128, 128), 128)
            total = jnp.zeros((128, 128), F32)
            for t in range(ptiles):
                k = k_ref[view, rows, t * 128 : (t + 1) * 128]
                total = total + k * c_ref[view, t : t + 1, :]
            row_ref[view, pl.ds(b, 1), :] = jnp.sum(total.T, axis=0, keepdims=True)
            return carry

        lax.fori_loop(0, fdense, step, 0, unroll=min(4, fdense))

    def proto_sums(view):
        def step(i, totals):
            rows = pl.ds(pl.multiple_of(i * 64, 64), 64)
            scale = rb_ref[view, rows, :]
            out = []
            for t in range(ptiles):
                k = k_ref[view, rows, t * 128 : (t + 1) * 128]
                out.append(totals[t] + jnp.sum((k * scale).reshape(8, 8, 128), axis=0))
            return tuple(out)

        totals = lax.fori_loop(
            0,
            frames // 64,
            step,
            tuple(jnp.zeros((8, 128), F32) for _ in range(ptiles)),
            unroll=2,
        )
        for t in range(ptiles):
            cs_ref[view, :, t * 128 : (t + 1) * 128] = totals[t]

    zero = jnp.int32(0)
    dp_start(1, zero, column_totals(1))
    dp_start(0, zero, column_totals(0))

    for view in range(2):
        rows_to_lanes(soft_acc_ref, view, soft_src.at[pl.ds(view * fdense, fdense)], frames)
    for j, device in enumerate(ys):
        send(soft_src, soft_ybuf.at[j], soft_s.at[0], soft_r.at[0], device)

    eye = jnp.where(
        lax.broadcasted_iota(jnp.int32, (width, width), 0)
        == lax.broadcasted_iota(jnp.int32, (width, width), 1),
        1.0,
        0.0,
    ).astype(BF16)

    rows_each = min(256, frames)
    pieces = frames // rows_each

    def transpose_view(view):
        for i in range(pieces):
            if view:
                block = partner_ref[i * rows_each : (i + 1) * rows_each, :]
            else:
                count = rows_each // group
                block = v_ref[i * count : (i + 1) * count, :, 0].reshape(rows_each, width)
            ut_ref[view, :, i * rows_each : (i + 1) * rows_each] = lax.dot_general(
                eye, block, NT, preferred_element_type=F32
            ).astype(BF16)

    def align_rows():
        second = v_ref[:, :, 1].reshape(frames, width)
        for i in range(pieces):
            rows = slice(i * rows_each, (i + 1) * rows_each)
            partner_ref[rows, :] = lax.dot_general(
                onehot_ref[rows, :], second, NN, preferred_element_type=F32
            ).astype(BF16)

    def align_kernel(first, count):
        def step(i, carry):
            rows = pl.ds(pl.multiple_of(i * rows_each, rows_each), rows_each)
            block = partner_ref[rows, :]
            for j in range(nx * CORES):
                scores = lax.dot_general(block, p_ref[j], NT, preferred_element_type=F32)
                ka_ref[rows, j * pr : (j + 1) * pr] = jnp.exp2(
                    scores * (2.0 * LOG2_E / SOFT_TEMP)
                )
            return carry

        lax.fori_loop(first, first + count, step, 0)

    def align_dense(dense):
        row = jnp.concatenate([dense[b : b + 1, :] for b in range(fdense)], axis=1)
        high = row.astype(BF16).astype(F32)
        middle = (row - high).astype(BF16).astype(F32)
        low = row - high - middle
        parts = jnp.concatenate([high, middle, low, jnp.zeros((13, frames), F32)], axis=0)
        out = lax.dot_general(
            parts.astype(BF16), onehot_ref[...], NT, preferred_element_type=F32
        )
        total = out[0:1] + out[1:2] + out[2:3]
        return jnp.concatenate(
            [total[:, b * 128 : (b + 1) * 128] for b in range(fdense)], axis=0
        )

    transpose_view(0)
    align_rows()

    def soft_rows():
        total = soft_src[...]
        drain(soft_ybuf, soft_r.at[0])
        for j in range(len(ys)):
            total = total + soft_ybuf[j]
        soft_mid[...] = total

    def soft_totals():
        drain(soft_zbuf, soft_r.at[1])
        total = soft_mid[...]
        for j in range(len(zs)):
            total = total + soft_zbuf[j]
        transpose_view(1)
        for view in range(2):
            dense = total[view * fdense : (view + 1) * fdense]
            if view:
                dense = align_dense(dense)
            lanes_to_rows(grad_scale / dense, sb_ref, view, frames)
            r_ref[2 + view] = jnp.log(dense)

    def cross_sums():
        def step(i, carry):
            rows = pl.ds(pl.multiple_of(i * 32, 32), 32)
            sums = [jnp.zeros((32, 128), F32) for _ in range(3)]
            for t in range(ptiles):
                k = [ref[rows, t * 128 : (t + 1) * 128] for ref in (k_ref.at[0], ka_ref)]
                terms = [k[v] * c_ref[v, t : t + 1, :] for v in range(2)]
                sums[0] = sums[0] + terms[0] * jnp.log(k[1])
                sums[1] = sums[1] + terms[1] * jnp.log(k[0])
                sums[2] = sums[2] + terms[1]
            acc_ref[0, rows, :] = 0.5 * sums[0]
            acc_ref[1, rows, :] = 0.5 * sums[1]
            soft_acc_ref[1, rows, :] = sums[2]
            return carry

        lax.fori_loop(0, frames // 32, step, 0)
        for v in range(2):
            rows_to_lanes(acc_ref, v, t_ref.at[v], frames)
        rows_to_lanes(soft_acc_ref, 1, row_ref.at[1], frames)

    def sweep(it, carry):
        for view in (1, 0):
            c_ref[view] = 1.0 / dp_wait(view, it)
            frame_sums(view)
            y_start(view, it)

        @pl.when(it == 0)
        def _():
            align_kernel(0, pieces // 2)
            soft_rows()

        for view in (1, 0):
            y_wait(view, it)

        @pl.when(it == 0)
        def _():
            for j, device in enumerate(zs):
                send(soft_mid, soft_zbuf.at[j], soft_s.at[1], soft_r.at[1], device)
            align_kernel(pieces // 2, pieces - pieces // 2)

        @pl.when(it == 1)
        def _():
            soft_totals()

        @pl.when(it == ITERS - 1)
        def _():
            cross_sums()

        for view in (1, 0):
            r_ref[view] = 1.0 / z_wait(view, it)

            @pl.when(it < ITERS - 1)
            def _(view=view):
                lanes_to_rows(r_ref[view], rb_ref, view, frames)
                proto_sums(view)
                dp_start(view, it + 1, column_totals(view))

            @pl.when(it == ITERS - 1)
            def _(view=view):
                if view:
                    r_ref[view] = align_dense(r_ref[view])
                lanes_to_rows(r_ref[view] * grad_scale, rb_ref, view, frames)

        return carry

    lax.fori_loop(0, ITERS, sweep, 0)

    loss = jnp.zeros((fdense, 128), F32)
    for v in range(2):
        loss = loss + r_ref[v] * (r_ref[3 - v] * row_ref[v] - t_ref[v])
    loss_src[0] = loss
    for j, device in enumerate(ys):
        send(loss_src.at[0], loss_ybuf.at[j], loss_s.at[0], loss_r.at[0], device)

    def loss_step(stage, buf, nextbuf, partners):
        drain(buf, loss_r.at[stage])
        total = loss_src[stage]
        for j in range(buf.shape[0]):
            total = total + buf[j]
        if nextbuf is None:
            return total
        loss_src[stage + 1] = total
        for j, device in enumerate(partners):
            send(
                loss_src.at[stage + 1],
                nextbuf.at[j],
                loss_s.at[stage + 1],
                loss_r.at[stage + 1],
                device,
            )
        return total

    def block_grad(owner):
        count = min(64, frames)
        for start in range(0, frames, count):
            rows = slice(start, start + count)
            for t in range(tiles_pr):
                tile = owner * tiles_pr + t
                cols = pl.ds(pl.multiple_of(tile * 128, 128), 128)
                k = [ref[rows, cols] for ref in (k_ref.at[0], ka_ref)]
                assigned = [
                    k[v] * (rb_ref[v, rows, :] * c_ref[v, pl.ds(tile, 1), :])
                    for v in range(2)
                ]
                for v in range(2):
                    w_ref[v, rows, t * 128 : (t + 1) * 128] = (
                        (k[v] * lax.rsqrt(k[v])) * sb_ref[v, rows, :] - assigned[1 - v]
                    ).astype(BF16)
        total = lax.dot_general(ut_ref[0], w_ref[0], NN, preferred_element_type=F32)
        total = total + lax.dot_general(ut_ref[1], w_ref[1], NN, preferred_element_type=F32)
        return total

    middle = width // 2
    lower, upper = pl.ds(0, middle), pl.ds(middle, middle)
    right, left = xs[0], xs[nx - 2]
    def scatter(n, carry):
        k, own = n // 2, n % 2
        d = (2 + 3 * k + (k // 2) * (3 - 2 * (k % 2))) % 4
        g_ref[k] = block_grad(lax.rem(x + d, nx) * CORES + lax.rem(core + 1 + own, CORES))

        @pl.when(own == 0)
        def _():
            ss_ref[k] = g_ref[k].astype(BF16)
            send(ss_ref.at[k], sr_ref.at[k], ss_s, ss_r.at[k], sib)

        @pl.when(own == 1)
        def _():
            drain(sr_ref.at[k], ss_r.at[k])

        @pl.when(n == 1)
        def _():
            xs_ref[0] = (g_ref[0] + sr_ref[0].astype(F32)).astype(BF16)
            send(xs_ref.at[0, lower], xo_ref.at[0], xo_s, xo_r.at[0], right)
            send(xs_ref.at[0, upper], xo_ref.at[1], xo_s, xo_r.at[1], left)

        @pl.when(n == 3)
        def _():
            xs_ref[1, upper] = (g_ref[1, upper] + sr_ref[1, upper].astype(F32)).astype(BF16)
            send(xs_ref.at[1, upper], xr_ref.at[0, upper], xs_s, xs_r, right)
            loss_step(0, loss_ybuf, loss_zbuf, zs)

        @pl.when(n == 5)
        def _():
            xs_ref[2, lower] = (g_ref[2, lower] + sr_ref[2, lower].astype(F32)).astype(BF16)
            send(xs_ref.at[2, lower], xr_ref.at[1, lower], xs_s, xs_r, left)
            for way, (rows, to) in enumerate(((lower, right), (upper, left))):
                drain(xo_ref.at[way], xo_r.at[way])
                xs_ref[1 + way, rows] = (
                    g_ref[1 + way, rows]
                    + sr_ref[1 + way, rows].astype(F32)
                    + xo_ref[way].astype(F32)
                ).astype(BF16)
                send(xs_ref.at[1 + way, rows], xr_ref.at[way, rows], xs_s, xs_r, to)

        return carry

    lax.fori_loop(0, 2 * nx, scatter, 0)
    loss_step(1, loss_zbuf, loss_xbuf, dps)
    drain(xr_ref, xs_r)
    for i in range(width // 128):
        for t in range(tiles_pr):
            rows, cols = slice(i * 128, (i + 1) * 128), slice(t * 128, (t + 1) * 128)
            total = g_ref[3, rows, cols] + sr_ref[3, rows, cols].astype(F32)
            for j in range(2):
                total = total + xr_ref[j, rows, cols].astype(F32)
            grad_ref[cols, rows] = total.T
    total = loss_step(2, loss_xbuf, None, None)
    loss_ref[0, 0] = jnp.sum(total) / (2.0 * frames * nx * CORES)

    drain(v_ref.at[0, pl.ds(0, ny - 1)], ay_s)
    drain(v_ref.at[pl.ds(0, 2 * (last - 1)), 0], zr_s.at[0])
    drain(v_ref.at[pl.ds(0, 2 * near - split), pl.ds(0, ny - 1)], zr_s.at[1])
    drain(chunk(0), zo_s)
    drain(v_ref.at[pl.ds(0, 2 * (last - 1 - near) + 1 + split), pl.ds(0, ny - 1)], fy_s)
    drain(p_ref.at[pl.ds(0, 3)], px_s)
    drain(p_ref.at[pl.ds(0, nx)], ps_s)
    for view in range(2):
        for slot in range(min(2, ITERS)):
            drain(dp_buf.at[view, slot], dp_s.at[view, slot])
            drain(y_buf.at[view, slot], y_s.at[view, slot])
            drain(z_buf.at[view, slot], z_s.at[view, slot])
    drain(soft_ybuf, soft_s.at[0])
    drain(soft_zbuf, soft_s.at[1])
    drain(loss_ybuf, loss_s.at[0])
    drain(loss_zbuf, loss_s.at[1])
    drain(loss_xbuf, loss_s.at[2])
    drain(sr_ref, ss_s)
    drain(xo_ref, xo_s)
    drain(xr_ref, xs_s)


def solution(mesh):
    ndp, nproto = mesh.shape["dp"], mesh.shape["proto"]
    nx, nz = ndp // CORES, DEPTH
    ny = nproto // nz

    def local(first, second, protos, pairing):
        fr, width = first.shape
        pr = protos.shape[0]
        frames = fr * nproto
        cols = pr * ndp
        fd = frames // 128
        ct = cols // 128
        sem = pltpu.SemaphoreType.DMA
        sizes = (nx, ny, nz, fr, width, pr)
        vmem = pltpu.VMEM
        grad, loss = pl.pallas_call(
            functools.partial(kernel, sizes),
            out_shape=(
                jax.ShapeDtypeStruct((pr, width), F32),
                jax.ShapeDtypeStruct((1, 1), F32),
            ),
            in_specs=[pl.BlockSpec(memory_space=pltpu.VMEM)] * 4,
            out_specs=(
                pl.BlockSpec(memory_space=pltpu.VMEM),
                pl.BlockSpec(memory_space=pltpu.SMEM),
            ),
            scratch_shapes=[
                vmem((nz, ny, 2, fr, width), BF16),
                vmem((frames, width), BF16),
                vmem((ndp, pr, width), BF16),
                vmem((frames, frames), BF16),
                vmem((2, width, frames), BF16),
                vmem((2, frames, cols), F32),
                vmem((frames, cols), F32),
                vmem((2, frames, 128), F32),
                vmem((2, frames, 128), F32),
                vmem((2, frames, 128), F32),
                vmem((2, frames, 128), F32),
                vmem((2, 8, cols), F32),
                vmem((2, ct, 128), F32),
                vmem((4, fd, 128), F32),
                vmem((2, fd, 128), F32),
                vmem((2, fd, 128), F32),
                vmem((2, frames, pr), BF16),
                vmem((nx, width, pr), F32),
                vmem((2, 2, ct, 128), F32),
                vmem((2, 2, ndp - 1, ct, 128), F32),
                vmem((2, 2, fd, 128), F32),
                vmem((2, 2, ny - 1, fd, 128), F32),
                vmem((2, 2, fd, 128), F32),
                vmem((2, 2, nz - 1, fd, 128), F32),
                vmem((2 * fd, 128), F32),
                vmem((ny - 1, 2 * fd, 128), F32),
                vmem((2 * fd, 128), F32),
                vmem((nz - 1, 2 * fd, 128), F32),
                vmem((3, fd, 128), F32),
                vmem((ny - 1, fd, 128), F32),
                vmem((nz - 1, fd, 128), F32),
                vmem((ndp - 1, fd, 128), F32),
                vmem((nx, width, pr), BF16),
                vmem((nx, width, pr), BF16),
                vmem((nx - 1, width, pr), BF16),
                vmem((2, width, pr), BF16),
                vmem((2, width // 2, pr), BF16),
                sem, sem((ny - 1,)),
                sem((2,)), sem((2, nz // 2, ny)),
                sem, sem,
                sem, sem((nz,)),
                sem, sem((2, 2)), sem((2,)),
                sem, sem,
                sem((2, 2)), sem((2, 2)),
                sem((2, 2)), sem((2, 2)),
                sem((2, 2)), sem((2, 2)),
                sem((2,)), sem((2,)),
                sem((3,)), sem((3,)),
                sem, sem((nx,)),
                sem, sem,
                sem, sem((2,)),
            ],
            compiler_params=pltpu.CompilerParams(
                collective_id=0, has_side_effects=True, vmem_limit_bytes=56 * 2**20
            ),
        )(first, second, protos, pairing.reshape(fd, 128))
        return grad, loss[0, 0]

    return jax.shard_map(
        local,
        mesh=mesh,
        in_specs=(
            P(("dp", "proto"), None),
            P(("dp", "proto"), None),
            P(("dp", "proto"), None),
            P("dp"),
        ),
        out_specs=(P(("dp", "proto"), None), P()),
        check_vma=False,
    )
```

```python
import functools
import math

import jax
import jax.numpy as jnp
from jax import lax
from jax.experimental import pallas as pl
from jax.experimental.pallas import tpu as pltpu
from jax.sharding import PartitionSpec as P

ITERS = 3
SOFT_TEMP = 0.1
LOG2_E = math.log2(math.e)
NORM_EPS = 1e-06
CORES = 2
DEPTH = 8

F32 = jnp.float32
BF16 = jnp.bfloat16
NT = (((1,), (1,)), ((), ()))
NN = (((1,), (0,)), ((), ()))


def unit_rows(matrix):
    widened = matrix.astype(F32)
    return (
        widened * lax.rsqrt(jnp.sum(widened * widened, axis=-1, keepdims=True) + NORM_EPS)
    ).astype(BF16)


def drain(ref, sem):
    pltpu.make_async_copy(ref, ref, sem).wait()


def rows_to_lanes(acc_ref, view, out_ref, rows):
    for b in range(rows // 128):
        block = acc_ref[view, b * 128 : (b + 1) * 128, :]
        out_ref[b : b + 1, :] = jnp.sum(block.T, axis=0, keepdims=True)


def lanes_to_rows(dense, out_ref, view, rows):
    for b in range(rows // 128):
        block = jnp.broadcast_to(dense[b : b + 1, :], (128, 128))
        out_ref[view, b * 128 : (b + 1) * 128, :] = block.T


def kernel(
    sizes,
    first_ref,
    second_ref,
    protos_ref,
    pair_ref,
    grad_ref,
    loss_ref,
    first_in,
    second_in,
    protos_in,
    pair_in,
    grad_out,
    v_ref,
    partner_ref,
    p_ref,
    onehot_ref,
    ut_ref,
    k_ref,
    ka_ref,
    acc_ref,
    soft_acc_ref,
    rb_ref,
    sb_ref,
    cs_ref,
    c_ref,
    r_ref,
    row_ref,
    t_ref,
    w_ref,
    g_ref,
    dp_src,
    dp_buf,
    y_src,
    y_buf,
    soft_src,
    soft_ybuf,
    soft_mid,
    soft_zbuf,
    loss_src,
    loss_ybuf,
    loss_zbuf,
    loss_xbuf,
    ss_ref,
    sr_ref,
    xs_ref,
    xr_ref,
    xo_ref,
    in_s,
    out_s,
    ay_s,
    ay_r,
    zr_s,
    zr_r,
    zo_s,
    zo_r,
    fy_s,
    fy_r,
    px_s,
    px_r,
    po_r,
    ps_s,
    ps_r,
    dp_s,
    dp_r,
    y_s,
    y_r,
    soft_s,
    soft_r,
    loss_s,
    loss_r,
    ss_s,
    ss_r,
    xs_s,
    xs_r,
    xo_s,
    xo_r,
):
    nx, ny, nz, fr, width, pr = sizes
    frames = fr * ny * nz
    group = fr * ny
    protos = pr * nx * CORES
    ptiles = protos // 128
    tiles_pr = pr // 128
    fdense = frames // 128
    grad_scale = protos * ny * nz / (SOFT_TEMP * math.sqrt(2.0 * frames * nx * CORES))

    dp, pi = lax.axis_index("dp"), lax.axis_index("proto")
    x, core = dp // CORES, dp % CORES
    y, z = pi // nz, pi % nz

    def at(dx=0, dc=0, dy=0, dz=0):
        return {
            "dp": lax.rem(x + dx, nx) * CORES + lax.rem(core + dc, CORES),
            "proto": lax.rem(y + dy, ny) * nz + lax.rem(z + dz, nz),
        }

    def send(src, dst, ssem, rsem, device):
        pltpu.make_async_remote_copy(
            src_ref=src,
            dst_ref=dst,
            send_sem=ssem,
            recv_sem=rsem,
            device_id=device,
            device_id_type=pl.DeviceIdType.MESH,
        ).start()

    sib = at(dc=1)
    xs = [at(dx=d) for d in range(1, nx)]
    ys = [at(dy=d) for d in range(1, ny)]
    zs = [at(dz=d) for d in range(1, nz)]
    around = lambda d, n: min(d, n - d)
    offsets = [(d, e) for d in range(ny) for e in range(nz) if d or e]
    offsets.sort(key=lambda o: -around(o[0], ny) - around(o[1], nz))
    yzs = [at(dy=d, dz=e) for d, e in offsets]
    dps = [at(dx=d, dc=e) for d in range(nx) for e in range(CORES) if d or e]

    last = nz // 2
    near = max(1, last - 2)
    split = near > 1

    def chunk(dz, q=0):
        return v_ref.at[lax.rem(z + nz + dz, nz), lax.rem(y + ny - q, ny)]

    def ring_send(step, q):
        for way, sign in enumerate((-1, 1)):
            part = chunk(sign * (step - 1), q)
            if q and split and step == near:
                part = part.at[0]
            send(part, part, zr_s.at[min(q, 1)], zr_r.at[way, step - 1, q], zs[0 if way == 0 else nz - 2])

    def ring_skip():
        for way in range(2):
            to = zs[1 if way == 0 else nz - 3]
            send(chunk(0), chunk(0), zr_s.at[0], zr_r.at[way, 1, 0], to)

    def ring_wait(step, q):
        for way, sign in enumerate((-1, 1)):
            part = chunk(sign * step, q)
            drain(part.at[0] if q and split and step == near else part, zr_r.at[way, step - 1, q])

    def far_part(dz):
        return chunk(dz).at[1] if abs(dz) == near else chunk(dz)

    def far_send(dz, index):
        for device in ys:
            send(far_part(dz), far_part(dz), fy_s, fy_r.at[index], device)

    def far_wait(dz, index):
        block = v_ref.at[lax.rem(z + nz + dz, nz), pl.ds(0, ny - 1)]
        drain(block.at[:, 1] if abs(dz) == near else block, fy_r.at[index])

    def far_index(dz):
        if dz == last:
            return 0
        return 2 * (abs(dz) - near) + (1 if dz < 0 else 2)

    half = pr // 2

    def proto_half(dx, part):
        owner = lax.rem(x + nx + dx, nx) * CORES + core
        return p_ref.at[owner, pl.ds(part * half, half)]

    def proto_near(way, part):
        piece = proto_half(-1 if way == 0 else 1, part)
        drain(piece, px_r.at[way, part])
        if part == way:
            send(piece, piece, px_s, po_r.at[part], xs[0 if way == 0 else nx - 2])
        send(piece, piece, ps_s, ps_r, sib)

    def proto_far(part):
        piece = proto_half(2, part)
        drain(piece, po_r.at[part])
        send(piece, piece, ps_s, ps_r, sib)

    loads = [
        pltpu.make_async_copy(source, target, in_s.at[i])
        for i, (source, target) in enumerate(
            (
                (first_ref, first_in),
                (second_ref, second_in),
                (protos_ref, protos_in),
                (pair_ref, pair_in),
            )
        )
    ]
    for load in loads:
        load.start()

    barrier = pltpu.get_barrier_semaphore()
    for device in dps + yzs:
        pl.semaphore_signal(
            barrier, inc=1, device_id=device, device_id_type=pl.DeviceIdType.MESH
        )
    for load in loads:
        load.wait()
    v_ref[z, y, 0] = unit_rows(first_in[...])
    v_ref[z, y, 1] = unit_rows(second_in[...])
    p_ref[dp] = unit_rows(protos_in[...])
    pl.semaphore_wait(barrier, len(dps) + len(yzs))

    for j, device in enumerate(ys):
        send(chunk(0), chunk(0), ay_s, ay_r.at[j], device)
    if last > 2:
        ring_skip()
    send(chunk(0), chunk(0), zo_s, zo_r, zs[last - 1])
    ring_send(1, 0)
    for part in range(2):
        for way in range(2):
            piece = proto_half(0, part if way == 0 else 1 - part)
            where = px_r.at[way, part if way == 0 else 1 - part]
            send(piece, piece, px_s, where, xs[0 if way == 0 else nx - 2])
    send(p_ref.at[dp], p_ref.at[dp], ps_s, ps_r, sib)

    pair = pair_in[...]
    where = (pair % (nz * fr) // fr) * group + (pair // (nz * fr)) * fr + pair % fr
    where = where.astype(F32)
    for b in range(fdense):
        column = jnp.broadcast_to(where[b : b + 1, :], (128, 128)).T
        for t in range(fdense):
            lane = (lax.broadcasted_iota(jnp.int32, (128, 128), 1) + t * 128).astype(F32)
            block = jnp.where(column == lane, 1.0, 0.0).astype(BF16)
            for q in range(128 // fr):
                natural = b * 128 + q * fr
                row = (natural % (nz * fr) // fr) * group + natural // (nz * fr) * fr
                onehot_ref[row : row + fr, t * 128 : (t + 1) * 128] = block[
                    q * fr : (q + 1) * fr, :
                ]
    cs_ref[...] = jnp.zeros_like(cs_ref)
    soft_acc_ref[...] = jnp.zeros_like(soft_acc_ref)

    def first_pass(view, starts, block):
        count = block.shape[0]
        each = count // len(starts)
        soft = jnp.zeros((count, 128), F32)
        for j in range(nx * CORES):
            scores = lax.dot_general(block, p_ref[j], NT, preferred_element_type=F32)
            e = jnp.exp2(scores * (LOG2_E / SOFT_TEMP))
            k = e * e
            for i, start in enumerate(starts):
                rows = pl.ds(pl.multiple_of(start, each), each)
                k_ref[view, rows, j * pr : (j + 1) * pr] = k[i * each : (i + 1) * each]
            for t in range(tiles_pr):
                soft = soft + e[:, t * 128 : (t + 1) * 128]
            cs_ref[view, :, j * pr : (j + 1) * pr] += jnp.sum(
                k.reshape(count // 8, 8, pr), axis=0
            )
        for i, start in enumerate(starts):
            rows = pl.ds(pl.multiple_of(start, each), each)
            soft_acc_ref[view, rows, :] = soft[i * each : (i + 1) * each]

    def frames_y(q):
        drain(chunk(0, q), ay_r.at[q - 1])
        ring_send(1, q)

    def ring_next(step, q):
        ring_wait(step, q)
        if (1 < step < last - 1) if q == 0 else step < near:
            ring_send(step + 1, q)
        if q == 0 and (step > near or (split and step == near)):
            far_send(-step, far_index(-step))
            far_send(step, far_index(step))

    def opposite():
        drain(chunk(last), zo_r)
        far_send(last, far_index(last))

    events = [(6.5, opposite)]
    for q in range(1, ny):
        events.append((4.0 + 0.5 * q, functools.partial(frames_y, q)))
    for step in range(1, last):
        when = 7.0 if step == 1 else 3.9 + 5.0 * (step - 2)
        events.append((when, functools.partial(ring_next, step, 0)))
    for q in range(1, ny):
        for step in range(1, near):
            when = 6.0 + 3.5 * step + 1.3 * q
            events.append((when, functools.partial(ring_next, step, q)))
    for way in range(2):
        events.append((6.0 + 0.1 * way, functools.partial(proto_near, way, way)))
        events.append((8.6 + 0.1 * way, functools.partial(proto_near, way, 1 - way)))
        events.append((12.0 + 0.1 * way, functools.partial(proto_far, way)))
    for when, event in sorted(events, key=lambda pair: pair[0]):
        event()
    drain(p_ref.at[pl.ds(0, nx)], ps_r)

    def pair_wait(p):
        if p == 0:
            if near == 1:
                for q in range(1, ny):
                    ring_wait(1, q)
        elif p == 1:
            far_wait(last, far_index(last))
        else:
            step = last + 1 - p
            if step <= near:
                for q in range(1, ny):
                    ring_wait(step, q)
            far_wait(-step, far_index(-step))
            far_wait(step, far_index(step))

    def pair_pass(n, carry):
        p, view = n // 2, n % 2
        for known in range(last):

            @pl.when(n == 2 * known)
            def _(known=known):
                pair_wait(known)

        step = lax.max(1, (last + 1 - p) * lax.min(p, 1))
        one = lax.rem(z + step, nz)
        two = lax.rem(z + nz - step * lax.min((p - 1) * (p - 1), 1), nz)
        block = jnp.concatenate(
            [v_ref[b, :, view].reshape(group, width) for b in (one, two)], axis=0
        )
        first_pass(view, [one * group, two * group], block)
        return carry

    lax.fori_loop(0, 2 * last, pair_pass, 0)

    def dp_start(view, it, source):
        slot = it % 2

        @pl.when(it >= 2)
        def _():
            drain(dp_buf.at[view, slot], dp_s.at[view, slot])

        dp_src[view, slot] = source
        for j, device in enumerate(dps):
            send(
                dp_src.at[view, slot],
                dp_buf.at[view, slot, j],
                dp_s.at[view, slot],
                dp_r.at[view, slot],
                device,
            )

    def dp_wait(view, it):
        slot = it % 2
        drain(dp_buf.at[view, slot], dp_r.at[view, slot])
        total = dp_src[view, slot]
        for j in range(len(dps)):
            total = total + dp_buf[view, slot, j]
        return total

    def yz_start(view, it):
        slot = it % 2

        @pl.when(it >= 2)
        def _():
            drain(y_buf.at[view, slot], y_s.at[view, slot])

        y_src[view, slot] = row_ref[view]
        for j, device in enumerate(yzs):
            send(
                y_src.at[view, slot],
                y_buf.at[view, slot, j],
                y_s.at[view, slot],
                y_r.at[view, slot],
                device,
            )

    def yz_wait(view, it):
        slot = it % 2
        drain(y_buf.at[view, slot], y_r.at[view, slot])
        total = y_src[view, slot]
        for j in range(len(yzs)):
            total = total + y_buf[view, slot, j]
        return total

    def column_totals(view):
        parts = [
            jnp.sum(cs_ref[view, :, t * 128 : (t + 1) * 128], axis=0, keepdims=True)
            for t in range(ptiles)
        ]
        return jnp.concatenate(parts, axis=0)

    def frame_sums(view):
        def step(b, carry):
            rows = pl.ds(pl.multiple_of(b * 128, 128), 128)
            total = jnp.zeros((128, 128), F32)
            for t in range(ptiles):
                k = k_ref[view, rows, t * 128 : (t + 1) * 128]
                total = total + k * c_ref[view, t : t + 1, :]
            row_ref[view, pl.ds(b, 1), :] = jnp.sum(total.T, axis=0, keepdims=True)
            return carry

        lax.fori_loop(0, fdense, step, 0, unroll=min(4, fdense))

    def proto_sums(view):
        def step(i, totals):
            rows = pl.ds(pl.multiple_of(i * 64, 64), 64)
            scale = rb_ref[view, rows, :]
            out = []
            for t in range(ptiles):
                k = k_ref[view, rows, t * 128 : (t + 1) * 128]
                out.append(totals[t] + jnp.sum((k * scale).reshape(8, 8, 128), axis=0))
            return tuple(out)

        totals = lax.fori_loop(
            0,
            frames // 64,
            step,
            tuple(jnp.zeros((8, 128), F32) for _ in range(ptiles)),
            unroll=2,
        )
        for t in range(ptiles):
            cs_ref[view, :, t * 128 : (t + 1) * 128] = totals[t]

    zero = jnp.int32(0)
    dp_start(1, zero, column_totals(1))
    dp_start(0, zero, column_totals(0))

    for view in range(2):
        rows_to_lanes(soft_acc_ref, view, soft_src.at[pl.ds(view * fdense, fdense)], frames)
    for j, device in enumerate(ys):
        send(soft_src, soft_ybuf.at[j], soft_s.at[0], soft_r.at[0], device)

    eye = jnp.where(
        lax.broadcasted_iota(jnp.int32, (width, width), 0)
        == lax.broadcasted_iota(jnp.int32, (width, width), 1),
        1.0,
        0.0,
    ).astype(BF16)

    rows_each = min(256, frames)
    pieces = frames // rows_each

    def transpose_view(view):
        for i in range(pieces):
            if view:
                block = partner_ref[i * rows_each : (i + 1) * rows_each, :]
            else:
                count = rows_each // group
                block = v_ref[i * count : (i + 1) * count, :, 0].reshape(rows_each, width)
            ut_ref[view, :, i * rows_each : (i + 1) * rows_each] = lax.dot_general(
                eye, block, NT, preferred_element_type=F32
            ).astype(BF16)

    def align_rows():
        second = v_ref[:, :, 1].reshape(frames, width)
        for i in range(pieces):
            rows = slice(i * rows_each, (i + 1) * rows_each)
            partner_ref[rows, :] = lax.dot_general(
                onehot_ref[rows, :], second, NN, preferred_element_type=F32
            ).astype(BF16)

    def align_kernel(first, count):
        def step(i, carry):
            rows = pl.ds(pl.multiple_of(i * rows_each, rows_each), rows_each)
            block = partner_ref[rows, :]
            for j in range(nx * CORES):
                scores = lax.dot_general(block, p_ref[j], NT, preferred_element_type=F32)
                ka_ref[rows, j * pr : (j + 1) * pr] = jnp.exp2(
                    scores * (2.0 * LOG2_E / SOFT_TEMP)
                )
            return carry

        lax.fori_loop(first, first + count, step, 0)

    def align_dense(dense):
        row = jnp.concatenate([dense[b : b + 1, :] for b in range(fdense)], axis=1)
        high = row.astype(BF16).astype(F32)
        middle = (row - high).astype(BF16).astype(F32)
        low = row - high - middle
        parts = jnp.concatenate([high, middle, low, jnp.zeros((13, frames), F32)], axis=0)
        out = lax.dot_general(
            parts.astype(BF16), onehot_ref[...], NT, preferred_element_type=F32
        )
        total = out[0:1] + out[1:2] + out[2:3]
        return jnp.concatenate(
            [total[:, b * 128 : (b + 1) * 128] for b in range(fdense)], axis=0
        )

    transpose_view(0)
    align_rows()

    def soft_rows():
        total = soft_src[...]
        drain(soft_ybuf, soft_r.at[0])
        for j in range(len(ys)):
            total = total + soft_ybuf[j]
        soft_mid[...] = total

    def soft_totals():
        drain(soft_zbuf, soft_r.at[1])
        total = soft_mid[...]
        for j in range(len(zs)):
            total = total + soft_zbuf[j]
        transpose_view(1)
        for view in range(2):
            dense = total[view * fdense : (view + 1) * fdense]
            if view:
                dense = align_dense(dense)
            lanes_to_rows(grad_scale / dense, sb_ref, view, frames)
            r_ref[2 + view] = jnp.log(dense)

    def cross_sums():
        def step(i, carry):
            rows = pl.ds(pl.multiple_of(i * 32, 32), 32)
            sums = [jnp.zeros((32, 128), F32) for _ in range(3)]
            for t in range(ptiles):
                k = [ref[rows, t * 128 : (t + 1) * 128] for ref in (k_ref.at[0], ka_ref)]
                terms = [k[v] * c_ref[v, t : t + 1, :] for v in range(2)]
                sums[0] = sums[0] + terms[0] * jnp.log(k[1])
                sums[1] = sums[1] + terms[1] * jnp.log(k[0])
                sums[2] = sums[2] + terms[1]
            acc_ref[0, rows, :] = 0.5 * sums[0]
            acc_ref[1, rows, :] = 0.5 * sums[1]
            soft_acc_ref[1, rows, :] = sums[2]
            return carry

        lax.fori_loop(0, frames // 32, step, 0)
        for v in range(2):
            rows_to_lanes(acc_ref, v, t_ref.at[v], frames)
        rows_to_lanes(soft_acc_ref, 1, row_ref.at[1], frames)

    def sweep(it, carry):
        for view in (1, 0):
            c_ref[view] = 1.0 / dp_wait(view, it)
            frame_sums(view)
            yz_start(view, it)

        @pl.when(it == 0)
        def _():
            align_kernel(0, pieces)
            soft_rows()
            for j, device in enumerate(zs):
                send(soft_mid, soft_zbuf.at[j], soft_s.at[1], soft_r.at[1], device)

        @pl.when(it == 1)
        def _():
            soft_totals()

        @pl.when(it == ITERS - 1)
        def _():
            cross_sums()

        for view in (1, 0):
            r_ref[view] = 1.0 / yz_wait(view, it)

            @pl.when(it < ITERS - 1)
            def _(view=view):
                lanes_to_rows(r_ref[view], rb_ref, view, frames)
                proto_sums(view)
                dp_start(view, it + 1, column_totals(view))

            @pl.when(it == ITERS - 1)
            def _(view=view):
                if view:
                    r_ref[view] = align_dense(r_ref[view])
                lanes_to_rows(r_ref[view] * grad_scale, rb_ref, view, frames)

        return carry

    lax.fori_loop(0, ITERS, sweep, 0)

    loss = jnp.zeros((fdense, 128), F32)
    for v in range(2):
        loss = loss + r_ref[v] * (r_ref[3 - v] * row_ref[v] - t_ref[v])
    loss_src[0] = loss
    for j, device in enumerate(ys):
        send(loss_src.at[0], loss_ybuf.at[j], loss_s.at[0], loss_r.at[0], device)

    def loss_step(stage, buf, nextbuf, partners):
        drain(buf, loss_r.at[stage])
        total = loss_src[stage]
        for j in range(buf.shape[0]):
            total = total + buf[j]
        if nextbuf is None:
            return total
        loss_src[stage + 1] = total
        for j, device in enumerate(partners):
            send(
                loss_src.at[stage + 1],
                nextbuf.at[j],
                loss_s.at[stage + 1],
                loss_r.at[stage + 1],
                device,
            )
        return total

    def block_grad(owner):
        count = min(64, frames)
        for start in range(0, frames, count):
            rows = slice(start, start + count)
            for t in range(tiles_pr):
                tile = owner * tiles_pr + t
                cols = pl.ds(pl.multiple_of(tile * 128, 128), 128)
                k = [ref[rows, cols] for ref in (k_ref.at[0], ka_ref)]
                assigned = [
                    k[v] * (rb_ref[v, rows, :] * c_ref[v, pl.ds(tile, 1), :])
                    for v in range(2)
                ]
                for v in range(2):
                    w_ref[v, rows, t * 128 : (t + 1) * 128] = (
                        (k[v] * lax.rsqrt(k[v])) * sb_ref[v, rows, :] - assigned[1 - v]
                    ).astype(BF16)
        total = lax.dot_general(ut_ref[0], w_ref[0], NN, preferred_element_type=F32)
        total = total + lax.dot_general(ut_ref[1], w_ref[1], NN, preferred_element_type=F32)
        return total

    middle = width // 2
    lower, upper = pl.ds(0, middle), pl.ds(middle, middle)
    right, left = xs[0], xs[nx - 2]
    def scatter(n, carry):
        k, own = n // 2, n % 2
        d = (2 + 3 * k + (k // 2) * (3 - 2 * (k % 2))) % 4
        g_ref[k] = block_grad(lax.rem(x + d, nx) * CORES + lax.rem(core + 1 + own, CORES))

        @pl.when(own == 0)
        def _():
            ss_ref[k] = g_ref[k].astype(BF16)
            send(ss_ref.at[k], sr_ref.at[k], ss_s, ss_r.at[k], sib)

        @pl.when(own == 1)
        def _():
            drain(sr_ref.at[k], ss_r.at[k])

        @pl.when(n == 1)
        def _():
            xs_ref[0] = (g_ref[0] + sr_ref[0].astype(F32)).astype(BF16)
            send(xs_ref.at[0, lower], xo_ref.at[0], xo_s, xo_r.at[0], right)
            send(xs_ref.at[0, upper], xo_ref.at[1], xo_s, xo_r.at[1], left)

        @pl.when(n == 3)
        def _():
            xs_ref[1, upper] = (g_ref[1, upper] + sr_ref[1, upper].astype(F32)).astype(BF16)
            send(xs_ref.at[1, upper], xr_ref.at[0, upper], xs_s, xs_r, right)
            loss_step(0, loss_ybuf, loss_zbuf, zs)

        @pl.when(n == 5)
        def _():
            xs_ref[2, lower] = (g_ref[2, lower] + sr_ref[2, lower].astype(F32)).astype(BF16)
            send(xs_ref.at[2, lower], xr_ref.at[1, lower], xs_s, xs_r, left)
            for way, (rows, to) in enumerate(((lower, right), (upper, left))):
                drain(xo_ref.at[way], xo_r.at[way])
                xs_ref[1 + way, rows] = (
                    g_ref[1 + way, rows]
                    + sr_ref[1 + way, rows].astype(F32)
                    + xo_ref[way].astype(F32)
                ).astype(BF16)
                send(xs_ref.at[1 + way, rows], xr_ref.at[way, rows], xs_s, xs_r, to)

        return carry

    lax.fori_loop(0, 2 * nx, scatter, 0)
    loss_step(1, loss_zbuf, loss_xbuf, dps)
    drain(xr_ref, xs_r)
    stores = []
    for i in range(width // 128):
        rows = slice(i * 128, (i + 1) * 128)
        for t in range(tiles_pr):
            cols = slice(t * 128, (t + 1) * 128)
            total = g_ref[3, rows, cols] + sr_ref[3, rows, cols].astype(F32)
            for j in range(2):
                total = total + xr_ref[j, rows, cols].astype(F32)
            grad_out[cols, rows] = total.T
        stores.append(
            pltpu.make_async_copy(grad_out.at[:, rows], grad_ref.at[:, rows], out_s.at[i])
        )
        stores[i].start()
    total = loss_step(2, loss_xbuf, None, None)
    loss_ref[0, 0] = jnp.sum(total) / (2.0 * frames * nx * CORES)

    for store in stores:
        store.wait()
    drain(v_ref.at[0, pl.ds(0, ny - 1)], ay_s)
    drain(v_ref.at[pl.ds(0, 2 * (last - 1)), 0], zr_s.at[0])
    drain(v_ref.at[pl.ds(0, 2 * near - split), pl.ds(0, ny - 1)], zr_s.at[1])
    drain(chunk(0), zo_s)
    drain(v_ref.at[pl.ds(0, 2 * (last - 1 - near) + 1 + split), pl.ds(0, ny - 1)], fy_s)
    drain(p_ref.at[pl.ds(0, 3)], px_s)
    drain(p_ref.at[pl.ds(0, nx)], ps_s)
    for view in range(2):
        for slot in range(min(2, ITERS)):
            drain(dp_buf.at[view, slot], dp_s.at[view, slot])
            drain(y_buf.at[view, slot], y_s.at[view, slot])
    drain(soft_ybuf, soft_s.at[0])
    drain(soft_zbuf, soft_s.at[1])
    drain(loss_ybuf, loss_s.at[0])
    drain(loss_zbuf, loss_s.at[1])
    drain(loss_xbuf, loss_s.at[2])
    drain(sr_ref, ss_s)
    drain(xo_ref, xo_s)
    drain(xr_ref, xs_s)


def solution(mesh):
    ndp, nproto = mesh.shape["dp"], mesh.shape["proto"]
    nx, nz = ndp // CORES, DEPTH
    ny = nproto // nz

    def local(first, second, protos, pairing):
        fr, width = first.shape
        pr = protos.shape[0]
        frames = fr * nproto
        cols = pr * ndp
        fd = frames // 128
        ct = cols // 128
        sem = pltpu.SemaphoreType.DMA
        sizes = (nx, ny, nz, fr, width, pr)
        vmem = pltpu.VMEM
        grad, loss = pl.pallas_call(
            functools.partial(kernel, sizes),
            out_shape=(
                jax.ShapeDtypeStruct((pr, width), F32),
                jax.ShapeDtypeStruct((1, 1), F32),
            ),
            in_specs=[pl.BlockSpec(memory_space=pl.ANY)] * 4,
            out_specs=(
                pl.BlockSpec(memory_space=pl.ANY),
                pl.BlockSpec(memory_space=pltpu.SMEM),
            ),
            scratch_shapes=[
                vmem((fr, width), BF16),
                vmem((fr, width), BF16),
                vmem((pr, width), F32),
                vmem((fd, 128), jnp.int32),
                vmem((pr, width), F32),
                vmem((nz, ny, 2, fr, width), BF16),
                vmem((frames, width), BF16),
                vmem((ndp, pr, width), BF16),
                vmem((frames, frames), BF16),
                vmem((2, width, frames), BF16),
                vmem((2, frames, cols), F32),
                vmem((frames, cols), F32),
                vmem((2, frames, 128), F32),
                vmem((2, frames, 128), F32),
                vmem((2, frames, 128), F32),
                vmem((2, frames, 128), F32),
                vmem((2, 8, cols), F32),
                vmem((2, ct, 128), F32),
                vmem((4, fd, 128), F32),
                vmem((2, fd, 128), F32),
                vmem((2, fd, 128), F32),
                vmem((2, frames, pr), BF16),
                vmem((nx, width, pr), F32),
                vmem((2, 2, ct, 128), F32),
                vmem((2, 2, ndp - 1, ct, 128), F32),
                vmem((2, 2, fd, 128), F32),
                vmem((2, 2, nproto - 1, fd, 128), F32),
                vmem((2 * fd, 128), F32),
                vmem((ny - 1, 2 * fd, 128), F32),
                vmem((2 * fd, 128), F32),
                vmem((nz - 1, 2 * fd, 128), F32),
                vmem((3, fd, 128), F32),
                vmem((ny - 1, fd, 128), F32),
                vmem((nz - 1, fd, 128), F32),
                vmem((ndp - 1, fd, 128), F32),
                vmem((nx, width, pr), BF16),
                vmem((nx, width, pr), BF16),
                vmem((nx - 1, width, pr), BF16),
                vmem((2, width, pr), BF16),
                vmem((2, width // 2, pr), BF16),
                sem((4,)), sem((width // 128,)),
                sem, sem((ny - 1,)),
                sem((2,)), sem((2, nz // 2, ny)),
                sem, sem,
                sem, sem((nz,)),
                sem, sem((2, 2)), sem((2,)),
                sem, sem,
                sem((2, 2)), sem((2, 2)),
                sem((2, 2)), sem((2, 2)),
                sem((2,)), sem((2,)),
                sem((3,)), sem((3,)),
                sem, sem((nx,)),
                sem, sem,
                sem, sem((2,)),
            ],
            compiler_params=pltpu.CompilerParams(
                collective_id=0, has_side_effects=True, vmem_limit_bytes=56 * 2**20
            ),
        )(first, second, protos, pairing.reshape(fd, 128))
        return grad, loss[0, 0]

    return jax.shard_map(
        local,
        mesh=mesh,
        in_specs=(
            P(("dp", "proto"), None),
            P(("dp", "proto"), None),
            P(("dp", "proto"), None),
            P("dp"),
        ),
        out_specs=(P(("dp", "proto"), None), P()),
        check_vma=False,
    )
```

```python
import functools
import math

import jax
import jax.numpy as jnp
from jax import lax
from jax.experimental import pallas as pl
from jax.experimental.pallas import tpu as pltpu
from jax.sharding import PartitionSpec as P

ITERS = 3
SOFT_TEMP = 0.1
LOG2_E = math.log2(math.e)
NORM_EPS = 1e-06
CORES = 2
DEPTH = 8

F32 = jnp.float32
BF16 = jnp.bfloat16
NT = (((1,), (1,)), ((), ()))
NN = (((1,), (0,)), ((), ()))


def unit_rows(matrix):
    widened = matrix.astype(F32)
    return (
        widened * lax.rsqrt(jnp.sum(widened * widened, axis=-1, keepdims=True) + NORM_EPS)
    ).astype(BF16)


def drain(ref, sem):
    pltpu.make_async_copy(ref, ref, sem).wait()


def rows_to_lanes(acc_ref, view, out_ref, rows):
    for b in range(rows // 128):
        block = acc_ref[view, b * 128 : (b + 1) * 128, :]
        out_ref[b : b + 1, :] = jnp.sum(block.T, axis=0, keepdims=True)


def lanes_to_rows(dense, out_ref, view, rows):
    for b in range(rows // 128):
        block = jnp.broadcast_to(dense[b : b + 1, :], (128, 128))
        out_ref[view, b * 128 : (b + 1) * 128, :] = block.T


def kernel(
    sizes,
    first_ref,
    second_ref,
    protos_ref,
    pair_ref,
    grad_ref,
    loss_ref,
    first_in,
    second_in,
    protos_in,
    pair_in,
    grad_out,
    v_ref,
    partner_ref,
    p_ref,
    onehot_ref,
    ut_ref,
    k_ref,
    ka_ref,
    acc_ref,
    soft_acc_ref,
    rb_ref,
    sb_ref,
    cs_ref,
    c_ref,
    r_ref,
    row_ref,
    t_ref,
    w_ref,
    g_ref,
    dp_src,
    dp_buf,
    y_src,
    y_buf,
    soft_src,
    soft_ybuf,
    soft_mid,
    soft_zbuf,
    loss_src,
    loss_ybuf,
    loss_zbuf,
    loss_xbuf,
    ss_ref,
    sr_ref,
    xs_ref,
    xr_ref,
    xo_ref,
    in_s,
    out_s,
    ay_s,
    ay_r,
    zr_s,
    zr_r,
    zo_s,
    zo_r,
    fy_s,
    fy_r,
    px_s,
    px_r,
    po_r,
    ps_s,
    ps_r,
    dp_s,
    dp_r,
    y_s,
    y_r,
    soft_s,
    soft_r,
    loss_s,
    loss_r,
    ss_s,
    ss_r,
    xs_s,
    xs_r,
    xo_s,
    xo_r,
):
    nx, ny, nz, fr, width, pr = sizes
    frames = fr * ny * nz
    group = fr * ny
    protos = pr * nx * CORES
    ptiles = protos // 128
    tiles_pr = pr // 128
    fdense = frames // 128
    grad_scale = protos * ny * nz / (SOFT_TEMP * math.sqrt(2.0 * frames * nx * CORES))

    dp, pi = lax.axis_index("dp"), lax.axis_index("proto")
    x, core = dp // CORES, dp % CORES
    y, z = pi // nz, pi % nz

    def at(dx=0, dc=0, dy=0, dz=0):
        return {
            "dp": lax.rem(x + dx, nx) * CORES + lax.rem(core + dc, CORES),
            "proto": lax.rem(y + dy, ny) * nz + lax.rem(z + dz, nz),
        }

    def send(src, dst, ssem, rsem, device):
        pltpu.make_async_remote_copy(
            src_ref=src,
            dst_ref=dst,
            send_sem=ssem,
            recv_sem=rsem,
            device_id=device,
            device_id_type=pl.DeviceIdType.MESH,
        ).start()

    sib = at(dc=1)
    xs = [at(dx=d) for d in range(1, nx)]
    ys = [at(dy=d) for d in range(1, ny)]
    zs = [at(dz=d) for d in range(1, nz)]
    around = lambda d, n: min(d, n - d)
    offsets = [(d, e) for d in range(ny) for e in range(nz) if d or e]
    offsets.sort(key=lambda o: -around(o[0], ny) - around(o[1], nz))
    yzs = [at(dy=d, dz=e) for d, e in offsets]
    dps = [at(dx=d, dc=e) for d in range(nx) for e in range(CORES) if d or e]

    last = nz // 2
    near = max(1, last - 2)
    split = near > 1

    def chunk(dz, q=0):
        return v_ref.at[lax.rem(z + nz + dz, nz), lax.rem(y + ny - q, ny)]

    def ring_send(step, q):
        for way, sign in enumerate((-1, 1)):
            part = chunk(sign * (step - 1), q)
            if q and split and step == near:
                part = part.at[0]
            send(part, part, zr_s.at[min(q, 1)], zr_r.at[way, step - 1, q], zs[0 if way == 0 else nz - 2])

    def ring_skip():
        for way in range(2):
            to = zs[1 if way == 0 else nz - 3]
            send(chunk(0), chunk(0), zr_s.at[0], zr_r.at[way, 1, 0], to)

    def ring_wait(step, q):
        for way, sign in enumerate((-1, 1)):
            part = chunk(sign * step, q)
            drain(part.at[0] if q and split and step == near else part, zr_r.at[way, step - 1, q])

    def far_part(dz):
        return chunk(dz).at[1] if abs(dz) == near else chunk(dz)

    def far_send(dz, index):
        for device in ys:
            send(far_part(dz), far_part(dz), fy_s, fy_r.at[index], device)

    def far_wait(dz, index):
        block = v_ref.at[lax.rem(z + nz + dz, nz), pl.ds(0, ny - 1)]
        drain(block.at[:, 1] if abs(dz) == near else block, fy_r.at[index])

    def far_index(dz):
        if dz == last:
            return 0
        return 2 * (abs(dz) - near) + (1 if dz < 0 else 2)

    half = pr // 2

    def proto_half(dx, part):
        owner = lax.rem(x + nx + dx, nx) * CORES + core
        return p_ref.at[owner, pl.ds(part * half, half)]

    def proto_near(way, part):
        piece = proto_half(-1 if way == 0 else 1, part)
        drain(piece, px_r.at[way, part])
        if part == way:
            send(piece, piece, px_s, po_r.at[part], xs[0 if way == 0 else nx - 2])
        send(piece, piece, ps_s, ps_r, sib)

    def proto_far(part):
        piece = proto_half(2, part)
        drain(piece, po_r.at[part])
        send(piece, piece, ps_s, ps_r, sib)

    loads = [
        pltpu.make_async_copy(source, target, in_s.at[i])
        for i, (source, target) in enumerate(
            (
                (first_ref, first_in),
                (second_ref, second_in),
                (protos_ref, protos_in),
                (pair_ref, pair_in),
            )
        )
    ]
    for load in loads:
        load.start()

    greeted = [sib, xs[0], xs[nx - 2], *ys]
    greeted += [zs[d - 1] for d in sorted({1, 2, last, nz - 2, nz - 1})]
    barrier = pltpu.get_barrier_semaphore()
    for device in greeted:
        pl.semaphore_signal(
            barrier, inc=1, device_id=device, device_id_type=pl.DeviceIdType.MESH
        )
    for load in loads:
        load.wait()
    v_ref[z, y, 0] = unit_rows(first_in[...])
    v_ref[z, y, 1] = unit_rows(second_in[...])
    p_ref[dp] = unit_rows(protos_in[...])
    pl.semaphore_wait(barrier, len(greeted))

    for j, device in enumerate(ys):
        send(chunk(0), chunk(0), ay_s, ay_r.at[j], device)
    if last > 2:
        ring_skip()
    send(chunk(0), chunk(0), zo_s, zo_r, zs[last - 1])
    ring_send(1, 0)
    for part in range(2):
        for way in range(2):
            piece = proto_half(0, part if way == 0 else 1 - part)
            where = px_r.at[way, part if way == 0 else 1 - part]
            send(piece, piece, px_s, where, xs[0 if way == 0 else nx - 2])
    send(p_ref.at[dp], p_ref.at[dp], ps_s, ps_r, sib)

    pair = pair_in[...]
    where = (pair % (nz * fr) // fr) * group + (pair // (nz * fr)) * fr + pair % fr
    where = where.astype(F32)
    for b in range(fdense):
        column = jnp.broadcast_to(where[b : b + 1, :], (128, 128)).T
        for t in range(fdense):
            lane = (lax.broadcasted_iota(jnp.int32, (128, 128), 1) + t * 128).astype(F32)
            block = jnp.where(column == lane, 1.0, 0.0).astype(BF16)
            for q in range(128 // fr):
                natural = b * 128 + q * fr
                row = (natural % (nz * fr) // fr) * group + natural // (nz * fr) * fr
                onehot_ref[row : row + fr, t * 128 : (t + 1) * 128] = block[
                    q * fr : (q + 1) * fr, :
                ]
    cs_ref[...] = jnp.zeros_like(cs_ref)
    soft_acc_ref[...] = jnp.zeros_like(soft_acc_ref)

    def first_pass(view, starts, block):
        count = block.shape[0]
        each = count // len(starts)
        soft = jnp.zeros((count, 128), F32)
        for j in range(nx * CORES):
            scores = lax.dot_general(block, p_ref[j], NT, preferred_element_type=F32)
            e = jnp.exp2(scores * (LOG2_E / SOFT_TEMP))
            k = e * e
            for i, start in enumerate(starts):
                rows = pl.ds(pl.multiple_of(start, each), each)
                k_ref[view, rows, j * pr : (j + 1) * pr] = k[i * each : (i + 1) * each]
            for t in range(tiles_pr):
                soft = soft + e[:, t * 128 : (t + 1) * 128]
            cs_ref[view, :, j * pr : (j + 1) * pr] += jnp.sum(
                k.reshape(count // 8, 8, pr), axis=0
            )
        for i, start in enumerate(starts):
            rows = pl.ds(pl.multiple_of(start, each), each)
            soft_acc_ref[view, rows, :] = soft[i * each : (i + 1) * each]

    def frames_y(q):
        drain(chunk(0, q), ay_r.at[q - 1])
        ring_send(1, q)

    def ring_next(step, q):
        ring_wait(step, q)
        if (1 < step < last - 1) if q == 0 else step < near:
            ring_send(step + 1, q)
        if q == 0 and (step > near or (split and step == near)):
            far_send(-step, far_index(-step))
            far_send(step, far_index(step))

    def opposite():
        drain(chunk(last), zo_r)
        far_send(last, far_index(last))

    events = [(6.5, opposite)]
    for q in range(1, ny):
        events.append((4.0 + 0.5 * q, functools.partial(frames_y, q)))
    for step in range(1, last):
        when = 7.0 if step == 1 else 3.9 + 5.0 * (step - 2)
        events.append((when, functools.partial(ring_next, step, 0)))
    for q in range(1, ny):
        for step in range(1, near):
            when = 6.0 + 3.5 * step + 1.3 * q
            events.append((when, functools.partial(ring_next, step, q)))
    for way in range(2):
        events.append((6.0 + 0.1 * way, functools.partial(proto_near, way, way)))
        events.append((8.6 + 0.1 * way, functools.partial(proto_near, way, 1 - way)))
        events.append((12.0 + 0.1 * way, functools.partial(proto_far, way)))
    for when, event in sorted(events, key=lambda pair: pair[0]):
        event()
    drain(p_ref.at[pl.ds(0, nx)], ps_r)

    def dp_start(view, it, source):
        slot = it % 2

        @pl.when(it >= 2)
        def _():
            drain(dp_buf.at[view, slot], dp_s.at[view, slot])

        dp_src[view, slot] = source
        for j, device in enumerate(dps):
            send(
                dp_src.at[view, slot],
                dp_buf.at[view, slot, j],
                dp_s.at[view, slot],
                dp_r.at[view, slot],
                device,
            )

    def dp_wait(view, it):
        slot = it % 2
        drain(dp_buf.at[view, slot], dp_r.at[view, slot])
        total = dp_src[view, slot]
        for j in range(len(dps)):
            total = total + dp_buf[view, slot, j]
        return total

    def yz_start(view, it):
        slot = it % 2

        @pl.when(it >= 2)
        def _():
            drain(y_buf.at[view, slot], y_s.at[view, slot])

        y_src[view, slot] = row_ref[view]
        for j, device in enumerate(yzs):
            send(
                y_src.at[view, slot],
                y_buf.at[view, slot, j],
                y_s.at[view, slot],
                y_r.at[view, slot],
                device,
            )

    def yz_wait(view, it):
        slot = it % 2
        drain(y_buf.at[view, slot], y_r.at[view, slot])
        total = y_src[view, slot]
        for j in range(len(yzs)):
            total = total + y_buf[view, slot, j]
        return total

    def column_totals(view):
        parts = [
            jnp.sum(cs_ref[view, :, t * 128 : (t + 1) * 128], axis=0, keepdims=True)
            for t in range(ptiles)
        ]
        return jnp.concatenate(parts, axis=0)

    def frame_sums(view):
        def step(b, carry):
            rows = pl.ds(pl.multiple_of(b * 128, 128), 128)
            total = jnp.zeros((128, 128), F32)
            for t in range(ptiles):
                k = k_ref[view, rows, t * 128 : (t + 1) * 128]
                total = total + k * c_ref[view, t : t + 1, :]
            row_ref[view, pl.ds(b, 1), :] = jnp.sum(total.T, axis=0, keepdims=True)
            return carry

        lax.fori_loop(0, fdense, step, 0, unroll=min(4, fdense))

    def proto_sums(view):
        def step(i, totals):
            rows = pl.ds(pl.multiple_of(i * 64, 64), 64)
            scale = rb_ref[view, rows, :]
            out = []
            for t in range(ptiles):
                k = k_ref[view, rows, t * 128 : (t + 1) * 128]
                out.append(totals[t] + jnp.sum((k * scale).reshape(8, 8, 128), axis=0))
            return tuple(out)

        totals = lax.fori_loop(
            0,
            frames // 64,
            step,
            tuple(jnp.zeros((8, 128), F32) for _ in range(ptiles)),
            unroll=2,
        )
        for t in range(ptiles):
            cs_ref[view, :, t * 128 : (t + 1) * 128] = totals[t]

    zero = jnp.int32(0)

    def pair_wait(p):
        if p == 0:
            if near == 1:
                for q in range(1, ny):
                    ring_wait(1, q)
        elif p == 1:
            far_wait(last, far_index(last))
        else:
            step = p
            if step <= near:
                for q in range(1, ny):
                    ring_wait(step, q)
            far_wait(-step, far_index(-step))
            far_wait(step, far_index(step))

    def pair_pass(n, carry):
        p, view = n // 2, 1 - n % 2
        for known in range(last):

            @pl.when(n == 2 * known)
            def _(known=known):
                pair_wait(known)

        opposite_pair = 1 - lax.min((p - 1) * (p - 1), 1)
        step = p + 1 - lax.min(p, 1) + opposite_pair * (last - 1)
        one = lax.rem(z + step, nz)
        two = lax.rem(z + nz - step * (1 - opposite_pair), nz)
        block = jnp.concatenate(
            [v_ref[b, :, view].reshape(group, width) for b in (one, two)], axis=0
        )
        first_pass(view, [one * group, two * group], block)

        @pl.when(n == 2 * last - 2)
        def _():
            dp_start(1, zero, column_totals(1))

        return carry

    lax.fori_loop(0, 2 * last, pair_pass, 0)
    dp_start(0, zero, column_totals(0))

    for view in range(2):
        rows_to_lanes(soft_acc_ref, view, soft_src.at[pl.ds(view * fdense, fdense)], frames)
    for j, device in enumerate(ys):
        send(soft_src, soft_ybuf.at[j], soft_s.at[0], soft_r.at[0], device)

    eye = jnp.where(
        lax.broadcasted_iota(jnp.int32, (width, width), 0)
        == lax.broadcasted_iota(jnp.int32, (width, width), 1),
        1.0,
        0.0,
    ).astype(BF16)

    rows_each = min(256, frames)
    pieces = frames // rows_each

    def transpose_view(view):
        for i in range(pieces):
            if view:
                block = partner_ref[i * rows_each : (i + 1) * rows_each, :]
            else:
                count = rows_each // group
                block = v_ref[i * count : (i + 1) * count, :, 0].reshape(rows_each, width)
            ut_ref[view, :, i * rows_each : (i + 1) * rows_each] = lax.dot_general(
                eye, block, NT, preferred_element_type=F32
            ).astype(BF16)

    def align_rows():
        second = v_ref[:, :, 1].reshape(frames, width)
        for i in range(pieces):
            rows = slice(i * rows_each, (i + 1) * rows_each)
            partner_ref[rows, :] = lax.dot_general(
                onehot_ref[rows, :], second, NN, preferred_element_type=F32
            ).astype(BF16)

    def align_kernel(first, count):
        def step(i, carry):
            rows = pl.ds(pl.multiple_of(i * rows_each, rows_each), rows_each)
            block = partner_ref[rows, :]
            for j in range(nx * CORES):
                scores = lax.dot_general(block, p_ref[j], NT, preferred_element_type=F32)
                ka_ref[rows, j * pr : (j + 1) * pr] = jnp.exp2(
                    scores * (2.0 * LOG2_E / SOFT_TEMP)
                )
            return carry

        lax.fori_loop(first, first + count, step, 0)

    def align_dense(dense):
        row = jnp.concatenate([dense[b : b + 1, :] for b in range(fdense)], axis=1)
        high = row.astype(BF16).astype(F32)
        middle = (row - high).astype(BF16).astype(F32)
        low = row - high - middle
        parts = jnp.concatenate([high, middle, low, jnp.zeros((13, frames), F32)], axis=0)
        out = lax.dot_general(
            parts.astype(BF16), onehot_ref[...], NT, preferred_element_type=F32
        )
        total = out[0:1] + out[1:2] + out[2:3]
        return jnp.concatenate(
            [total[:, b * 128 : (b + 1) * 128] for b in range(fdense)], axis=0
        )

    transpose_view(0)
    align_rows()

    def soft_rows():
        total = soft_src[...]
        drain(soft_ybuf, soft_r.at[0])
        for j in range(len(ys)):
            total = total + soft_ybuf[j]
        soft_mid[...] = total

    def soft_totals():
        drain(soft_zbuf, soft_r.at[1])
        total = soft_mid[...]
        for j in range(len(zs)):
            total = total + soft_zbuf[j]
        transpose_view(1)
        for view in range(2):
            dense = total[view * fdense : (view + 1) * fdense]
            if view:
                dense = align_dense(dense)
            lanes_to_rows(grad_scale / dense, sb_ref, view, frames)
            r_ref[2 + view] = jnp.log(dense)

    def cross_sums():
        def step(i, carry):
            rows = pl.ds(pl.multiple_of(i * 32, 32), 32)
            sums = [jnp.zeros((32, 128), F32) for _ in range(3)]
            for t in range(ptiles):
                k = [ref[rows, t * 128 : (t + 1) * 128] for ref in (k_ref.at[0], ka_ref)]
                terms = [k[v] * c_ref[v, t : t + 1, :] for v in range(2)]
                sums[0] = sums[0] + terms[0] * jnp.log(k[1])
                sums[1] = sums[1] + terms[1] * jnp.log(k[0])
                sums[2] = sums[2] + terms[1]
            acc_ref[0, rows, :] = 0.5 * sums[0]
            acc_ref[1, rows, :] = 0.5 * sums[1]
            soft_acc_ref[1, rows, :] = sums[2]
            return carry

        lax.fori_loop(0, frames // 32, step, 0)
        for v in range(2):
            rows_to_lanes(acc_ref, v, t_ref.at[v], frames)
        rows_to_lanes(soft_acc_ref, 1, row_ref.at[1], frames)

    def sweep(it, carry):
        for view in (1, 0):
            c_ref[view] = 1.0 / dp_wait(view, it)
            frame_sums(view)
            yz_start(view, it)

        @pl.when(it == 0)
        def _():
            align_kernel(0, pieces)
            soft_rows()
            for j, device in enumerate(zs):
                send(soft_mid, soft_zbuf.at[j], soft_s.at[1], soft_r.at[1], device)

        @pl.when(it == 1)
        def _():
            soft_totals()

        @pl.when(it == ITERS - 1)
        def _():
            cross_sums()

        for view in (1, 0):
            r_ref[view] = 1.0 / yz_wait(view, it)

            @pl.when(it < ITERS - 1)
            def _(view=view):
                lanes_to_rows(r_ref[view], rb_ref, view, frames)
                proto_sums(view)
                dp_start(view, it + 1, column_totals(view))

            @pl.when(it == ITERS - 1)
            def _(view=view):
                if view:
                    r_ref[view] = align_dense(r_ref[view])
                lanes_to_rows(r_ref[view] * grad_scale, rb_ref, view, frames)

        return carry

    lax.fori_loop(0, ITERS, sweep, 0)

    loss = jnp.zeros((fdense, 128), F32)
    for v in range(2):
        loss = loss + r_ref[v] * (r_ref[3 - v] * row_ref[v] - t_ref[v])
    loss_src[0] = loss
    for j, device in enumerate(ys):
        send(loss_src.at[0], loss_ybuf.at[j], loss_s.at[0], loss_r.at[0], device)

    def loss_step(stage, buf, nextbuf, partners):
        drain(buf, loss_r.at[stage])
        total = loss_src[stage]
        for j in range(buf.shape[0]):
            total = total + buf[j]
        if nextbuf is None:
            return total
        loss_src[stage + 1] = total
        for j, device in enumerate(partners):
            send(
                loss_src.at[stage + 1],
                nextbuf.at[j],
                loss_s.at[stage + 1],
                loss_r.at[stage + 1],
                device,
            )
        return total

    def block_grad(owner):
        count = min(64, frames)
        for start in range(0, frames, count):
            rows = slice(start, start + count)
            for t in range(tiles_pr):
                tile = owner * tiles_pr + t
                cols = pl.ds(pl.multiple_of(tile * 128, 128), 128)
                k = [ref[rows, cols] for ref in (k_ref.at[0], ka_ref)]
                assigned = [
                    k[v] * (rb_ref[v, rows, :] * c_ref[v, pl.ds(tile, 1), :])
                    for v in range(2)
                ]
                for v in range(2):
                    w_ref[v, rows, t * 128 : (t + 1) * 128] = (
                        (k[v] * lax.rsqrt(k[v])) * sb_ref[v, rows, :] - assigned[1 - v]
                    ).astype(BF16)
        total = lax.dot_general(ut_ref[0], w_ref[0], NN, preferred_element_type=F32)
        total = total + lax.dot_general(ut_ref[1], w_ref[1], NN, preferred_element_type=F32)
        return total

    middle = width // 2
    lower, upper = pl.ds(0, middle), pl.ds(middle, middle)
    right, left = xs[0], xs[nx - 2]
    def scatter(n, carry):
        k, own = n // 2, n % 2
        d = (2 + 3 * k + (k // 2) * (3 - 2 * (k % 2))) % 4
        g_ref[k] = block_grad(lax.rem(x + d, nx) * CORES + lax.rem(core + 1 + own, CORES))

        @pl.when(own == 0)
        def _():
            ss_ref[k] = g_ref[k].astype(BF16)
            send(ss_ref.at[k], sr_ref.at[k], ss_s, ss_r.at[k], sib)

        @pl.when(own == 1)
        def _():
            drain(sr_ref.at[k], ss_r.at[k])

        @pl.when(n == 1)
        def _():
            xs_ref[0] = (g_ref[0] + sr_ref[0].astype(F32)).astype(BF16)
            send(xs_ref.at[0, lower], xo_ref.at[0], xo_s, xo_r.at[0], right)
            send(xs_ref.at[0, upper], xo_ref.at[1], xo_s, xo_r.at[1], left)

        @pl.when(n == 3)
        def _():
            xs_ref[1, upper] = (g_ref[1, upper] + sr_ref[1, upper].astype(F32)).astype(BF16)
            send(xs_ref.at[1, upper], xr_ref.at[0, upper], xs_s, xs_r, right)
            loss_step(0, loss_ybuf, loss_zbuf, zs)

        @pl.when(n == 5)
        def _():
            xs_ref[2, lower] = (g_ref[2, lower] + sr_ref[2, lower].astype(F32)).astype(BF16)
            send(xs_ref.at[2, lower], xr_ref.at[1, lower], xs_s, xs_r, left)
            for way, (rows, to) in enumerate(((lower, right), (upper, left))):
                drain(xo_ref.at[way], xo_r.at[way])
                xs_ref[1 + way, rows] = (
                    g_ref[1 + way, rows]
                    + sr_ref[1 + way, rows].astype(F32)
                    + xo_ref[way].astype(F32)
                ).astype(BF16)
                send(xs_ref.at[1 + way, rows], xr_ref.at[way, rows], xs_s, xs_r, to)

        return carry

    lax.fori_loop(0, 2 * nx, scatter, 0)
    loss_step(1, loss_zbuf, loss_xbuf, dps)
    drain(xr_ref, xs_r)
    stores = []
    for i in range(width // 128):
        rows = slice(i * 128, (i + 1) * 128)
        for t in range(tiles_pr):
            cols = slice(t * 128, (t + 1) * 128)
            total = g_ref[3, rows, cols] + sr_ref[3, rows, cols].astype(F32)
            for j in range(2):
                total = total + xr_ref[j, rows, cols].astype(F32)
            grad_out[cols, rows] = total.T
        stores.append(
            pltpu.make_async_copy(grad_out.at[:, rows], grad_ref.at[:, rows], out_s.at[i])
        )
        stores[i].start()
    total = loss_step(2, loss_xbuf, None, None)
    loss_ref[0, 0] = jnp.sum(total) / (2.0 * frames * nx * CORES)

    for store in stores:
        store.wait()
    drain(v_ref.at[0, pl.ds(0, ny - 1)], ay_s)
    drain(v_ref.at[pl.ds(0, 2 * (last - 1)), 0], zr_s.at[0])
    drain(v_ref.at[pl.ds(0, 2 * near - split), pl.ds(0, ny - 1)], zr_s.at[1])
    drain(chunk(0), zo_s)
    drain(v_ref.at[pl.ds(0, 2 * (last - 1 - near) + 1 + split), pl.ds(0, ny - 1)], fy_s)
    drain(p_ref.at[pl.ds(0, 3)], px_s)
    drain(p_ref.at[pl.ds(0, nx)], ps_s)
    for view in range(2):
        for slot in range(min(2, ITERS)):
            drain(dp_buf.at[view, slot], dp_s.at[view, slot])
            drain(y_buf.at[view, slot], y_s.at[view, slot])
    drain(soft_ybuf, soft_s.at[0])
    drain(soft_zbuf, soft_s.at[1])
    drain(loss_ybuf, loss_s.at[0])
    drain(loss_zbuf, loss_s.at[1])
    drain(loss_xbuf, loss_s.at[2])
    drain(sr_ref, ss_s)
    drain(xo_ref, xo_s)
    drain(xr_ref, xs_s)


def solution(mesh):
    ndp, nproto = mesh.shape["dp"], mesh.shape["proto"]
    nx, nz = ndp // CORES, DEPTH
    ny = nproto // nz

    def local(first, second, protos, pairing):
        fr, width = first.shape
        pr = protos.shape[0]
        frames = fr * nproto
        cols = pr * ndp
        fd = frames // 128
        ct = cols // 128
        sem = pltpu.SemaphoreType.DMA
        sizes = (nx, ny, nz, fr, width, pr)
        vmem = pltpu.VMEM
        grad, loss = pl.pallas_call(
            functools.partial(kernel, sizes),
            out_shape=(
                jax.ShapeDtypeStruct((pr, width), F32),
                jax.ShapeDtypeStruct((1, 1), F32),
            ),
            in_specs=[pl.BlockSpec(memory_space=pl.ANY)] * 4,
            out_specs=(
                pl.BlockSpec(memory_space=pl.ANY),
                pl.BlockSpec(memory_space=pltpu.SMEM),
            ),
            scratch_shapes=[
                vmem((fr, width), BF16),
                vmem((fr, width), BF16),
                vmem((pr, width), F32),
                vmem((fd, 128), jnp.int32),
                vmem((pr, width), F32),
                vmem((nz, ny, 2, fr, width), BF16),
                vmem((frames, width), BF16),
                vmem((ndp, pr, width), BF16),
                vmem((frames, frames), BF16),
                vmem((2, width, frames), BF16),
                vmem((2, frames, cols), F32),
                vmem((frames, cols), F32),
                vmem((2, frames, 128), F32),
                vmem((2, frames, 128), F32),
                vmem((2, frames, 128), F32),
                vmem((2, frames, 128), F32),
                vmem((2, 8, cols), F32),
                vmem((2, ct, 128), F32),
                vmem((4, fd, 128), F32),
                vmem((2, fd, 128), F32),
                vmem((2, fd, 128), F32),
                vmem((2, frames, pr), BF16),
                vmem((nx, width, pr), F32),
                vmem((2, 2, ct, 128), F32),
                vmem((2, 2, ndp - 1, ct, 128), F32),
                vmem((2, 2, fd, 128), F32),
                vmem((2, 2, nproto - 1, fd, 128), F32),
                vmem((2 * fd, 128), F32),
                vmem((ny - 1, 2 * fd, 128), F32),
                vmem((2 * fd, 128), F32),
                vmem((nz - 1, 2 * fd, 128), F32),
                vmem((3, fd, 128), F32),
                vmem((ny - 1, fd, 128), F32),
                vmem((nz - 1, fd, 128), F32),
                vmem((ndp - 1, fd, 128), F32),
                vmem((nx, width, pr), BF16),
                vmem((nx, width, pr), BF16),
                vmem((nx - 1, width, pr), BF16),
                vmem((2, width, pr), BF16),
                vmem((2, width // 2, pr), BF16),
                sem((4,)), sem((width // 128,)),
                sem, sem((ny - 1,)),
                sem((2,)), sem((2, nz // 2, ny)),
                sem, sem,
                sem, sem((nz,)),
                sem, sem((2, 2)), sem((2,)),
                sem, sem,
                sem((2, 2)), sem((2, 2)),
                sem((2, 2)), sem((2, 2)),
                sem((2,)), sem((2,)),
                sem((3,)), sem((3,)),
                sem, sem((nx,)),
                sem, sem,
                sem, sem((2,)),
            ],
            compiler_params=pltpu.CompilerParams(
                collective_id=0, has_side_effects=True, vmem_limit_bytes=56 * 2**20
            ),
        )(first, second, protos, pairing.reshape(fd, 128))
        return grad, loss[0, 0]

    return jax.shard_map(
        local,
        mesh=mesh,
        in_specs=(
            P(("dp", "proto"), None),
            P(("dp", "proto"), None),
            P(("dp", "proto"), None),
            P("dp"),
        ),
        out_specs=(P(("dp", "proto"), None), P()),
        check_vma=False,
    )
```

```python
import functools
import math

import jax
import jax.numpy as jnp
from jax import lax
from jax.experimental import pallas as pl
from jax.experimental.pallas import tpu as pltpu
from jax.sharding import PartitionSpec as P

ITERS = 3
SOFT_TEMP = 0.1
LOG2_E = math.log2(math.e)
NORM_EPS = 1e-06
CORES = 2
DEPTH = 8

F32 = jnp.float32
BF16 = jnp.bfloat16
NT = (((1,), (1,)), ((), ()))
NN = (((1,), (0,)), ((), ()))


def unit_rows(matrix):
    widened = matrix.astype(F32)
    return (
        widened * lax.rsqrt(jnp.sum(widened * widened, axis=-1, keepdims=True) + NORM_EPS)
    ).astype(BF16)


def drain(ref, sem):
    pltpu.make_async_copy(ref, ref, sem).wait()


def rows_to_lanes(acc_ref, view, out_ref, rows):
    for b in range(rows // 128):
        block = acc_ref[view, b * 128 : (b + 1) * 128, :]
        out_ref[b : b + 1, :] = jnp.sum(block.T, axis=0, keepdims=True)


def lanes_to_rows(dense, out_ref, view, rows):
    for b in range(rows // 128):
        block = jnp.broadcast_to(dense[b : b + 1, :], (128, 128))
        out_ref[view, b * 128 : (b + 1) * 128, :] = block.T


def kernel(
    sizes,
    first_ref,
    second_ref,
    protos_ref,
    pair_ref,
    grad_ref,
    loss_ref,
    first_in,
    second_in,
    protos_in,
    pair_in,
    grad_out,
    v_ref,
    partner_ref,
    p_ref,
    onehot_ref,
    ut_ref,
    k_ref,
    ka_ref,
    acc_ref,
    soft_acc_ref,
    rb_ref,
    sb_ref,
    cs_ref,
    c_ref,
    r_ref,
    row_ref,
    t_ref,
    w_ref,
    g_ref,
    dp_src,
    dp_buf,
    y_src,
    y_buf,
    soft_src,
    soft_ybuf,
    soft_mid,
    soft_zbuf,
    loss_src,
    loss_ybuf,
    loss_zbuf,
    loss_xbuf,
    ss_ref,
    sr_ref,
    xs_ref,
    xr_ref,
    xo_ref,
    in_s,
    out_s,
    ay_s,
    ay_r,
    zr_s,
    zr_r,
    zo_s,
    zo_r,
    fy_s,
    fy_r,
    px_s,
    px_r,
    po_r,
    ps_s,
    ps_r,
    dp_s,
    dp_r,
    y_s,
    y_r,
    soft_s,
    soft_r,
    loss_s,
    loss_r,
    ss_s,
    ss_r,
    xs_s,
    xs_r,
    xo_s,
    xo_r,
):
    nx, ny, nz, fr, width, pr = sizes
    frames = fr * ny * nz
    group = fr * ny
    protos = pr * nx * CORES
    ptiles = protos // 128
    tiles_pr = pr // 128
    fdense = frames // 128
    grad_scale = protos * ny * nz / (SOFT_TEMP * math.sqrt(2.0 * frames * nx * CORES))

    dp, pi = lax.axis_index("dp"), lax.axis_index("proto")
    x, core = dp // CORES, dp % CORES
    y, z = pi // nz, pi % nz

    def at(dx=0, dc=0, dy=0, dz=0):
        return {
            "dp": lax.rem(x + dx, nx) * CORES + lax.rem(core + dc, CORES),
            "proto": lax.rem(y + dy, ny) * nz + lax.rem(z + dz, nz),
        }

    def send(src, dst, ssem, rsem, device):
        pltpu.make_async_remote_copy(
            src_ref=src,
            dst_ref=dst,
            send_sem=ssem,
            recv_sem=rsem,
            device_id=device,
            device_id_type=pl.DeviceIdType.MESH,
        ).start()

    sib = at(dc=1)
    xs = [at(dx=d) for d in range(1, nx)]
    ys = [at(dy=d) for d in range(1, ny)]
    zs = [at(dz=d) for d in range(1, nz)]
    around = lambda d, n: min(d, n - d)
    offsets = [(d, e) for d in range(ny) for e in range(nz) if d or e]
    offsets.sort(key=lambda o: -around(o[0], ny) - around(o[1], nz))
    yzs = [at(dy=d, dz=e) for d, e in offsets]
    dps = [at(dx=d, dc=e) for d in range(nx) for e in range(CORES) if d or e]

    last = nz // 2
    near = max(1, last - 2)
    split = near > 1

    def chunk(dz, q=0):
        return v_ref.at[lax.rem(z + nz + dz, nz), lax.rem(y + ny - q, ny)]

    def ring_send(step, q):
        for way, sign in enumerate((-1, 1)):
            part = chunk(sign * (step - 1), q)
            if q and split and step == near:
                part = part.at[0]
            send(part, part, zr_s.at[min(q, 1)], zr_r.at[way, step - 1, q], zs[0 if way == 0 else nz - 2])

    def ring_skip():
        for way in range(2):
            to = zs[1 if way == 0 else nz - 3]
            send(chunk(0), chunk(0), zr_s.at[0], zr_r.at[way, 1, 0], to)

    def ring_wait(step, q):
        for way, sign in enumerate((-1, 1)):
            part = chunk(sign * step, q)
            drain(part.at[0] if q and split and step == near else part, zr_r.at[way, step - 1, q])

    def far_part(dz):
        return chunk(dz).at[1] if abs(dz) == near else chunk(dz)

    def far_send(dz, index):
        for device in ys:
            send(far_part(dz), far_part(dz), fy_s, fy_r.at[index], device)

    def far_wait(dz, index):
        block = v_ref.at[lax.rem(z + nz + dz, nz), pl.ds(0, ny - 1)]
        drain(block.at[:, 1] if abs(dz) == near else block, fy_r.at[index])

    def far_index(dz):
        if dz == last:
            return 0
        return 2 * (abs(dz) - near) + (1 if dz < 0 else 2)

    half = pr // 2

    def proto_half(dx, part):
        owner = lax.rem(x + nx + dx, nx) * CORES + core
        return p_ref.at[owner, pl.ds(part * half, half)]

    def proto_near(way, part):
        piece = proto_half(-1 if way == 0 else 1, part)
        drain(piece, px_r.at[way, part])
        if part == way:
            send(piece, piece, px_s, po_r.at[part], xs[0 if way == 0 else nx - 2])
        send(piece, piece, ps_s, ps_r, sib)

    def proto_far(part):
        piece = proto_half(2, part)
        drain(piece, po_r.at[part])
        send(piece, piece, ps_s, ps_r, sib)

    loads = [
        pltpu.make_async_copy(source, target, in_s.at[i])
        for i, (source, target) in enumerate(
            (
                (first_ref, first_in),
                (second_ref, second_in),
                (protos_ref, protos_in),
                (pair_ref, pair_in),
            )
        )
    ]
    for load in loads:
        load.start()

    greeted = [sib, xs[0], xs[nx - 2], *ys]
    greeted += [zs[d - 1] for d in sorted({1, 2, last, nz - 2, nz - 1})]
    barrier = pltpu.get_barrier_semaphore()
    for device in greeted:
        pl.semaphore_signal(
            barrier, inc=1, device_id=device, device_id_type=pl.DeviceIdType.MESH
        )
    for load in loads:
        load.wait()
    v_ref[z, y, 0] = unit_rows(first_in[...])
    v_ref[z, y, 1] = unit_rows(second_in[...])
    p_ref[dp] = unit_rows(protos_in[...])
    pl.semaphore_wait(barrier, len(greeted))

    for j, device in enumerate(ys):
        send(chunk(0), chunk(0), ay_s, ay_r.at[j], device)
    if last > 2:
        ring_skip()
    send(chunk(0), chunk(0), zo_s, zo_r, zs[last - 1])
    ring_send(1, 0)
    for part in range(2):
        for way in range(2):
            piece = proto_half(0, part if way == 0 else 1 - part)
            where = px_r.at[way, part if way == 0 else 1 - part]
            send(piece, piece, px_s, where, xs[0 if way == 0 else nx - 2])
    send(p_ref.at[dp], p_ref.at[dp], ps_s, ps_r, sib)

    pair = pair_in[...]
    where = (pair % (nz * fr) // fr) * group + (pair // (nz * fr)) * fr + pair % fr
    where = where.astype(F32)
    for b in range(fdense):
        column = jnp.broadcast_to(where[b : b + 1, :], (128, 128)).T
        for t in range(fdense):
            lane = (lax.broadcasted_iota(jnp.int32, (128, 128), 1) + t * 128).astype(F32)
            block = jnp.where(column == lane, 1.0, 0.0).astype(BF16)
            for q in range(128 // fr):
                natural = b * 128 + q * fr
                row = (natural % (nz * fr) // fr) * group + natural // (nz * fr) * fr
                onehot_ref[row : row + fr, t * 128 : (t + 1) * 128] = block[
                    q * fr : (q + 1) * fr, :
                ]
    cs_ref[...] = jnp.zeros_like(cs_ref)
    soft_acc_ref[...] = jnp.zeros_like(soft_acc_ref)

    def first_pass(view, starts, block):
        count = block.shape[0]
        each = count // len(starts)
        soft = jnp.zeros((count, 128), F32)
        for j in range(nx * CORES):
            scores = lax.dot_general(block, p_ref[j], NT, preferred_element_type=F32)
            e = jnp.exp2(scores * (LOG2_E / SOFT_TEMP))
            k = e * e
            for i, start in enumerate(starts):
                rows = pl.ds(pl.multiple_of(start, each), each)
                k_ref[view, rows, j * pr : (j + 1) * pr] = k[i * each : (i + 1) * each]
            for t in range(tiles_pr):
                soft = soft + e[:, t * 128 : (t + 1) * 128]
            cs_ref[view, :, j * pr : (j + 1) * pr] += jnp.sum(
                k.reshape(count // 8, 8, pr), axis=0
            )
        for i, start in enumerate(starts):
            rows = pl.ds(pl.multiple_of(start, each), each)
            soft_acc_ref[view, rows, :] = soft[i * each : (i + 1) * each]

    def frames_y(q):
        drain(chunk(0, q), ay_r.at[q - 1])
        ring_send(1, q)

    def ring_next(step, q):
        ring_wait(step, q)
        if (1 < step < last - 1) if q == 0 else step < near:
            ring_send(step + 1, q)
        if q == 0 and (step > near or (split and step == near)):
            far_send(-step, far_index(-step))
            far_send(step, far_index(step))

    def opposite():
        drain(chunk(last), zo_r)
        far_send(last, far_index(last))

    events = [(6.5, opposite)]
    for q in range(1, ny):
        events.append((4.0 + 0.5 * q, functools.partial(frames_y, q)))
    for step in range(1, last):
        when = 7.0 if step == 1 else 3.9 + 5.0 * (step - 2)
        events.append((when, functools.partial(ring_next, step, 0)))
    for q in range(1, ny):
        for step in range(1, near):
            when = 6.0 + 3.5 * step + 1.3 * q
            events.append((when, functools.partial(ring_next, step, q)))
    for way in range(2):
        events.append((6.0 + 0.1 * way, functools.partial(proto_near, way, way)))
        events.append((8.6 + 0.1 * way, functools.partial(proto_near, way, 1 - way)))
        events.append((12.0 + 0.1 * way, functools.partial(proto_far, way)))
    for when, event in sorted(events, key=lambda pair: pair[0]):
        event()
    drain(p_ref.at[pl.ds(0, nx)], ps_r)

    def dp_start(view, it, source):
        slot = it % 2

        @pl.when(it >= 2)
        def _():
            drain(dp_buf.at[view, slot], dp_s.at[view, slot])

        dp_src[view, slot] = source
        for j, device in enumerate(dps):
            send(
                dp_src.at[view, slot],
                dp_buf.at[view, slot, j],
                dp_s.at[view, slot],
                dp_r.at[view, slot],
                device,
            )

    def dp_wait(view, it):
        slot = it % 2
        drain(dp_buf.at[view, slot], dp_r.at[view, slot])
        total = dp_src[view, slot]
        for j in range(len(dps)):
            total = total + dp_buf[view, slot, j]
        return total

    def yz_start(view, it):
        slot = it % 2

        @pl.when(it >= 2)
        def _():
            drain(y_buf.at[view, slot], y_s.at[view, slot])

        y_src[view, slot] = row_ref[view]
        for j, device in enumerate(yzs):
            send(
                y_src.at[view, slot],
                y_buf.at[view, slot, j],
                y_s.at[view, slot],
                y_r.at[view, slot],
                device,
            )

    def yz_wait(view, it):
        slot = it % 2
        drain(y_buf.at[view, slot], y_r.at[view, slot])
        total = y_src[view, slot]
        for j in range(len(yzs)):
            total = total + y_buf[view, slot, j]
        return total

    def column_totals(view):
        parts = [
            jnp.sum(cs_ref[view, :, t * 128 : (t + 1) * 128], axis=0, keepdims=True)
            for t in range(ptiles)
        ]
        return jnp.concatenate(parts, axis=0)

    def frame_sums(view):
        def step(b, carry):
            rows = pl.ds(pl.multiple_of(b * 128, 128), 128)
            total = jnp.zeros((128, 128), F32)
            for t in range(ptiles):
                k = k_ref[view, rows, t * 128 : (t + 1) * 128]
                total = total + k * c_ref[view, t : t + 1, :]
            row_ref[view, pl.ds(b, 1), :] = jnp.sum(total.T, axis=0, keepdims=True)
            return carry

        lax.fori_loop(0, fdense, step, 0, unroll=fdense)

    def proto_sums(view):
        def step(i, totals):
            rows = pl.ds(pl.multiple_of(i * 64, 64), 64)
            scale = rb_ref[view, rows, :]
            out = []
            for t in range(ptiles):
                k = k_ref[view, rows, t * 128 : (t + 1) * 128]
                out.append(totals[t] + jnp.sum((k * scale).reshape(8, 8, 128), axis=0))
            return tuple(out)

        totals = lax.fori_loop(
            0,
            frames // 64,
            step,
            tuple(jnp.zeros((8, 128), F32) for _ in range(ptiles)),
            unroll=2,
        )
        for t in range(ptiles):
            cs_ref[view, :, t * 128 : (t + 1) * 128] = totals[t]

    zero = jnp.int32(0)

    def pair_wait(p):
        if p == 0:
            if near == 1:
                for q in range(1, ny):
                    ring_wait(1, q)
        elif p == 1:
            far_wait(last, far_index(last))
        else:
            step = p
            if step <= near:
                for q in range(1, ny):
                    ring_wait(step, q)
            far_wait(-step, far_index(-step))
            far_wait(step, far_index(step))

    def pair_pass(n, carry):
        p, view = n // 2, 1 - n % 2
        for known in range(last):

            @pl.when(n == 2 * known)
            def _(known=known):
                pair_wait(known)

        opposite_pair = 1 - lax.min((p - 1) * (p - 1), 1)
        step = p + 1 - lax.min(p, 1) + opposite_pair * (last - 1)
        one = lax.rem(z + step, nz)
        two = lax.rem(z + nz - step * (1 - opposite_pair), nz)
        block = jnp.concatenate(
            [v_ref[b, :, view].reshape(group, width) for b in (one, two)], axis=0
        )
        first_pass(view, [one * group, two * group], block)

        @pl.when(n == 2 * last - 2)
        def _():
            dp_start(1, zero, column_totals(1))

        return carry

    lax.fori_loop(0, 2 * last, pair_pass, 0)
    dp_start(0, zero, column_totals(0))

    for view in range(2):
        rows_to_lanes(soft_acc_ref, view, soft_src.at[pl.ds(view * fdense, fdense)], frames)
    for j, device in enumerate(ys):
        send(soft_src, soft_ybuf.at[j], soft_s.at[0], soft_r.at[0], device)

    eye = jnp.where(
        lax.broadcasted_iota(jnp.int32, (width, width), 0)
        == lax.broadcasted_iota(jnp.int32, (width, width), 1),
        1.0,
        0.0,
    ).astype(BF16)

    rows_each = min(256, frames)
    pieces = frames // rows_each

    def transpose_view(view):
        for i in range(pieces):
            if view:
                block = partner_ref[i * rows_each : (i + 1) * rows_each, :]
            else:
                count = rows_each // group
                block = v_ref[i * count : (i + 1) * count, :, 0].reshape(rows_each, width)
            ut_ref[view, :, i * rows_each : (i + 1) * rows_each] = lax.dot_general(
                eye, block, NT, preferred_element_type=F32
            ).astype(BF16)

    def align_rows():
        second = v_ref[:, :, 1].reshape(frames, width)
        for i in range(pieces):
            rows = slice(i * rows_each, (i + 1) * rows_each)
            partner_ref[rows, :] = lax.dot_general(
                onehot_ref[rows, :], second, NN, preferred_element_type=F32
            ).astype(BF16)

    def align_kernel(first, count):
        def step(i, carry):
            rows = pl.ds(pl.multiple_of(i * rows_each, rows_each), rows_each)
            block = partner_ref[rows, :]
            for j in range(nx * CORES):
                scores = lax.dot_general(block, p_ref[j], NT, preferred_element_type=F32)
                ka_ref[rows, j * pr : (j + 1) * pr] = jnp.exp2(
                    scores * (2.0 * LOG2_E / SOFT_TEMP)
                )
            return carry

        lax.fori_loop(first, first + count, step, 0)

    def align_dense(dense):
        row = jnp.concatenate([dense[b : b + 1, :] for b in range(fdense)], axis=1)
        high = row.astype(BF16).astype(F32)
        middle = (row - high).astype(BF16).astype(F32)
        low = row - high - middle
        parts = jnp.concatenate([high, middle, low, jnp.zeros((13, frames), F32)], axis=0)
        out = lax.dot_general(
            parts.astype(BF16), onehot_ref[...], NT, preferred_element_type=F32
        )
        total = out[0:1] + out[1:2] + out[2:3]
        return jnp.concatenate(
            [total[:, b * 128 : (b + 1) * 128] for b in range(fdense)], axis=0
        )

    transpose_view(0)
    align_rows()

    def soft_rows():
        total = soft_src[...]
        drain(soft_ybuf, soft_r.at[0])
        for j in range(len(ys)):
            total = total + soft_ybuf[j]
        soft_mid[...] = total

    def soft_totals():
        drain(soft_zbuf, soft_r.at[1])
        total = soft_mid[...]
        for j in range(len(zs)):
            total = total + soft_zbuf[j]
        transpose_view(1)
        for view in range(2):
            dense = total[view * fdense : (view + 1) * fdense]
            if view:
                dense = align_dense(dense)
            lanes_to_rows(grad_scale / dense, sb_ref, view, frames)
            r_ref[2 + view] = jnp.log(dense)

    def cross_sums():
        def step(i, carry):
            rows = pl.ds(pl.multiple_of(i * 32, 32), 32)
            sums = [jnp.zeros((32, 128), F32) for _ in range(3)]
            for t in range(ptiles):
                k = [ref[rows, t * 128 : (t + 1) * 128] for ref in (k_ref.at[0], ka_ref)]
                terms = [k[v] * c_ref[v, t : t + 1, :] for v in range(2)]
                sums[0] = sums[0] + terms[0] * jnp.log(k[1])
                sums[1] = sums[1] + terms[1] * jnp.log(k[0])
                sums[2] = sums[2] + terms[1]
            acc_ref[0, rows, :] = 0.5 * sums[0]
            acc_ref[1, rows, :] = 0.5 * sums[1]
            soft_acc_ref[1, rows, :] = sums[2]
            return carry

        lax.fori_loop(0, frames // 32, step, 0)
        for v in range(2):
            rows_to_lanes(acc_ref, v, t_ref.at[v], frames)
        rows_to_lanes(soft_acc_ref, 1, row_ref.at[1], frames)

    def sweep(it, carry):
        for view in (1, 0):
            c_ref[view] = 1.0 / dp_wait(view, it)
            frame_sums(view)
            yz_start(view, it)

        @pl.when(it == 0)
        def _():
            align_kernel(0, pieces)
            soft_rows()
            for j, device in enumerate(zs):
                send(soft_mid, soft_zbuf.at[j], soft_s.at[1], soft_r.at[1], device)

        @pl.when(it == 1)
        def _():
            soft_totals()

        @pl.when(it == ITERS - 1)
        def _():
            cross_sums()

        for view in (1, 0):
            r_ref[view] = 1.0 / yz_wait(view, it)

            @pl.when(it < ITERS - 1)
            def _(view=view):
                lanes_to_rows(r_ref[view], rb_ref, view, frames)
                proto_sums(view)
                dp_start(view, it + 1, column_totals(view))

            @pl.when(it == ITERS - 1)
            def _(view=view):
                if view:
                    r_ref[view] = align_dense(r_ref[view])
                lanes_to_rows(r_ref[view] * grad_scale, rb_ref, view, frames)

        return carry

    lax.fori_loop(0, ITERS, sweep, 0)

    loss = jnp.zeros((fdense, 128), F32)
    for v in range(2):
        loss = loss + r_ref[v] * (r_ref[3 - v] * row_ref[v] - t_ref[v])
    loss_src[0] = loss
    for j, device in enumerate(ys):
        send(loss_src.at[0], loss_ybuf.at[j], loss_s.at[0], loss_r.at[0], device)

    def loss_step(stage, buf, nextbuf, partners):
        drain(buf, loss_r.at[stage])
        total = loss_src[stage]
        for j in range(buf.shape[0]):
            total = total + buf[j]
        if nextbuf is None:
            return total
        loss_src[stage + 1] = total
        for j, device in enumerate(partners):
            send(
                loss_src.at[stage + 1],
                nextbuf.at[j],
                loss_s.at[stage + 1],
                loss_r.at[stage + 1],
                device,
            )
        return total

    def block_grad(owner):
        count = min(64, frames)
        for start in range(0, frames, count):
            rows = slice(start, start + count)
            for t in range(tiles_pr):
                tile = owner * tiles_pr + t
                cols = pl.ds(pl.multiple_of(tile * 128, 128), 128)
                k = [ref[rows, cols] for ref in (k_ref.at[0], ka_ref)]
                assigned = [
                    k[v] * (rb_ref[v, rows, :] * c_ref[v, pl.ds(tile, 1), :])
                    for v in range(2)
                ]
                for v in range(2):
                    w_ref[v, rows, t * 128 : (t + 1) * 128] = (
                        (k[v] * lax.rsqrt(k[v])) * sb_ref[v, rows, :] - assigned[1 - v]
                    ).astype(BF16)
        total = lax.dot_general(ut_ref[0], w_ref[0], NN, preferred_element_type=F32)
        total = total + lax.dot_general(ut_ref[1], w_ref[1], NN, preferred_element_type=F32)
        return total

    middle = width // 2
    lower, upper = pl.ds(0, middle), pl.ds(middle, middle)
    right, left = xs[0], xs[nx - 2]
    def scatter(n, carry):
        k, own = n // 2, n % 2
        d = (2 + 3 * k + (k // 2) * (3 - 2 * (k % 2))) % 4
        g_ref[k] = block_grad(lax.rem(x + d, nx) * CORES + lax.rem(core + 1 + own, CORES))

        @pl.when(own == 0)
        def _():
            ss_ref[k] = g_ref[k].astype(BF16)
            send(ss_ref.at[k], sr_ref.at[k], ss_s, ss_r.at[k], sib)

        @pl.when(own == 1)
        def _():
            drain(sr_ref.at[k], ss_r.at[k])

        @pl.when(n == 1)
        def _():
            xs_ref[0] = (g_ref[0] + sr_ref[0].astype(F32)).astype(BF16)
            send(xs_ref.at[0, lower], xo_ref.at[0], xo_s, xo_r.at[0], right)
            send(xs_ref.at[0, upper], xo_ref.at[1], xo_s, xo_r.at[1], left)

        @pl.when(n == 3)
        def _():
            xs_ref[1, upper] = (g_ref[1, upper] + sr_ref[1, upper].astype(F32)).astype(BF16)
            send(xs_ref.at[1, upper], xr_ref.at[0, upper], xs_s, xs_r, right)
            loss_step(0, loss_ybuf, loss_zbuf, zs)

        @pl.when(n == 5)
        def _():
            xs_ref[2, lower] = (g_ref[2, lower] + sr_ref[2, lower].astype(F32)).astype(BF16)
            send(xs_ref.at[2, lower], xr_ref.at[1, lower], xs_s, xs_r, left)
            for way, (rows, to) in enumerate(((lower, right), (upper, left))):
                drain(xo_ref.at[way], xo_r.at[way])
                xs_ref[1 + way, rows] = (
                    g_ref[1 + way, rows]
                    + sr_ref[1 + way, rows].astype(F32)
                    + xo_ref[way].astype(F32)
                ).astype(BF16)
                send(xs_ref.at[1 + way, rows], xr_ref.at[way, rows], xs_s, xs_r, to)

        return carry

    lax.fori_loop(0, 2 * nx, scatter, 0)
    loss_step(1, loss_zbuf, loss_xbuf, dps)
    drain(xr_ref, xs_r)
    stores = []
    for i in range(width // 128):
        rows = slice(i * 128, (i + 1) * 128)
        for t in range(tiles_pr):
            cols = slice(t * 128, (t + 1) * 128)
            total = g_ref[3, rows, cols] + sr_ref[3, rows, cols].astype(F32)
            for j in range(2):
                total = total + xr_ref[j, rows, cols].astype(F32)
            grad_out[cols, rows] = total.T
        stores.append(
            pltpu.make_async_copy(grad_out.at[:, rows], grad_ref.at[:, rows], out_s.at[i])
        )
        stores[i].start()
    total = loss_step(2, loss_xbuf, None, None)
    loss_ref[0, 0] = jnp.sum(total) / (2.0 * frames * nx * CORES)

    for store in stores:
        store.wait()
    drain(v_ref.at[0, pl.ds(0, ny - 1)], ay_s)
    drain(v_ref.at[pl.ds(0, 2 * (last - 1)), 0], zr_s.at[0])
    drain(v_ref.at[pl.ds(0, 2 * near - split), pl.ds(0, ny - 1)], zr_s.at[1])
    drain(chunk(0), zo_s)
    drain(v_ref.at[pl.ds(0, 2 * (last - 1 - near) + 1 + split), pl.ds(0, ny - 1)], fy_s)
    drain(p_ref.at[pl.ds(0, 3)], px_s)
    drain(p_ref.at[pl.ds(0, nx)], ps_s)
    for view in range(2):
        for slot in range(min(2, ITERS)):
            drain(dp_buf.at[view, slot], dp_s.at[view, slot])
            drain(y_buf.at[view, slot], y_s.at[view, slot])
    drain(soft_ybuf, soft_s.at[0])
    drain(soft_zbuf, soft_s.at[1])
    drain(loss_ybuf, loss_s.at[0])
    drain(loss_zbuf, loss_s.at[1])
    drain(loss_xbuf, loss_s.at[2])
    drain(sr_ref, ss_s)
    drain(xo_ref, xo_s)
    drain(xr_ref, xs_s)


def solution(mesh):
    ndp, nproto = mesh.shape["dp"], mesh.shape["proto"]
    nx, nz = ndp // CORES, DEPTH
    ny = nproto // nz

    def local(first, second, protos, pairing):
        fr, width = first.shape
        pr = protos.shape[0]
        frames = fr * nproto
        cols = pr * ndp
        fd = frames // 128
        ct = cols // 128
        sem = pltpu.SemaphoreType.DMA
        sizes = (nx, ny, nz, fr, width, pr)
        vmem = pltpu.VMEM
        grad, loss = pl.pallas_call(
            functools.partial(kernel, sizes),
            out_shape=(
                jax.ShapeDtypeStruct((pr, width), F32),
                jax.ShapeDtypeStruct((1, 1), F32),
            ),
            in_specs=[pl.BlockSpec(memory_space=pl.ANY)] * 4,
            out_specs=(
                pl.BlockSpec(memory_space=pl.ANY),
                pl.BlockSpec(memory_space=pltpu.SMEM),
            ),
            scratch_shapes=[
                vmem((fr, width), BF16),
                vmem((fr, width), BF16),
                vmem((pr, width), F32),
                vmem((fd, 128), jnp.int32),
                vmem((pr, width), F32),
                vmem((nz, ny, 2, fr, width), BF16),
                vmem((frames, width), BF16),
                vmem((ndp, pr, width), BF16),
                vmem((frames, frames), BF16),
                vmem((2, width, frames), BF16),
                vmem((2, frames, cols), F32),
                vmem((frames, cols), F32),
                vmem((2, frames, 128), F32),
                vmem((2, frames, 128), F32),
                vmem((2, frames, 128), F32),
                vmem((2, frames, 128), F32),
                vmem((2, 8, cols), F32),
                vmem((2, ct, 128), F32),
                vmem((4, fd, 128), F32),
                vmem((2, fd, 128), F32),
                vmem((2, fd, 128), F32),
                vmem((2, frames, pr), BF16),
                vmem((nx, width, pr), F32),
                vmem((2, 2, ct, 128), F32),
                vmem((2, 2, ndp - 1, ct, 128), F32),
                vmem((2, 2, fd, 128), F32),
                vmem((2, 2, nproto - 1, fd, 128), F32),
                vmem((2 * fd, 128), F32),
                vmem((ny - 1, 2 * fd, 128), F32),
                vmem((2 * fd, 128), F32),
                vmem((nz - 1, 2 * fd, 128), F32),
                vmem((3, fd, 128), F32),
                vmem((ny - 1, fd, 128), F32),
                vmem((nz - 1, fd, 128), F32),
                vmem((ndp - 1, fd, 128), F32),
                vmem((nx, width, pr), BF16),
                vmem((nx, width, pr), BF16),
                vmem((nx - 1, width, pr), BF16),
                vmem((2, width, pr), BF16),
                vmem((2, width // 2, pr), BF16),
                sem((4,)), sem((width // 128,)),
                sem, sem((ny - 1,)),
                sem((2,)), sem((2, nz // 2, ny)),
                sem, sem,
                sem, sem((nz,)),
                sem, sem((2, 2)), sem((2,)),
                sem, sem,
                sem((2, 2)), sem((2, 2)),
                sem((2, 2)), sem((2, 2)),
                sem((2,)), sem((2,)),
                sem((3,)), sem((3,)),
                sem, sem((nx,)),
                sem, sem,
                sem, sem((2,)),
            ],
            compiler_params=pltpu.CompilerParams(
                collective_id=0, has_side_effects=True, vmem_limit_bytes=56 * 2**20
            ),
        )(first, second, protos, pairing.reshape(fd, 128))
        return grad, loss[0, 0]

    return jax.shard_map(
        local,
        mesh=mesh,
        in_specs=(
            P(("dp", "proto"), None),
            P(("dp", "proto"), None),
            P(("dp", "proto"), None),
            P("dp"),
        ),
        out_specs=(P(("dp", "proto"), None), P()),
        check_vma=False,
    )
```

```python
import functools
import math

import jax
import jax.numpy as jnp
from jax import lax
from jax.experimental import pallas as pl
from jax.experimental.pallas import tpu as pltpu
from jax.sharding import PartitionSpec as P

ITERS = 3
SOFT_TEMP = 0.1
LOG2_E = math.log2(math.e)
NORM_EPS = 1e-06
CORES = 2
DEPTH = 8

F32 = jnp.float32
BF16 = jnp.bfloat16
NT = (((1,), (1,)), ((), ()))
NN = (((1,), (0,)), ((), ()))


def unit_rows(matrix):
    widened = matrix.astype(F32)
    return (
        widened * lax.rsqrt(jnp.sum(widened * widened, axis=-1, keepdims=True) + NORM_EPS)
    ).astype(BF16)


def drain(ref, sem):
    pltpu.make_async_copy(ref, ref, sem).wait()


def rows_to_lanes(acc_ref, view, out_ref, rows):
    for b in range(rows // 128):
        block = acc_ref[view, b * 128 : (b + 1) * 128, :]
        out_ref[b : b + 1, :] = jnp.sum(block.T, axis=0, keepdims=True)


def lanes_to_rows(dense, out_ref, view, rows):
    for b in range(rows // 128):
        block = jnp.broadcast_to(dense[b : b + 1, :], (128, 128))
        out_ref[view, b * 128 : (b + 1) * 128, :] = block.T


def kernel(
    sizes,
    first_ref,
    second_ref,
    protos_ref,
    pair_ref,
    grad_ref,
    loss_ref,
    first_in,
    second_in,
    protos_in,
    pair_in,
    grad_out,
    v_ref,
    partner_ref,
    p_ref,
    onehot_ref,
    ut_ref,
    k_ref,
    ka_ref,
    acc_ref,
    soft_acc_ref,
    rb_ref,
    sb_ref,
    cs_ref,
    c_ref,
    r_ref,
    row_ref,
    t_ref,
    w_ref,
    g_ref,
    dp_src,
    dp_buf,
    y_src,
    y_buf,
    soft_src,
    soft_ybuf,
    soft_mid,
    soft_zbuf,
    loss_src,
    loss_ybuf,
    loss_zbuf,
    loss_xbuf,
    ss_ref,
    sr_ref,
    xs_ref,
    xr_ref,
    xo_ref,
    in_s,
    out_s,
    ay_s,
    ay_r,
    zr_s,
    zr_r,
    zo_s,
    zo_r,
    fy_s,
    fy_r,
    px_s,
    px_r,
    po_r,
    ps_s,
    ps_r,
    dp_s,
    dp_r,
    y_s,
    y_r,
    soft_s,
    soft_r,
    loss_s,
    loss_r,
    ss_s,
    ss_r,
    xs_s,
    xs_r,
    xo_s,
    xo_r,
):
    nx, ny, nz, fr, width, pr = sizes
    frames = fr * ny * nz
    group = fr * ny
    protos = pr * nx * CORES
    ptiles = protos // 128
    tiles_pr = pr // 128
    fdense = frames // 128
    grad_scale = protos * ny * nz / (SOFT_TEMP * math.sqrt(2.0 * frames * nx * CORES))

    dp, pi = lax.axis_index("dp"), lax.axis_index("proto")
    x, core = dp // CORES, dp % CORES
    y, z = pi // nz, pi % nz

    def at(dx=0, dc=0, dy=0, dz=0):
        return {
            "dp": lax.rem(x + dx, nx) * CORES + lax.rem(core + dc, CORES),
            "proto": lax.rem(y + dy, ny) * nz + lax.rem(z + dz, nz),
        }

    def send(src, dst, ssem, rsem, device):
        pltpu.make_async_remote_copy(
            src_ref=src,
            dst_ref=dst,
            send_sem=ssem,
            recv_sem=rsem,
            device_id=device,
            device_id_type=pl.DeviceIdType.MESH,
        ).start()

    sib = at(dc=1)
    xs = [at(dx=d) for d in range(1, nx)]
    ys = [at(dy=d) for d in range(1, ny)]
    zs = [at(dz=d) for d in range(1, nz)]
    around = lambda d, n: min(d, n - d)
    offsets = [(d, e) for d in range(ny) for e in range(nz) if d or e]
    offsets.sort(key=lambda o: -around(o[0], ny) - around(o[1], nz))
    yzs = [at(dy=d, dz=e) for d, e in offsets]
    dps = [at(dx=d, dc=e) for d in range(nx) for e in range(CORES) if d or e]

    last = nz // 2
    near = max(1, last - 2)
    split = near > 1

    def chunk(dz, q=0):
        return v_ref.at[lax.rem(z + nz + dz, nz), lax.rem(y + ny - q, ny)]

    def ring_send(step, q):
        for way, sign in enumerate((-1, 1)):
            part = chunk(sign * (step - 1), q)
            if q and split and step == near:
                part = part.at[0]
            send(part, part, zr_s.at[min(q, 1)], zr_r.at[way, step - 1, q], zs[0 if way == 0 else nz - 2])

    def ring_skip():
        for way in range(2):
            to = zs[1 if way == 0 else nz - 3]
            send(chunk(0), chunk(0), zr_s.at[0], zr_r.at[way, 1, 0], to)

    def ring_wait(step, q):
        for way, sign in enumerate((-1, 1)):
            part = chunk(sign * step, q)
            drain(part.at[0] if q and split and step == near else part, zr_r.at[way, step - 1, q])

    def far_part(dz):
        return chunk(dz).at[1] if abs(dz) == near else chunk(dz)

    def far_send(dz, index):
        for device in ys:
            send(far_part(dz), far_part(dz), fy_s, fy_r.at[index], device)

    def far_wait(dz, index):
        block = v_ref.at[lax.rem(z + nz + dz, nz), pl.ds(0, ny - 1)]
        drain(block.at[:, 1] if abs(dz) == near else block, fy_r.at[index])

    def far_index(dz):
        if dz == last:
            return 0
        return 2 * (abs(dz) - near) + (1 if dz < 0 else 2)

    half = pr // 2

    def proto_half(dx, part):
        owner = lax.rem(x + nx + dx, nx) * CORES + core
        return p_ref.at[owner, pl.ds(part * half, half)]

    def proto_near(way, part):
        piece = proto_half(-1 if way == 0 else 1, part)
        drain(piece, px_r.at[way, part])
        if part == way:
            send(piece, piece, px_s, po_r.at[part], xs[0 if way == 0 else nx - 2])
        send(piece, piece, ps_s, ps_r, sib)

    def proto_far(part):
        piece = proto_half(2, part)
        drain(piece, po_r.at[part])
        send(piece, piece, ps_s, ps_r, sib)

    loads = [
        pltpu.make_async_copy(source, target, in_s.at[i])
        for i, (source, target) in enumerate(
            (
                (first_ref, first_in),
                (second_ref, second_in),
                (protos_ref, protos_in),
                (pair_ref, pair_in),
            )
        )
    ]
    for load in loads:
        load.start()

    greeted = [sib, xs[0], xs[nx - 2], *ys]
    greeted += [zs[d - 1] for d in sorted({1, 2, last, nz - 2, nz - 1})]
    barrier = pltpu.get_barrier_semaphore()
    for device in greeted:
        pl.semaphore_signal(
            barrier, inc=1, device_id=device, device_id_type=pl.DeviceIdType.MESH
        )
    for load in loads:
        load.wait()
    v_ref[z, y, 0] = unit_rows(first_in[...])
    v_ref[z, y, 1] = unit_rows(second_in[...])
    p_ref[dp] = unit_rows(protos_in[...])
    pl.semaphore_wait(barrier, len(greeted))

    for j, device in enumerate(ys):
        send(chunk(0), chunk(0), ay_s, ay_r.at[j], device)
    if last > 2:
        ring_skip()
    send(chunk(0), chunk(0), zo_s, zo_r, zs[last - 1])
    ring_send(1, 0)
    for part in range(2):
        for way in range(2):
            piece = proto_half(0, part if way == 0 else 1 - part)
            where = px_r.at[way, part if way == 0 else 1 - part]
            send(piece, piece, px_s, where, xs[0 if way == 0 else nx - 2])
    send(p_ref.at[dp], p_ref.at[dp], ps_s, ps_r, sib)

    pair = pair_in[...]
    where = (pair % (nz * fr) // fr) * group + (pair // (nz * fr)) * fr + pair % fr
    where = where.astype(F32)
    for b in range(fdense):
        column = jnp.broadcast_to(where[b : b + 1, :], (128, 128)).T
        for t in range(fdense):
            lane = (lax.broadcasted_iota(jnp.int32, (128, 128), 1) + t * 128).astype(F32)
            block = jnp.where(column == lane, 1.0, 0.0).astype(BF16)
            for q in range(128 // fr):
                natural = b * 128 + q * fr
                row = (natural % (nz * fr) // fr) * group + natural // (nz * fr) * fr
                onehot_ref[row : row + fr, t * 128 : (t + 1) * 128] = block[
                    q * fr : (q + 1) * fr, :
                ]
    cs_ref[...] = jnp.zeros_like(cs_ref)
    soft_acc_ref[...] = jnp.zeros_like(soft_acc_ref)

    def first_pass(view, starts, block):
        count = block.shape[0]
        each = count // len(starts)
        soft = jnp.zeros((count, 128), F32)
        for j in range(nx * CORES):
            scores = lax.dot_general(block, p_ref[j], NT, preferred_element_type=F32)
            e = jnp.exp2(scores * (LOG2_E / SOFT_TEMP))
            k = e * e
            for i, start in enumerate(starts):
                rows = pl.ds(pl.multiple_of(start, each), each)
                k_ref[view, rows, j * pr : (j + 1) * pr] = k[i * each : (i + 1) * each]
            for t in range(tiles_pr):
                soft = soft + e[:, t * 128 : (t + 1) * 128]
            cs_ref[view, :, j * pr : (j + 1) * pr] += jnp.sum(
                k.reshape(count // 8, 8, pr), axis=0
            )
        for i, start in enumerate(starts):
            rows = pl.ds(pl.multiple_of(start, each), each)
            soft_acc_ref[view, rows, :] = soft[i * each : (i + 1) * each]

    def frames_y(q):
        drain(chunk(0, q), ay_r.at[q - 1])
        ring_send(1, q)

    def ring_next(step, q):
        ring_wait(step, q)
        if (1 < step < last - 1) if q == 0 else step < near:
            ring_send(step + 1, q)
        if q == 0 and (step > near or (split and step == near)):
            far_send(-step, far_index(-step))
            far_send(step, far_index(step))

    def opposite():
        drain(chunk(last), zo_r)
        far_send(last, far_index(last))

    events = [(6.5, opposite)]
    for q in range(1, ny):
        events.append((4.0 + 0.5 * q, functools.partial(frames_y, q)))
    for step in range(1, last):
        when = 7.0 if step == 1 else 3.9 + 5.0 * (step - 2)
        events.append((when, functools.partial(ring_next, step, 0)))
    for q in range(1, ny):
        for step in range(1, near):
            when = 6.0 + 3.5 * step + 1.3 * q
            events.append((when, functools.partial(ring_next, step, q)))
    for way in range(2):
        events.append((6.0 + 0.1 * way, functools.partial(proto_near, way, way)))
        events.append((8.6 + 0.1 * way, functools.partial(proto_near, way, 1 - way)))
        events.append((12.0 + 0.1 * way, functools.partial(proto_far, way)))
    for when, event in sorted(events, key=lambda pair: pair[0]):
        event()
    drain(p_ref.at[pl.ds(0, nx)], ps_r)

    def dp_start(view, it, source):
        slot = it % 2

        @pl.when(it >= 2)
        def _():
            drain(dp_buf.at[view, slot], dp_s.at[view, slot])

        dp_src[view, slot] = source
        for j, device in enumerate(dps):
            send(
                dp_src.at[view, slot],
                dp_buf.at[view, slot, j],
                dp_s.at[view, slot],
                dp_r.at[view, slot],
                device,
            )

    def dp_wait(view, it):
        slot = it % 2
        drain(dp_buf.at[view, slot], dp_r.at[view, slot])
        total = dp_src[view, slot]
        for j in range(len(dps)):
            total = total + dp_buf[view, slot, j]
        return total

    def yz_start(view, it):
        slot = it % 2

        @pl.when(it >= 2)
        def _():
            drain(y_buf.at[view, slot], y_s.at[view, slot])

        y_src[view, slot] = row_ref[view]
        for j, device in enumerate(yzs):
            send(
                y_src.at[view, slot],
                y_buf.at[view, slot, j],
                y_s.at[view, slot],
                y_r.at[view, slot],
                device,
            )

    def yz_wait(view, it):
        slot = it % 2
        drain(y_buf.at[view, slot], y_r.at[view, slot])
        total = y_src[view, slot]
        for j in range(len(yzs)):
            total = total + y_buf[view, slot, j]
        return total

    def column_totals(view):
        parts = [
            jnp.sum(cs_ref[view, :, t * 128 : (t + 1) * 128], axis=0, keepdims=True)
            for t in range(ptiles)
        ]
        return jnp.concatenate(parts, axis=0)

    def frame_sums(view):
        def step(b, carry):
            rows = pl.ds(pl.multiple_of(b * 128, 128), 128)
            total = jnp.zeros((128, 128), F32)
            for t in range(ptiles):
                k = k_ref[view, rows, t * 128 : (t + 1) * 128]
                total = total + k * c_ref[view, t : t + 1, :]
            row_ref[view, pl.ds(b, 1), :] = jnp.sum(total.T, axis=0, keepdims=True)
            return carry

        lax.fori_loop(0, fdense, step, 0, unroll=fdense)

    def proto_sums(view):
        def step(b, totals):
            rows = pl.ds(pl.multiple_of(b * 128, 128), 128)
            scale = jnp.broadcast_to(r_ref[view, pl.ds(b, 1), :], (128, 128)).T
            out = []
            for t in range(ptiles):
                k = k_ref[view, rows, t * 128 : (t + 1) * 128]
                out.append(totals[t] + jnp.sum((k * scale).reshape(16, 8, 128), axis=0))
            return tuple(out)

        totals = lax.fori_loop(
            0,
            fdense,
            step,
            tuple(jnp.zeros((8, 128), F32) for _ in range(ptiles)),
            unroll=fdense,
        )
        for t in range(ptiles):
            cs_ref[view, :, t * 128 : (t + 1) * 128] = totals[t]

    zero = jnp.int32(0)

    def pair_wait(p):
        if p == 0:
            if near == 1:
                for q in range(1, ny):
                    ring_wait(1, q)
        elif p == 1:
            far_wait(last, far_index(last))
        else:
            step = p
            if step <= near:
                for q in range(1, ny):
                    ring_wait(step, q)
            far_wait(-step, far_index(-step))
            far_wait(step, far_index(step))

    def pair_pass(n, carry):
        p, view = n // 2, 1 - n % 2
        for known in range(last):

            @pl.when(n == 2 * known)
            def _(known=known):
                pair_wait(known)

        opposite_pair = 1 - lax.min((p - 1) * (p - 1), 1)
        step = p + 1 - lax.min(p, 1) + opposite_pair * (last - 1)
        one = lax.rem(z + step, nz)
        two = lax.rem(z + nz - step * (1 - opposite_pair), nz)
        block = jnp.concatenate(
            [v_ref[b, :, view].reshape(group, width) for b in (one, two)], axis=0
        )
        first_pass(view, [one * group, two * group], block)

        @pl.when(n == 2 * last - 2)
        def _():
            dp_start(1, zero, column_totals(1))

        return carry

    lax.fori_loop(0, 2 * last, pair_pass, 0)
    dp_start(0, zero, column_totals(0))

    for view in range(2):
        rows_to_lanes(soft_acc_ref, view, soft_src.at[pl.ds(view * fdense, fdense)], frames)
    for j, device in enumerate(ys):
        send(soft_src, soft_ybuf.at[j], soft_s.at[0], soft_r.at[0], device)

    eye = jnp.where(
        lax.broadcasted_iota(jnp.int32, (width, width), 0)
        == lax.broadcasted_iota(jnp.int32, (width, width), 1),
        1.0,
        0.0,
    ).astype(BF16)

    rows_each = min(256, frames)
    pieces = frames // rows_each

    def transpose_view(view):
        for i in range(pieces):
            if view:
                block = partner_ref[i * rows_each : (i + 1) * rows_each, :]
            else:
                count = rows_each // group
                block = v_ref[i * count : (i + 1) * count, :, 0].reshape(rows_each, width)
            ut_ref[view, :, i * rows_each : (i + 1) * rows_each] = lax.dot_general(
                eye, block, NT, preferred_element_type=F32
            ).astype(BF16)

    def align_rows():
        second = v_ref[:, :, 1].reshape(frames, width)
        for i in range(pieces):
            rows = slice(i * rows_each, (i + 1) * rows_each)
            partner_ref[rows, :] = lax.dot_general(
                onehot_ref[rows, :], second, NN, preferred_element_type=F32
            ).astype(BF16)

    def align_kernel(first, count):
        def step(i, carry):
            rows = pl.ds(pl.multiple_of(i * rows_each, rows_each), rows_each)
            block = partner_ref[rows, :]
            for j in range(nx * CORES):
                scores = lax.dot_general(block, p_ref[j], NT, preferred_element_type=F32)
                ka_ref[rows, j * pr : (j + 1) * pr] = jnp.exp2(
                    scores * (2.0 * LOG2_E / SOFT_TEMP)
                )
            return carry

        lax.fori_loop(first, first + count, step, 0)

    def align_dense(dense):
        row = jnp.concatenate([dense[b : b + 1, :] for b in range(fdense)], axis=1)
        high = row.astype(BF16).astype(F32)
        middle = (row - high).astype(BF16).astype(F32)
        low = row - high - middle
        parts = jnp.concatenate([high, middle, low, jnp.zeros((13, frames), F32)], axis=0)
        out = lax.dot_general(
            parts.astype(BF16), onehot_ref[...], NT, preferred_element_type=F32
        )
        total = out[0:1] + out[1:2] + out[2:3]
        return jnp.concatenate(
            [total[:, b * 128 : (b + 1) * 128] for b in range(fdense)], axis=0
        )

    transpose_view(0)
    align_rows()

    def soft_rows():
        total = soft_src[...]
        drain(soft_ybuf, soft_r.at[0])
        for j in range(len(ys)):
            total = total + soft_ybuf[j]
        soft_mid[...] = total

    def soft_totals():
        drain(soft_zbuf, soft_r.at[1])
        total = soft_mid[...]
        for j in range(len(zs)):
            total = total + soft_zbuf[j]
        transpose_view(1)
        for view in range(2):
            dense = total[view * fdense : (view + 1) * fdense]
            if view:
                dense = align_dense(dense)
            lanes_to_rows(grad_scale / dense, sb_ref, view, frames)
            r_ref[2 + view] = jnp.log(dense)

    def cross_sums():
        def step(i, carry):
            rows = pl.ds(pl.multiple_of(i * 32, 32), 32)
            sums = [jnp.zeros((32, 128), F32) for _ in range(3)]
            for t in range(ptiles):
                k = [ref[rows, t * 128 : (t + 1) * 128] for ref in (k_ref.at[0], ka_ref)]
                terms = [k[v] * c_ref[v, t : t + 1, :] for v in range(2)]
                sums[0] = sums[0] + terms[0] * jnp.log(k[1])
                sums[1] = sums[1] + terms[1] * jnp.log(k[0])
                sums[2] = sums[2] + terms[1]
            acc_ref[0, rows, :] = 0.5 * sums[0]
            acc_ref[1, rows, :] = 0.5 * sums[1]
            soft_acc_ref[1, rows, :] = sums[2]
            return carry

        lax.fori_loop(0, frames // 32, step, 0)
        for v in range(2):
            rows_to_lanes(acc_ref, v, t_ref.at[v], frames)
        rows_to_lanes(soft_acc_ref, 1, row_ref.at[1], frames)

    def sweep(it, carry):
        for view in (1, 0):
            c_ref[view] = 1.0 / dp_wait(view, it)
            frame_sums(view)
            yz_start(view, it)

        @pl.when(it == 0)
        def _():
            align_kernel(0, pieces)
            soft_rows()
            for j, device in enumerate(zs):
                send(soft_mid, soft_zbuf.at[j], soft_s.at[1], soft_r.at[1], device)

        @pl.when(it == 1)
        def _():
            soft_totals()

        @pl.when(it == ITERS - 1)
        def _():
            cross_sums()

        for view in (1, 0):
            r_ref[view] = 1.0 / yz_wait(view, it)

            @pl.when(it < ITERS - 1)
            def _(view=view):
                proto_sums(view)
                dp_start(view, it + 1, column_totals(view))

            @pl.when(it == ITERS - 1)
            def _(view=view):
                if view:
                    r_ref[view] = align_dense(r_ref[view])
                lanes_to_rows(r_ref[view] * grad_scale, rb_ref, view, frames)

        return carry

    lax.fori_loop(0, ITERS, sweep, 0)

    loss = jnp.zeros((fdense, 128), F32)
    for v in range(2):
        loss = loss + r_ref[v] * (r_ref[3 - v] * row_ref[v] - t_ref[v])
    loss_src[0] = loss
    for j, device in enumerate(ys):
        send(loss_src.at[0], loss_ybuf.at[j], loss_s.at[0], loss_r.at[0], device)

    def loss_step(stage, buf, nextbuf, partners):
        drain(buf, loss_r.at[stage])
        total = loss_src[stage]
        for j in range(buf.shape[0]):
            total = total + buf[j]
        if nextbuf is None:
            return total
        loss_src[stage + 1] = total
        for j, device in enumerate(partners):
            send(
                loss_src.at[stage + 1],
                nextbuf.at[j],
                loss_s.at[stage + 1],
                loss_r.at[stage + 1],
                device,
            )
        return total

    def block_grad(owner):
        count = min(64, frames)
        for start in range(0, frames, count):
            rows = slice(start, start + count)
            for t in range(tiles_pr):
                tile = owner * tiles_pr + t
                cols = pl.ds(pl.multiple_of(tile * 128, 128), 128)
                k = [ref[rows, cols] for ref in (k_ref.at[0], ka_ref)]
                assigned = [
                    k[v] * (rb_ref[v, rows, :] * c_ref[v, pl.ds(tile, 1), :])
                    for v in range(2)
                ]
                for v in range(2):
                    w_ref[v, rows, t * 128 : (t + 1) * 128] = (
                        (k[v] * lax.rsqrt(k[v])) * sb_ref[v, rows, :] - assigned[1 - v]
                    ).astype(BF16)
        total = lax.dot_general(ut_ref[0], w_ref[0], NN, preferred_element_type=F32)
        total = total + lax.dot_general(ut_ref[1], w_ref[1], NN, preferred_element_type=F32)
        return total

    middle = width // 2
    lower, upper = pl.ds(0, middle), pl.ds(middle, middle)
    right, left = xs[0], xs[nx - 2]
    def scatter(n, carry):
        k, own = n // 2, n % 2
        d = (2 + 3 * k + (k // 2) * (3 - 2 * (k % 2))) % 4
        g_ref[k] = block_grad(lax.rem(x + d, nx) * CORES + lax.rem(core + 1 + own, CORES))

        @pl.when(own == 0)
        def _():
            ss_ref[k] = g_ref[k].astype(BF16)
            send(ss_ref.at[k], sr_ref.at[k], ss_s, ss_r.at[k], sib)

        @pl.when(own == 1)
        def _():
            drain(sr_ref.at[k], ss_r.at[k])

        @pl.when(n == 1)
        def _():
            xs_ref[0] = (g_ref[0] + sr_ref[0].astype(F32)).astype(BF16)
            send(xs_ref.at[0, lower], xo_ref.at[0], xo_s, xo_r.at[0], right)
            send(xs_ref.at[0, upper], xo_ref.at[1], xo_s, xo_r.at[1], left)

        @pl.when(n == 3)
        def _():
            xs_ref[1, upper] = (g_ref[1, upper] + sr_ref[1, upper].astype(F32)).astype(BF16)
            send(xs_ref.at[1, upper], xr_ref.at[0, upper], xs_s, xs_r, right)
            loss_step(0, loss_ybuf, loss_zbuf, zs)

        @pl.when(n == 5)
        def _():
            xs_ref[2, lower] = (g_ref[2, lower] + sr_ref[2, lower].astype(F32)).astype(BF16)
            send(xs_ref.at[2, lower], xr_ref.at[1, lower], xs_s, xs_r, left)
            for way, (rows, to) in enumerate(((lower, right), (upper, left))):
                drain(xo_ref.at[way], xo_r.at[way])
                xs_ref[1 + way, rows] = (
                    g_ref[1 + way, rows]
                    + sr_ref[1 + way, rows].astype(F32)
                    + xo_ref[way].astype(F32)
                ).astype(BF16)
                send(xs_ref.at[1 + way, rows], xr_ref.at[way, rows], xs_s, xs_r, to)

        return carry

    lax.fori_loop(0, 2 * nx, scatter, 0)
    loss_step(1, loss_zbuf, loss_xbuf, dps)
    drain(xr_ref, xs_r)
    stores = []
    for i in range(width // 128):
        rows = slice(i * 128, (i + 1) * 128)
        for t in range(tiles_pr):
            cols = slice(t * 128, (t + 1) * 128)
            total = g_ref[3, rows, cols] + sr_ref[3, rows, cols].astype(F32)
            for j in range(2):
                total = total + xr_ref[j, rows, cols].astype(F32)
            grad_out[cols, rows] = total.T
        stores.append(
            pltpu.make_async_copy(grad_out.at[:, rows], grad_ref.at[:, rows], out_s.at[i])
        )
        stores[i].start()
    total = loss_step(2, loss_xbuf, None, None)
    loss_ref[0, 0] = jnp.sum(total) / (2.0 * frames * nx * CORES)

    for store in stores:
        store.wait()
    drain(v_ref.at[0, pl.ds(0, ny - 1)], ay_s)
    drain(v_ref.at[pl.ds(0, 2 * (last - 1)), 0], zr_s.at[0])
    drain(v_ref.at[pl.ds(0, 2 * near - split), pl.ds(0, ny - 1)], zr_s.at[1])
    drain(chunk(0), zo_s)
    drain(v_ref.at[pl.ds(0, 2 * (last - 1 - near) + 1 + split), pl.ds(0, ny - 1)], fy_s)
    drain(p_ref.at[pl.ds(0, 3)], px_s)
    drain(p_ref.at[pl.ds(0, nx)], ps_s)
    for view in range(2):
        for slot in range(min(2, ITERS)):
            drain(dp_buf.at[view, slot], dp_s.at[view, slot])
            drain(y_buf.at[view, slot], y_s.at[view, slot])
    drain(soft_ybuf, soft_s.at[0])
    drain(soft_zbuf, soft_s.at[1])
    drain(loss_ybuf, loss_s.at[0])
    drain(loss_zbuf, loss_s.at[1])
    drain(loss_xbuf, loss_s.at[2])
    drain(sr_ref, ss_s)
    drain(xo_ref, xo_s)
    drain(xr_ref, xs_s)


def solution(mesh):
    ndp, nproto = mesh.shape["dp"], mesh.shape["proto"]
    nx, nz = ndp // CORES, DEPTH
    ny = nproto // nz

    def local(first, second, protos, pairing):
        fr, width = first.shape
        pr = protos.shape[0]
        frames = fr * nproto
        cols = pr * ndp
        fd = frames // 128
        ct = cols // 128
        sem = pltpu.SemaphoreType.DMA
        sizes = (nx, ny, nz, fr, width, pr)
        vmem = pltpu.VMEM
        grad, loss = pl.pallas_call(
            functools.partial(kernel, sizes),
            out_shape=(
                jax.ShapeDtypeStruct((pr, width), F32),
                jax.ShapeDtypeStruct((1, 1), F32),
            ),
            in_specs=[pl.BlockSpec(memory_space=pl.ANY)] * 4,
            out_specs=(
                pl.BlockSpec(memory_space=pl.ANY),
                pl.BlockSpec(memory_space=pltpu.SMEM),
            ),
            scratch_shapes=[
                vmem((fr, width), BF16),
                vmem((fr, width), BF16),
                vmem((pr, width), F32),
                vmem((fd, 128), jnp.int32),
                vmem((pr, width), F32),
                vmem((nz, ny, 2, fr, width), BF16),
                vmem((frames, width), BF16),
                vmem((ndp, pr, width), BF16),
                vmem((frames, frames), BF16),
                vmem((2, width, frames), BF16),
                vmem((2, frames, cols), F32),
                vmem((frames, cols), F32),
                vmem((2, frames, 128), F32),
                vmem((2, frames, 128), F32),
                vmem((2, frames, 128), F32),
                vmem((2, frames, 128), F32),
                vmem((2, 8, cols), F32),
                vmem((2, ct, 128), F32),
                vmem((4, fd, 128), F32),
                vmem((2, fd, 128), F32),
                vmem((2, fd, 128), F32),
                vmem((2, frames, pr), BF16),
                vmem((nx, width, pr), F32),
                vmem((2, 2, ct, 128), F32),
                vmem((2, 2, ndp - 1, ct, 128), F32),
                vmem((2, 2, fd, 128), F32),
                vmem((2, 2, nproto - 1, fd, 128), F32),
                vmem((2 * fd, 128), F32),
                vmem((ny - 1, 2 * fd, 128), F32),
                vmem((2 * fd, 128), F32),
                vmem((nz - 1, 2 * fd, 128), F32),
                vmem((3, fd, 128), F32),
                vmem((ny - 1, fd, 128), F32),
                vmem((nz - 1, fd, 128), F32),
                vmem((ndp - 1, fd, 128), F32),
                vmem((nx, width, pr), BF16),
                vmem((nx, width, pr), BF16),
                vmem((nx - 1, width, pr), BF16),
                vmem((2, width, pr), BF16),
                vmem((2, width // 2, pr), BF16),
                sem((4,)), sem((width // 128,)),
                sem, sem((ny - 1,)),
                sem((2,)), sem((2, nz // 2, ny)),
                sem, sem,
                sem, sem((nz,)),
                sem, sem((2, 2)), sem((2,)),
                sem, sem,
                sem((2, 2)), sem((2, 2)),
                sem((2, 2)), sem((2, 2)),
                sem((2,)), sem((2,)),
                sem((3,)), sem((3,)),
                sem, sem((nx,)),
                sem, sem,
                sem, sem((2,)),
            ],
            compiler_params=pltpu.CompilerParams(
                collective_id=0, has_side_effects=True, vmem_limit_bytes=56 * 2**20
            ),
        )(first, second, protos, pairing.reshape(fd, 128))
        return grad, loss[0, 0]

    return jax.shard_map(
        local,
        mesh=mesh,
        in_specs=(
            P(("dp", "proto"), None),
            P(("dp", "proto"), None),
            P(("dp", "proto"), None),
            P("dp"),
        ),
        out_specs=(P(("dp", "proto"), None), P()),
        check_vma=False,
    )
```
